32 devices in a mesh: dp: 8 (over z, y), head: 4 (over x, core).
Axes of the slice: x: 2, y: 2, z: 4, core: 2. Of those that a mesh axis runs over, the one named last changes fastest.
Arguments:
- tokens: bfloat16 [12288, 768], P('dp'), may hold values from -6 to 6
- cotangent: bfloat16 [12288, 768], P('dp'), may hold values from -6 to 6
- memory: bfloat16 [10, 768], replicated, may hold values from -6 to 6
- query_weight: bfloat16 [768, 768], P(None, 'head'), may hold values from -0.21875 to 0.21875
- query_bias: float32 [768], P('head'), may hold values from -3 to 3
- key_weight: bfloat16 [768, 768], P(None, 'head'), may hold values from -0.21875 to 0.21875
- value_weight: bfloat16 [768, 768], P(None, 'head'), may hold values from -0.21875 to 0.21875
- value_bias: float32 [768], P('head'), may hold values from -3 to 3
- out_weight: bfloat16 [768, 768], P('head'), may hold values from -2.5 to 2.5
- out_bias: float32 [768], replicated, may hold values from -3 to 3
- gain_one: float32 [768], replicated, may hold values from 0.5 to 1.5
- shift_one: float32 [768], replicated, may hold values from -2 to 2
- inner_weight: bfloat16 [768, 3072], replicated, may hold values from -0.21875 to 0.21875
- inner_bias: float32 [3072], replicated, may hold values from -3 to 3
- outer_weight: bfloat16 [3072, 768], replicated, may hold values from -0.109375 to 0.109375
- outer_bias: float32 [768], replicated, may hold values from -3 to 3
- gain_two: float32 [768], replicated, may hold values from 0.5 to 1.5
- shift_two: float32 [768], replicated, may hold values from -2 to 2
- group_sizes: int32 [4], replicated, may hold values from 1 to 4, 8 in all
- group_section: int32 [4], replicated, may hold values from 0 to 3, each once
- last_valid: int32 [8], P('dp'), may hold values from 128 to 512
Outputs:
- layer_out: float32 [12288, 768], P('dp')
- grad_tokens: float32 [12288, 768], P('dp')
- grad_memory: float32 [10, 768], replicated
- grad_query_weight: float32 [768, 768], P(None, 'head')
- grad_query_bias: float32 [768], P('head')
- grad_key_weight: float32 [768, 768], P(None, 'head')
- grad_value_weight: float32 [768, 768], P(None, 'head')
- grad_value_bias: float32 [768], P('head')
- grad_out_weight: float32 [768, 768], P('head')
- grad_out_bias: float32 [768], replicated
- grad_gain_one: float32 [768], replicated
- grad_shift_one: float32 [768], replicated
- grad_inner_weight: float32 [768, 3072], P(None, 'dp')
- grad_inner_bias: float32 [3072], P('dp')
- grad_outer_weight: float32 [3072, 768], P('dp')
- grad_outer_bias: float32 [768], replicated
- grad_gain_two: float32 [768], replicated
- grad_shift_two: float32 [768], replicated
The draws below stay inside these ranges and needn't reach their ends.
Inputs may be any that keep to these rules, and one draw needn't show every extreme that they name: `group_section`: each section occurs once; a chain whose group has section g holds (g mod (2)) + 2 segments with tokens, the later slots being empty. `group_sizes`: groups cover the chains in order and sum to 8.
All inputs are finite; a program needn't handle non-finite values.
Results may differ from the reference program's by a relative error of at most 0.015.
Values sent between devices are 32-bit elements; how exact they have to be, the bound alone decides.
No kernel may reach another device: no remote copies, remote signals or barrier semaphores. Data moves between devices by JAX's collectives and lax.ppermute only.
A program may use at most 192 MiB of HBM per device.

```python
import math
import jax
import jax.numpy as jnp
import numpy as np
from jax import lax

HEAD_DIM = 64
FF = 3072
MEM = 10
SEG_LEN = 512
SEGS = 3
GROUPS = 4
D = 768
CHAINS = 8
TOKENS = 12288


def draw_last_valid(key, part):
    key = jax.random.fold_in(key, 7)
    first_key, second_key = jax.random.split(key)
    values = jax.random.randint(first_key, (CHAINS,), SEG_LEN // 4, SEG_LEN + 1)
    chosen = jax.random.randint(second_key, (), 0, CHAINS)
    return jnp.where(jnp.arange(CHAINS) == chosen, SEG_LEN, values).astype(jnp.int32)


def steps_of(stream_key, dims, cuts, least, high):
    factor_of, own = 1.0, jax.random.fold_in(stream_key, 6)
    for position, shards_of in cuts:
        steps = jnp.exp(jax.random.uniform(jax.random.fold_in(own, position), (shards_of,), jnp.float32, least / len(cuts), high / len(cuts)))
        factor_of = factor_of * jnp.repeat(steps, dims[position] // shards_of).reshape([-1 if axis == position else 1 for axis in range(len(dims))])
    return factor_of


def length_profile(count, total, most, skew):
    portions = [(1 << 20) // math.isqrt(rank ** skew) + 1 for rank in range(2, count + 1)]
    surplus, given = total - most - (count - 1), [1] * (count - 1)
    while surplus > 0:
        candidates = [i for i in range(count - 1) if given[i] < most]
        pool, budget = sum([portions[i] for i in candidates]), surplus
        for i in candidates:
            extra = min(most - given[i], max(1, budget * portions[i] // pool), surplus)
            given[i] = given[i] + extra
            surplus = surplus - extra
    return np.array([most] + given)


def uneven(own_key, count, total, reach, skew):
    if count == 2:
        one = jax.random.randint(own_key, (), max(1, total - reach), min(reach, total - 1) + 1)
        return jnp.stack([one, total - one])
    lengths = jnp.asarray(length_profile(count, total, reach, skew), jnp.int32)
    couples = (count - 1) // 2
    source_of, receiver = lengths[1:1 + 2 * couples:2], lengths[2:2 + 2 * couples:2]
    margin = jnp.minimum(source_of - 1, reach - receiver)
    shifted = jax.random.randint(jax.random.fold_in(own_key, 1), (couples,), 0, 1 << 20) % (margin + 1)
    lengths = lengths.at[1:1 + 2 * couples:2].set(source_of - shifted).at[2:2 + 2 * couples:2].set(receiver + shifted)
    return lengths[jax.random.permutation(jax.random.fold_in(own_key, 2), count)]


def centred(own_key, dims, deviation, most, shards=(), kind=jnp.bfloat16):
    factor_of = steps_of(own_key, dims, shards, -0.22, 0.18) if shards else 1.0
    values = jax.random.normal(own_key, dims, jnp.float32) * deviation * factor_of
    return jnp.minimum(jnp.maximum(values, -most), most).astype(kind)


def setup_inputs(seed: int = 0) -> dict:
    arg_keys = jax.random.split(jax.random.key(seed), 22)
    return {
        "tokens": centred(arg_keys[0], (TOKENS, D), 1.0, 6.0, ((0, 8),)),
        "cotangent": centred(arg_keys[1], (TOKENS, D), 1.0, 6.0, ((0, 8),)),
        "memory": centred(arg_keys[2], (MEM, D), 1.0, 6.0),
        "query_weight": centred(arg_keys[3], (D, D), D ** -0.5, 0.21875, ((1, 4),)),
        "query_bias": centred(arg_keys[4], (D,), 0.5, 3.0, ((0, 4),), jnp.float32),
        "key_weight": centred(arg_keys[5], (D, D), D ** -0.5, 0.21875, ((1, 4),)),
        "value_weight": centred(arg_keys[6], (D, D), D ** -0.5, 0.21875, ((1, 4),)),
        "value_bias": centred(arg_keys[7], (D,), 0.5, 3.0, ((0, 4),), jnp.float32),
        "out_weight": centred(arg_keys[8], (D, D), (max(D // 128, 1)) ** -0.5, 2.5, ((0, 4),)),
        "out_bias": centred(arg_keys[9], (D,), 0.5, 3.0, (), jnp.float32),
        "gain_one": jnp.clip(1.0 + 0.1 * jax.random.normal(arg_keys[10], (D,), jnp.float32), 0.5, 1.5),
        "shift_one": centred(arg_keys[11], (D,), 0.3, 2.0, (), jnp.float32),
        "inner_weight": centred(arg_keys[12], (D, FF), D ** -0.5, 0.21875),
        "inner_bias": centred(arg_keys[13], (FF,), 0.5, 3.0, (), jnp.float32),
        "outer_weight": centred(arg_keys[14], (FF, D), FF ** -0.5, 0.109375),
        "outer_bias": centred(arg_keys[15], (D,), 0.5, 3.0, (), jnp.float32),
        "gain_two": jnp.clip(1.0 + 0.1 * jax.random.normal(arg_keys[16], (D,), jnp.float32), 0.5, 1.5),
        "shift_two": centred(arg_keys[17], (D,), 0.3, 2.0, (), jnp.float32),
        "group_sizes": uneven(arg_keys[18], GROUPS, CHAINS, CHAINS // 2, 1).astype(jnp.int32),
        "group_section": jax.random.permutation(arg_keys[19], GROUPS).astype(jnp.int32),
        "last_valid": draw_last_valid(jax.random.fold_in(arg_keys[21], 71), 0),
    }


@jax.custom_vjp
def low(v):
    return lax.optimization_barrier(v.astype(jnp.bfloat16)).astype(jnp.float32)

@jax.custom_vjp
def low_back(v):
    return v

def low_keep(v):
    return (low(v), None)

def low_pass(kept, grad):
    return (grad,)

def back_keep(v):
    return (v, None)

def back_low(kept, grad):
    return (low(grad),)
low.defvjp(low_keep, low_pass)
low_back.defvjp(back_keep, back_low)
epsilon = 1e-06
highest = lax.Precision.HIGHEST

def normalize(value, gain, shift):
    centered = value - lax.optimization_barrier(jnp.mean(value, axis=-1, keepdims=True))
    spread = lax.optimization_barrier(jnp.mean(centered * centered, axis=-1, keepdims=True))
    return centered * lax.rsqrt(spread + epsilon) * gain + shift

def softmax_rows(scores):
    top_value = lax.optimization_barrier(jnp.max(scores, axis=-1, keepdims=True))
    weights = jnp.exp(scores - top_value)
    return weights / lax.optimization_barrier(jnp.sum(weights, axis=-1, keepdims=True))

def segment_layer(params, inputs_now, key_valid):
    start_memory, query_weight, query_bias, key_weight, value_weight, value_bias, out_weight, out_bias, gain_one, shift_one, inner_weight, inner_bias, outer_weight, outer_bias, gain_two, shift_two = params
    row_count = inputs_now.shape[0]
    head_count = query_weight.shape[1] // HEAD_DIM
    scale = HEAD_DIM ** (-0.5)
    inputs_low = low(inputs_now)
    query = low(low_back(jnp.dot(inputs_low, query_weight, precision=highest) + query_bias))
    keys = low(low_back(jnp.dot(inputs_low, key_weight, precision=highest)))
    values = low(low_back(jnp.dot(inputs_low, value_weight, precision=highest) + value_bias))
    query = query.reshape(row_count, head_count, HEAD_DIM)
    keys = keys.reshape(row_count, head_count, HEAD_DIM)
    values = values.reshape(row_count, head_count, HEAD_DIM)
    scores = low_back(jnp.einsum('qhd,khd->hqk', query, keys, precision=highest) * scale)
    scores = jnp.where(key_valid[None, None, :], scores, -1000000000.0)
    probs = low(softmax_rows(scores))
    context = jnp.einsum('hqk,khd->qhd', probs, values, precision=highest).reshape(row_count, head_count * HEAD_DIM)
    context = low(low_back(context))
    attended = low_back(jnp.dot(context, out_weight, precision=highest))
    normed = normalize(inputs_now + attended + out_bias, gain_one, shift_one)
    inner = low_back(jnp.dot(low(normed), inner_weight, precision=highest) + inner_bias)
    outer = low_back(jnp.dot(low(jax.nn.gelu(inner, approximate=False)), outer_weight, precision=highest))
    return normalize(normed + outer + outer_bias, gain_two, shift_two)

def chain_forward(params, chain_tokens, count, valid_last):
    memory_now = params[0]
    positions = jnp.arange(SEG_LEN)
    pieces = []
    for segment in range(SEGS):
        token_valid = (segment < count) & ((segment < count - 1) | (positions < valid_last))
        edge = jnp.ones((MEM,), jnp.bool_)
        key_valid = jnp.concatenate([edge, token_valid, edge], 0)
        block = chain_tokens[segment * SEG_LEN:(segment + 1) * SEG_LEN]
        inputs_now = jnp.concatenate([memory_now, block, memory_now], 0)
        result = segment_layer(params, inputs_now, key_valid)
        pieces.append(jnp.where(token_valid[:, None], result[MEM:MEM + SEG_LEN], 0.0))
        memory_now = result[SEG_LEN + MEM:]
    return jnp.concatenate(pieces, 0)

def reference(tokens, cotangent, memory, query_weight, query_bias, key_weight, value_weight, value_bias, out_weight, out_bias, gain_one, shift_one, inner_weight, inner_bias, outer_weight, outer_bias, gain_two, shift_two, group_sizes, group_section, last_valid):
    params = tuple((value.astype(jnp.float32) for value in (memory, query_weight, query_bias, key_weight, value_weight, value_bias, out_weight, out_bias, gain_one, shift_one, inner_weight, inner_bias, outer_weight, outer_bias, gain_two, shift_two)))
    ends = jnp.cumsum(group_sizes)
    chain_ids = jnp.arange(CHAINS).astype(jnp.int32)
    group_index = lax.optimization_barrier(jnp.sum((ends[None, :] <= chain_ids[:, None]).astype(jnp.int32), axis=1))
    sections = lax.optimization_barrier(jnp.sum(jnp.where(jnp.arange(GROUPS)[None, :] == group_index[:, None], group_section[None, :], 0), axis=1))
    counts = (sections % (SEGS - 1) + 2).astype(jnp.int32)
    chain_tokens = tokens.astype(jnp.float32).reshape(CHAINS, SEGS * SEG_LEN, D)
    chain_cot = cotangent.astype(jnp.float32).reshape(CHAINS, SEGS * SEG_LEN, D)

    def step(total, item):
        block, block_cot, count, valid_last = item

        def forward(param_tuple, inputs_block):
            return chain_forward(param_tuple, inputs_block, count, valid_last)
        result, pull = jax.vjp(forward, params, block)
        grads, grad_block = pull(block_cot)
        return (jax.tree.map(jnp.add, total, grads), (result, grad_block))
    zeros = jax.tree.map(jnp.zeros_like, params)
    totals, outputs = lax.scan(step, zeros, (chain_tokens, chain_cot, counts, last_valid))
    results, grad_blocks = outputs
    return (results.reshape(TOKENS, D), grad_blocks.reshape(TOKENS, D), totals[0], totals[1], totals[2], totals[3], totals[4], totals[5], totals[6], totals[7], totals[8], totals[9], totals[10], totals[11], totals[12], totals[13], totals[14], totals[15])
```

```python
from functools import partial

import jax
import jax.numpy as jnp
from jax import lax
from jax.experimental import pallas as pl
from jax.experimental.pallas import tpu as pltpu
from jax.sharding import PartitionSpec as P

HEAD_DIM = 64
MEM = 10
MEM_PAD = 16
SEG_LEN = 512
SEGS = 3
CHAINED = SEGS - 1
KEYS = SEG_LEN + MEM_PAD
HALF_ROWS = SEG_LEN // 2
EPS = 1e-06
SCALE = HEAD_DIM ** (-0.5)
MASKED = -1000000000.0
LN_TWO = 0.6931471805599453

F32 = jnp.float32
BF16 = jnp.bfloat16


def nn(left, right):
    return jnp.dot(left, right, preferred_element_type=F32)


def nt(left, right):
    return lax.dot_general(left, right, (((1,), (1,)), ((), ())), preferred_element_type=F32)


def tn(left, right):
    return lax.dot_general(left, right, (((0,), (0,)), ((), ())), preferred_element_type=F32)


def norm_fwd(value, gain, shift):
    centered = value - jnp.mean(value, axis=-1, keepdims=True)
    spread = jnp.mean(centered * centered, axis=-1, keepdims=True)
    root = lax.rsqrt(spread + EPS)
    unit = centered * root
    return unit * gain + shift, unit, root


def norm_bwd(d_out, unit, root, gain):
    d_unit = d_out * gain
    mean_one = jnp.mean(d_unit, axis=-1, keepdims=True)
    mean_two = jnp.mean(d_unit * unit, axis=-1, keepdims=True)
    return root * (d_unit - mean_one - unit * mean_two)


def gelu_parts(inner):
    cdf = 0.5 * (1.0 + lax.erf(inner * 0.7071067811865476))
    pdf = jnp.exp(-0.5 * inner * inner) * 0.3989422804014327
    return inner * cdf, cdf + inner * pdf


def column_sum(value):
    return jnp.sum(value, axis=0, keepdims=True)


OUT_BIAS, GAIN_ONE, SHIFT_ONE, OUTER_BIAS, GAIN_TWO, SHIFT_TWO, QUERY_BIAS, VALUE_BIAS = range(8)


def row_of(vectors, index):
    return vectors[index : index + 1]


def head_mask(width):
    count = width // HEAD_DIM
    shape = (count, MEM_PAD, width)
    head = lax.broadcasted_iota(jnp.int32, shape, 0)
    lane = lax.broadcasted_iota(jnp.int32, shape, 2) // HEAD_DIM
    return (head == lane).astype(F32)


def spread_heads(value, mask):
    count, rows, width = mask.shape
    return (value.astype(F32)[None] * mask).reshape(count * rows, width).astype(BF16)


def gather_heads(value, mask):
    return jnp.sum(value.reshape(mask.shape) * mask, axis=0)


def memory_forward_kernel(
    place_ref,
    tokens_ref,
    memory_ref,
    own_ref,
    partner_ref,
    far_ref,
    far_partner_ref,
    vectors_ref,
    inner_bias_ref,
    key_bias_ref,
    inner_hbm,
    outer_hbm,
    weights_ref,
    keys_ref,
    values_ref,
    query_ref,
    low_ref,
    mem_query_ref,
    mem_context_ref,
    mem_probs_ref,
    mem_hidden_ref,
    mem_total_ref,
    mem_slope_ref,
    mem_active_ref,
    inner_ref,
    outer_ref,
    sems,
):
    copies = [
        pltpu.make_async_copy(inner_hbm, inner_ref, sems.at[0]),
        pltpu.make_async_copy(outer_hbm, outer_ref, sems.at[1]),
    ]
    for copy in copies:
        copy.start()
    side, core = place_ref[0], place_ref[1]
    quarter = own_ref.shape[1]
    width = memory_ref.shape[1]
    pieces = (
        (own_ref, side, core),
        (partner_ref, side, 1 - core),
        (far_ref, 1 - side, core),
        (far_partner_ref, 1 - side, 1 - core),
    )
    for ref, at_side, at_core in pieces:
        start = pl.multiple_of((2 * at_side + at_core) * quarter, quarter)
        for which in range(4):
            weights_ref[which, pl.ds(start, quarter)] = ref[which].astype(BF16)
    vectors = vectors_ref[...]
    query_bias = row_of(vectors, QUERY_BIAS)
    value_bias = row_of(vectors, VALUE_BIAS)

    def project(index, carry):
        segment, part = index // 2, index % 2
        rows = tokens_ref[segment, pl.ds(part * HALF_ROWS, HALF_ROWS)]
        span = pl.ds(part * HALF_ROWS, HALF_ROWS)
        keys_ref[segment, span] = nt(rows, weights_ref[1]).astype(BF16)
        values_ref[segment, span] = (nt(rows, weights_ref[2]) + value_bias).astype(BF16)

        @pl.when(part == core)
        def _():
            query_ref[segment] = (nt(rows, weights_ref[0]) + query_bias).astype(BF16) * SCALE

        return carry

    lax.fori_loop(0, 2 * SEGS, project, 0)

    mask = head_mask(width)
    now = memory_ref[...]
    for segment in range(SEGS):
        low = now.astype(BF16)
        low_ref[segment] = low
        keys_ref[segment, SEG_LEN:] = nt(low, weights_ref[1]).astype(BF16)
        values_ref[segment, SEG_LEN:] = (nt(low, weights_ref[2]) + value_bias).astype(BF16)
        if segment == CHAINED:
            break
        query = (nt(low, weights_ref[0]) + query_bias).astype(BF16) * SCALE
        mem_query_ref[segment] = query
        scores = nt(keys_ref[segment], spread_heads(query, mask)) + key_bias_ref[segment]
        weights = jnp.exp(scores - jnp.max(scores, axis=0, keepdims=True))
        probs = weights * (1.0 / jnp.sum(weights, axis=0, keepdims=True))
        mem_probs_ref[segment] = probs
        context = gather_heads(tn(probs.astype(BF16), values_ref[segment]), mask).astype(BF16)
        mem_context_ref[segment] = context
        hidden = now + nn(context, weights_ref[3]) + row_of(vectors, OUT_BIAS)
        mem_hidden_ref[segment] = hidden
        normed, _, _ = norm_fwd(hidden, row_of(vectors, GAIN_ONE), row_of(vectors, SHIFT_ONE))
        if segment == 0:
            copies[0].wait()
        active, slope = gelu_parts(nn(normed.astype(BF16), inner_ref[...]) + inner_bias_ref[...])
        active = active.astype(BF16)
        mem_slope_ref[segment] = slope
        mem_active_ref[segment] = active
        if segment == 0:
            copies[1].wait()
        total = normed + nn(active, outer_ref[...]) + row_of(vectors, OUTER_BIAS)
        mem_total_ref[segment] = total
        now, _, _ = norm_fwd(total, row_of(vectors, GAIN_TWO), row_of(vectors, SHIFT_TWO))


def memory_forward(
    place, tokens, memory, pieces, vectors, inner_bias, key_bias, inner_weight, outer_weight
):
    width = memory.shape[1]
    ff = inner_weight.shape[1]
    head_rows = MEM_PAD * width // HEAD_DIM
    vmem = pl.BlockSpec(memory_space=pltpu.VMEM)

    def like(shape, dtype):
        return jax.ShapeDtypeStruct(shape, dtype)

    return pl.pallas_call(
        memory_forward_kernel,
        in_specs=[pl.BlockSpec(memory_space=pltpu.SMEM)]
        + [vmem] * 9
        + [pl.BlockSpec(memory_space=pl.ANY)] * 2,
        out_specs=[vmem] * 12,
        out_shape=[
            like((4, width, width), BF16),
            like((SEGS, KEYS, width), BF16),
            like((SEGS, KEYS, width), BF16),
            like((SEGS, HALF_ROWS, width), BF16),
            like((SEGS, MEM_PAD, width), BF16),
            like((CHAINED, MEM_PAD, width), BF16),
            like((CHAINED, MEM_PAD, width), BF16),
            like((CHAINED, KEYS, head_rows), F32),
            like((CHAINED, MEM_PAD, width), F32),
            like((CHAINED, MEM_PAD, width), F32),
            like((CHAINED, MEM_PAD, ff), F32),
            like((CHAINED, MEM_PAD, ff), BF16),
        ],
        scratch_shapes=[
            pltpu.VMEM((width, ff), BF16),
            pltpu.VMEM((ff, width), BF16),
            pltpu.SemaphoreType.DMA((2,)),
        ],
        compiler_params=pltpu.CompilerParams(vmem_limit_bytes=60 << 20),
        cost_estimate=pl.CostEstimate(
            flops=2 * SEGS * SEG_LEN * width * width * 5 // 2,
            bytes_accessed=40 << 20,
            transcendentals=0,
        ),
        name="memory_forward",
    )(place, tokens, memory, *pieces, vectors, inner_bias, key_bias, inner_weight, outer_weight)


def lane_masks(rows):
    lane = lax.broadcasted_iota(jnp.int32, (rows, 2 * HEAD_DIM), 1)
    first = (lane < HEAD_DIM).astype(F32)
    return first.astype(BF16), (1.0 - first).astype(BF16)


def pair_of(head):
    start = 2 * HEAD_DIM * (head // 2)
    return slice(start, start + 2 * HEAD_DIM)


def attend_kernel(bias_ref, q_ref, k_ref, v_ref, out_ref, probs_ref):
    bias = bias_ref[0]
    count = q_ref.shape[2] // HEAD_DIM
    q_masks, k_masks = lane_masks(q_ref.shape[1]), lane_masks(KEYS)

    def score(head):
        cols = pair_of(head)
        return nt(k_ref[0, :, cols], q_ref[0, :, cols] * q_masks[head % 2])

    def finish(head, probs, held):
        cols = pair_of(head)
        part = tn(probs, v_ref[0, :, cols] * k_masks[head % 2])
        if head % 2 == 0:
            return part
        out_ref[0, :, cols] = (held + part).astype(BF16)
        return None

    held = before = None
    later = score(0)
    for head in range(count):
        scores = later + bias
        if head + 1 < count:
            later = score(head + 1)
        if before is not None:
            held = finish(head - 1, before, held)
        weights = jnp.exp(scores - jnp.max(scores, axis=0, keepdims=True))
        before = (weights * (1.0 / jnp.sum(weights, axis=0, keepdims=True))).astype(BF16)
        probs_ref[0, head] = before
    finish(count - 1, before, held)


def attend(bias, query, keys, values):
    segs, rows, width = query.shape
    wide = width // 2

    def block(length):
        return pl.BlockSpec((1, length, wide), lambda s, h: (s, 0, h))

    return pl.pallas_call(
        attend_kernel,
        grid=(segs, 2),
        in_specs=[
            pl.BlockSpec((1, KEYS, 1), lambda s, h: (s, 0, 0)),
            block(rows),
            block(KEYS),
            block(KEYS),
        ],
        out_specs=[
            block(rows),
            pl.BlockSpec((1, wide // HEAD_DIM, KEYS, rows), lambda s, h: (s, h, 0, 0)),
        ],
        out_shape=[
            jax.ShapeDtypeStruct(query.shape, BF16),
            jax.ShapeDtypeStruct((segs, width // HEAD_DIM, KEYS, rows), BF16),
        ],
        compiler_params=pltpu.CompilerParams(vmem_limit_bytes=56 << 20),
        cost_estimate=pl.CostEstimate(flops=10**10, bytes_accessed=20 << 20, transcendentals=0),
        name="attend",
    )(bias, query, keys, values)


def attend_back_kernel(q_ref, k_ref, v_ref, d_ref, p_ref, dq_ref, dk_ref, dv_ref):
    count = q_ref.shape[2] // HEAD_DIM
    q_masks, k_masks = lane_masks(q_ref.shape[1]), lane_masks(KEYS)

    def first(head):
        cols = pair_of(head)
        return nt(v_ref[0, :, cols], d_ref[0, :, cols] * q_masks[head % 2])

    def last(head, d_scores, held):
        cols, mask = pair_of(head), q_masks[head % 2]
        dv = nn(p_ref[0, head], d_ref[0, :, cols] * mask)
        dk = nn(d_scores, q_ref[0, :, cols] * mask)
        dq = tn(d_scores, k_ref[0, :, cols] * k_masks[head % 2])
        if head % 2 == 0:
            return dv, dk, dq
        dv_ref[0, :, cols] = held[0] + dv
        dk_ref[0, :, cols] = held[1] + dk
        dq_ref[0, :, cols] = ((held[2] + dq) * SCALE).astype(BF16)
        return None

    held = before = None
    later = first(0)
    for head in range(count):
        d_probs = later
        if head + 1 < count:
            later = first(head + 1)
        if before is not None:
            held = last(head - 1, before, held)
        probs = p_ref[0, head].astype(F32)
        delta = jnp.sum(probs * d_probs, axis=0, keepdims=True)
        before = (probs * (d_probs - delta)).astype(BF16)
    last(count - 1, before, held)


def attend_back(query, keys, values, d_context, probs):
    segs, rows, width = query.shape
    wide = width // 2

    def block(length):
        return pl.BlockSpec((1, length, wide), lambda s, h: (s, 0, h))

    return pl.pallas_call(
        attend_back_kernel,
        grid=(segs, 2),
        in_specs=[
            block(rows),
            block(KEYS),
            block(KEYS),
            block(rows),
            pl.BlockSpec((1, wide // HEAD_DIM, KEYS, rows), lambda s, h: (s, h, 0, 0)),
        ],
        out_specs=[block(rows), block(KEYS), block(KEYS)],
        out_shape=[
            jax.ShapeDtypeStruct(query.shape, BF16),
            jax.ShapeDtypeStruct(keys.shape, F32),
            jax.ShapeDtypeStruct(keys.shape, F32),
        ],
        compiler_params=pltpu.CompilerParams(vmem_limit_bytes=56 << 20),
        cost_estimate=pl.CostEstimate(flops=10**10, bytes_accessed=30 << 20, transcendentals=0),
        name="attend_back",
    )(query, keys, values, d_context, probs)


def feed_kernel(
    rows_ref,
    context_ref,
    cot_ref,
    valid_ref,
    out_weight_ref,
    inner_ref,
    outer_ref,
    vectors_ref,
    inner_bias_ref,
    out_ref,
    normed_ref,
    active_ref,
    d_inner_ref,
    d_total_ref,
    d_hidden_ref,
    d_hidden_low_ref,
    d_context_ref,
    sums_ref,
    slope_ref,
):
    vectors = vectors_ref[...]
    gain_one, gain_two = row_of(vectors, GAIN_ONE), row_of(vectors, GAIN_TWO)
    width = rows_ref.shape[1]
    chunks = [slice(at, at + width) for at in range(0, inner_ref.shape[1], width)]
    valid = valid_ref[...]
    hidden = (
        rows_ref[...].astype(F32)
        + nn(context_ref[...], out_weight_ref[0])
        + row_of(vectors, OUT_BIAS)
    )
    normed, unit_one, root_one = norm_fwd(hidden, gain_one, row_of(vectors, SHIFT_ONE))
    normed_low = normed.astype(BF16)
    normed_ref[...] = normed_low
    total = normed + row_of(vectors, OUTER_BIAS)
    for chunk in chunks:
        inner = nn(normed_low, inner_ref[:, chunk]) + inner_bias_ref[:, chunk]
        active, slope = gelu_parts(inner)
        active = active.astype(BF16)
        active_ref[:, chunk] = active
        slope_ref[:, chunk] = slope
        total = total + nn(active, outer_ref[chunk])
    result, unit_two, root_two = norm_fwd(total, gain_two, row_of(vectors, SHIFT_TWO))
    out_ref[...] = jnp.where(valid > 0.0, result, 0.0)

    d_result = jnp.where(valid > 0.0, cot_ref[...].astype(F32), 0.0)
    d_total = norm_bwd(d_result, unit_two, root_two, gain_two)
    d_total_low = d_total.astype(BF16)
    d_total_ref[...] = d_total_low
    d_normed = d_total
    inner_sums = []
    for chunk in chunks:
        d_inner = (nt(d_total_low, outer_ref[chunk]) * slope_ref[:, chunk]).astype(BF16)
        d_inner_ref[:, chunk] = d_inner
        inner_sums.append(column_sum(d_inner.astype(F32)))
        d_normed = d_normed + nt(d_inner, inner_ref[:, chunk])
    d_hidden = norm_bwd(d_normed, unit_one, root_one, gain_one)
    d_hidden_ref[...] = d_hidden
    d_hidden_low = d_hidden.astype(BF16)
    d_hidden_low_ref[...] = d_hidden_low
    d_context_ref[...] = nt(d_hidden_low, out_weight_ref[0]).astype(BF16)
    sums = [
        column_sum(d_hidden),
        column_sum(d_normed * unit_one),
        column_sum(d_normed),
        column_sum(d_total),
        column_sum(d_result * unit_two),
        column_sum(d_result),
    ] + inner_sums
    sums = jnp.concatenate(sums + [jnp.zeros((SUM_ROWS - len(sums), width), F32)], 0)

    @pl.when(pl.program_id(0) == 0)
    def _():
        sums_ref[...] = sums

    @pl.when(pl.program_id(0) > 0)
    def _():
        sums_ref[...] += sums


SUM_ROWS = 24
QUERY_SUM = 10
VALUE_SUM = 11
MEMORY_SUM = 12


def feed(rows, context, cot, valid, weights, inner_weight, outer_weight, vectors, inner_bias):
    count, width = rows.shape
    ff = inner_weight.shape[1]
    step = HALF_ROWS

    def block(wide):
        return pl.BlockSpec((step, wide), lambda i: (i, 0))

    def fixed(shape, index=(0, 0)):
        return pl.BlockSpec(shape, lambda i: index, pipeline_mode=pl.Buffered(1))

    def like(wide, dtype):
        return jax.ShapeDtypeStruct((count, wide), dtype)

    return pl.pallas_call(
        feed_kernel,
        grid=(count // step,),
        in_specs=[
            block(width),
            block(width),
            block(width),
            block(1),
            fixed((1, width, width), (3, 0, 0)),
            fixed((width, ff)),
            fixed((ff, width)),
            fixed(vectors.shape),
            fixed(inner_bias.shape),
        ],
        out_specs=[
            block(width),
            block(width),
            block(ff),
            block(ff),
            block(width),
            block(width),
            block(width),
            block(width),
            pl.BlockSpec((SUM_ROWS, width), lambda i: (0, 0)),
        ],
        out_shape=[
            like(width, F32),
            like(width, BF16),
            like(ff, BF16),
            like(ff, BF16),
            like(width, BF16),
            like(width, F32),
            like(width, BF16),
            like(width, BF16),
            jax.ShapeDtypeStruct((SUM_ROWS, width), F32),
        ],
        scratch_shapes=[pltpu.VMEM((step, ff), F32)],
        compiler_params=pltpu.CompilerParams(vmem_limit_bytes=60 << 20),
        cost_estimate=pl.CostEstimate(
            flops=2 * count * width * (4 * ff + 2 * width),
            bytes_accessed=40 << 20,
            transcendentals=0,
        ),
        name="feed",
    )(rows, context, cot, valid, weights, inner_weight, outer_weight, vectors, inner_bias)


def memory_backward_kernel(
    place_ref,
    kv_mem_ref,
    weights_ref,
    keys_ref,
    values_ref,
    low_ref,
    mem_query_ref,
    mem_context_ref,
    mem_probs_ref,
    mem_hidden_ref,
    mem_total_ref,
    mem_slope_ref,
    mem_active_ref,
    vectors_ref,
    inner_hbm,
    outer_hbm,
    kv_rows_ref,
    factors_ref,
    d_inner_ref,
    grads_ref,
    sums_ref,
    inner_ref,
    outer_ref,
    grad_ref,
    sems,
):
    copies = [
        pltpu.make_async_copy(outer_hbm, outer_ref, sems.at[0]),
        pltpu.make_async_copy(inner_hbm, inner_ref, sems.at[1]),
    ]
    for copy in copies:
        copy.start()
    side, core = place_ref[0], place_ref[1]
    width = low_ref.shape[2]
    quarter = grads_ref.shape[1]
    vectors = vectors_ref[...]
    gain_one, gain_two = row_of(vectors, GAIN_ONE), row_of(vectors, GAIN_TWO)
    mask = head_mask(width)
    own = pl.ds(core * HALF_ROWS, HALF_ROWS)
    d_memory = None
    sums = None
    queries, hiddens, key_rows, value_rows = [], [], [], []
    for segment in reversed(range(SEGS)):
        d_keys, d_values = kv_mem_ref[0, segment], kv_mem_ref[1, segment]
        if d_memory is None:
            d_next = None
        else:
            normed, unit_one, root_one = norm_fwd(
                mem_hidden_ref[segment], gain_one, row_of(vectors, SHIFT_ONE)
            )
            _, unit_two, root_two = norm_fwd(
                mem_total_ref[segment], gain_two, row_of(vectors, SHIFT_TWO)
            )
            d_total = norm_bwd(d_memory, unit_two, root_two, gain_two)
            d_total_low = d_total.astype(BF16)
            if segment == CHAINED - 1:
                copies[0].wait()
            d_inner = (nt(d_total_low, outer_ref[...]) * mem_slope_ref[segment]).astype(BF16)
            if segment == CHAINED - 1:
                copies[1].wait()
            d_normed = d_total + nt(d_inner, inner_ref[...])
            d_hidden = norm_bwd(d_normed, unit_one, root_one, gain_one)
            d_hidden_low = d_hidden.astype(BF16)
            d_context = spread_heads(nt(d_hidden_low, weights_ref[3]).astype(BF16), mask)
            query = spread_heads(mem_query_ref[segment], mask)
            probs = mem_probs_ref[segment]
            probs_low = probs.astype(BF16)
            d_probs = nt(values_ref[segment], d_context)
            delta = jnp.sum(probs * d_probs, axis=0, keepdims=True)
            d_scores = (probs * (d_probs - delta)).astype(BF16)
            d_query = gather_heads(tn(d_scores, keys_ref[segment]), mask) * SCALE
            d_query = d_query.astype(BF16)
            more_keys = nn(d_scores, query)
            more_values = nn(probs_low, d_context)
            grad_ref[0, :SEG_LEN] = more_keys[:SEG_LEN]
            grad_ref[1, :SEG_LEN] = more_values[:SEG_LEN]
            kv_rows_ref[0, segment] = grad_ref[0, own]
            kv_rows_ref[1, segment] = grad_ref[1, own]
            d_keys = d_keys + more_keys[SEG_LEN:]
            d_values = d_values + more_values[SEG_LEN:]
            d_next = d_hidden + nn(d_query, weights_ref[0])
            queries.append(d_query)
            hiddens.append(d_hidden_low)
            factors_ref[0, segment] = normed.astype(BF16)
            factors_ref[1, segment] = d_total_low
            d_inner_ref[segment] = d_inner
            wide = column_sum(d_inner.astype(F32))
            rows = [
                column_sum(d_hidden),
                column_sum(d_normed * unit_one),
                column_sum(d_normed),
                column_sum(d_total),
                column_sum(d_memory * unit_two),
                column_sum(d_memory),
            ]
            rows += [wide[:, at : at + width] for at in range(0, wide.shape[1], width)]
            rows.append(column_sum(d_query.astype(F32)))
            rows = jnp.concatenate(rows, 0)
            sums = rows if sums is None else sums + rows
        d_keys, d_values = d_keys.astype(BF16), d_values.astype(BF16)
        key_rows.append(d_keys)
        value_rows.append(d_values)
        d_next = 0.0 if d_next is None else d_next
        d_memory = d_next + nn(d_keys, weights_ref[1]) + nn(d_values, weights_ref[2])
    low = [low_ref[segment] for segment in reversed(range(SEGS))]
    low_all = jnp.concatenate(low, 0)
    low_chained = jnp.concatenate(low[1:], 0)
    context = jnp.concatenate([mem_context_ref[s] for s in reversed(range(CHAINED))], 0)
    pairs = (
        (jnp.concatenate(queries, 0), low_chained),
        (jnp.concatenate(key_rows, 0), low_all),
        (jnp.concatenate(value_rows, 0), low_all),
        (context, jnp.concatenate(hiddens, 0)),
    )
    start = pl.ds(pl.multiple_of((2 * side + core) * quarter, quarter), quarter)
    for index, (cols, rows) in enumerate(pairs):
        grad_ref[0, :width] = tn(cols, rows)
        grads_ref[index] = grad_ref[0, start]
    value_sum = column_sum(jnp.concatenate(value_rows, 0).astype(F32))
    filler = SUM_ROWS - MEMORY_SUM - MEM
    sums_ref[...] = jnp.concatenate(
        [sums, value_sum, d_memory[:MEM], jnp.zeros((filler, width), F32)], 0
    )


def memory_backward(place, kv_mem, weights, keys, values, saved, vectors, inner_weight, outer_weight):
    low, mem_query, mem_context, mem_probs, mem_hidden, mem_total, mem_slope, mem_active = saved
    width, ff = inner_weight.shape
    quarter = width // 4
    vmem = pl.BlockSpec(memory_space=pltpu.VMEM)

    def like(shape, dtype):
        return jax.ShapeDtypeStruct(shape, dtype)

    return pl.pallas_call(
        memory_backward_kernel,
        in_specs=[pl.BlockSpec(memory_space=pltpu.SMEM)]
        + [vmem] * 13
        + [pl.BlockSpec(memory_space=pl.ANY)] * 2,
        out_specs=[vmem] * 5,
        out_shape=[
            like((2, CHAINED, HALF_ROWS, width), F32),
            like((2, CHAINED, MEM_PAD, width), BF16),
            like((CHAINED, MEM_PAD, ff), BF16),
            like((4, quarter, width), F32),
            like((SUM_ROWS, width), F32),
        ],
        scratch_shapes=[
            pltpu.VMEM((width, ff), BF16),
            pltpu.VMEM((ff, width), BF16),
            pltpu.VMEM((2, width, width), F32),
            pltpu.SemaphoreType.DMA((2,)),
        ],
        compiler_params=pltpu.CompilerParams(vmem_limit_bytes=60 << 20),
        cost_estimate=pl.CostEstimate(flops=2 * 10**9, bytes_accessed=40 << 20, transcendentals=0),
        name="memory_backward",
    )(
        place,
        kv_mem,
        weights,
        keys,
        values,
        low,
        mem_query,
        mem_context,
        mem_probs,
        mem_hidden,
        mem_total,
        mem_slope,
        mem_active,
        vectors,
        inner_weight,
        outer_weight,
    )


def swap_core(value):
    return lax.ppermute(value, "head", [(0, 1), (1, 0), (2, 3), (3, 2)])


def swap_side(value):
    return lax.ppermute(value, "head", [(0, 2), (2, 0), (1, 3), (3, 1)])


def swap_dp(value, bits):
    size = lax.axis_size("dp")
    return lax.ppermute(value, "dp", [(i, i ^ bits) for i in range(size)])


def fetch_far(value):
    part = lax.axis_index("dp") % 4
    mine = swap_side(lax.dynamic_index_in_dim(value, part, 0, False))
    whole = jnp.zeros(value.shape, value.dtype)
    for bits in range(4):
        other = swap_dp(mine, bits) if bits else mine
        whole = lax.dynamic_update_index_in_dim(whole, other, part ^ bits, 0)
    return whole


def shift_dp(value, step, size, moves):
    perm = [(2 * a + y, 2 * (a + step) + y) for a in moves for y in range(2)]
    return lax.ppermute(value, "dp", perm)


def scatter_dp(value):
    size = value.shape[0]
    if size != 8:
        return lax.psum_scatter(value, "dp", scatter_dimension=0, tiled=False)
    index = lax.axis_index("dp")
    slow, fast = index // 2, index % 2
    long = size // 2
    pairs = value.reshape((long, 2) + value.shape[1:])
    own = lax.dynamic_index_in_dim(pairs, fast, 1, False)
    other = lax.dynamic_index_in_dim(pairs, 1 - fast, 1, False)
    own = own + swap_dp(other, 1)

    def block(at):
        return lax.dynamic_index_in_dim(own, jnp.clip(at, 0, long - 1), 0, False)

    up = down = None
    for step in range(1, long):
        send_up = block(long - step + slow)
        send_down = block(slow - long + step)
        if step > 1:
            send_up, send_down = send_up + up, send_down + down
        up = shift_dp(send_up, 1, size, range(step))
        down = shift_dp(send_down, -1, size, range(long - step, long))
    return block(slow) + up + down


def gather_dp(value):
    size = lax.axis_size("dp")
    if size != 8:
        return lax.all_gather(value, "dp")
    index = lax.axis_index("dp")
    slow, fast = index // 2, index % 2
    long = size // 2
    up = down = value
    line = jnp.zeros((long,) + value.shape, value.dtype)
    line = lax.dynamic_update_index_in_dim(line, value, slow, 0)
    for step in range(1, long):
        up = shift_dp(up, 1, size, range(long - 1))
        down = shift_dp(down, -1, size, range(1, long))
        at_up, at_down = slow - step, slow + step
        line = jnp.where(
            (jnp.arange(long) == at_up).reshape((long,) + (1,) * value.ndim), up[None], line
        )
        line = jnp.where(
            (jnp.arange(long) == at_down).reshape((long,) + (1,) * value.ndim), down[None], line
        )
    other = swap_dp(line, 1)
    first = jnp.where(fast == 0, line, other)
    second = jnp.where(fast == 0, other, line)
    return jnp.stack([first, second], 1).reshape((size,) + value.shape)


def on_device(
    tokens,
    cotangent,
    memory,
    query_weight,
    query_bias,
    key_weight,
    value_weight,
    value_bias,
    out_weight,
    out_bias,
    gain_one,
    shift_one,
    inner_weight,
    inner_bias,
    outer_weight,
    outer_bias,
    gain_two,
    shift_two,
    group_sizes,
    group_section,
    last_valid,
):
    width = memory.shape[1]
    ff = inner_weight.shape[1]
    dp_size = lax.axis_size("dp")
    chain_index = lax.axis_index("dp")
    head_index = lax.axis_index("head")
    side = head_index // 2
    core = head_index % 2
    quarter = query_weight.shape[1]
    place = jnp.stack([side, core]).astype(jnp.int32)

    ends = jnp.cumsum(group_sizes)
    group_index = jnp.sum((ends <= chain_index).astype(jnp.int32))
    section = jnp.sum(jnp.where(jnp.arange(group_sizes.shape[0]) == group_index, group_section, 0))
    count = section % (SEGS - 1) + 2
    positions = jnp.arange(SEG_LEN)
    slots = jnp.arange(SEGS)[:, None]
    token_valid = (slots < count) & ((slots < count - 1) | (positions[None] < last_valid[0]))
    key_bias = jnp.concatenate(
        [
            jnp.where(token_valid, 0.0, MASKED),
            jnp.full((SEGS, MEM), LN_TWO, F32),
            jnp.full((SEGS, MEM_PAD - MEM), MASKED, F32),
        ],
        1,
    )[..., None]

    own_weights = jnp.stack([query_weight.T, key_weight.T, value_weight.T, out_weight])
    wide_weights = own_weights.astype(F32)
    partner = swap_core(wide_weights)
    far = fetch_far(wide_weights)
    far_partner = swap_core(far)
    biases = lax.all_gather(jnp.stack([query_bias, value_bias]), "head")
    biases = biases.transpose(1, 0, 2).reshape(2, width)
    vectors = jnp.concatenate(
        [
            jnp.stack([out_bias, gain_one, shift_one, outer_bias, gain_two, shift_two]),
            biases,
        ],
        0,
    )
    inner_bias_row = inner_bias[None]

    token_rows = tokens.reshape(SEGS, SEG_LEN, width)
    own_start = core * HALF_ROWS
    own_rows = lax.dynamic_slice_in_dim(token_rows, own_start, HALF_ROWS, 1)
    own_flat = own_rows.reshape(SEGS * HALF_ROWS, width)
    own_cot = lax.dynamic_slice_in_dim(
        cotangent.reshape(SEGS, SEG_LEN, width), own_start, HALF_ROWS, 1
    ).reshape(SEGS * HALF_ROWS, width)
    own_valid = lax.dynamic_slice_in_dim(token_valid, own_start, HALF_ROWS, 1)
    own_valid = own_valid.reshape(-1, 1).astype(F32)
    memory_pad = jnp.concatenate(
        [memory.astype(F32), jnp.zeros((MEM_PAD - MEM, width), F32)], 0
    )

    weights, keys, values, own_query, *saved = memory_forward(
        place,
        token_rows,
        memory_pad,
        (own_weights, partner, far, far_partner),
        vectors,
        inner_bias_row,
        key_bias,
        inner_weight,
        outer_weight,
    )
    context, probs = attend(key_bias, own_query, keys, values)
    context_flat = context.reshape(-1, width)
    own_out, normed_low, active, d_inner, d_total_low, d_hidden, d_hidden_low, d_context, sums = feed(
        own_flat,
        context_flat,
        own_cot,
        own_valid,
        weights,
        inner_weight,
        outer_weight,
        vectors,
        inner_bias_row,
    )
    d_query, d_keys, d_values = attend_back(
        own_query, keys, values, d_context.reshape(own_query.shape), probs
    )

    kv_mem = jnp.stack([d_keys[:, SEG_LEN:], d_values[:, SEG_LEN:]])
    kv_mem = kv_mem + swap_core(kv_mem)
    other_start = HALF_ROWS - own_start
    d_kv_other = jnp.stack(
        [lax.dynamic_slice_in_dim(v, other_start, HALF_ROWS, 1) for v in (d_keys, d_values)]
    )
    d_kv_own = jnp.stack(
        [lax.dynamic_slice_in_dim(v, own_start, HALF_ROWS, 1) for v in (d_keys, d_values)]
    )
    d_kv_own = d_kv_own + swap_core(d_kv_other)

    kv_more, mem_factors, mem_d_inner, mem_grads, mem_sums = memory_backward(
        place, kv_mem, weights, keys, values, saved, vectors, inner_weight, outer_weight
    )
    mem_active = saved[7]
    kv_more = jnp.concatenate([kv_more, jnp.zeros((2, 1, HALF_ROWS, width), F32)], 1)
    d_kv_low = (d_kv_own + kv_more).astype(BF16).reshape(2, SEGS * HALF_ROWS, width)
    d_query = d_query.reshape(-1, width)
    d_inputs = (
        d_hidden
        + nn(d_query, weights[0])
        + nn(d_kv_low[0], weights[1])
        + nn(d_kv_low[1], weights[2])
    )

    half = 2 * quarter

    def of_side(value):
        return lax.dynamic_slice_in_dim(value, side * half, half, 1)

    attn = jnp.stack(
        [
            tn(of_side(d_query), own_flat),
            tn(of_side(d_kv_low[0]), own_flat),
            tn(of_side(d_kv_low[1]), own_flat),
            tn(of_side(context_flat), d_hidden_low),
        ]
    ).reshape(4, 2, quarter, width)
    attn_own = lax.dynamic_index_in_dim(attn, core, 1, False)
    attn_other = lax.dynamic_index_in_dim(attn, 1 - core, 1, False)
    attn_grads = attn_own + swap_core(attn_other) + mem_grads

    d_half = width // 2

    def of_d(value):
        return lax.dynamic_slice_in_dim(value, side * d_half, d_half, 1)

    def with_mem(main, mem):
        return jnp.concatenate([main, lax.dynamic_index_in_dim(mem, core, 0, False)], 0)

    ffn = jnp.stack(
        [
            tn(with_mem(d_inner, mem_d_inner), of_d(with_mem(normed_low, mem_factors[0]))),
            tn(with_mem(active, mem_active), of_d(with_mem(d_total_low, mem_factors[1]))),
        ]
    )
    piece = ff // dp_size
    ffn = ffn.reshape(2, dp_size, 2, piece // 2, d_half)
    ffn_own = lax.dynamic_index_in_dim(ffn, core, 2, False)
    ffn_other = lax.dynamic_index_in_dim(ffn, 1 - core, 2, False)
    ffn_own = ffn_own + swap_core(ffn_other)
    ffn_shard = jnp.stack([scatter_dp(ffn_own[0]), scatter_dp(ffn_own[1])])
    ffn_all = lax.all_gather(ffn_shard, "head")
    ffn_all = ffn_all.reshape(2, 2, 2, piece // 2, d_half)
    ffn_all = ffn_all.transpose(2, 1, 3, 0, 4).reshape(2, piece, width)
    grad_inner = ffn_all[0].T
    grad_outer = ffn_all[1]

    bias_sums = jnp.stack(
        [jnp.sum(d_query.astype(F32), 0), jnp.sum(d_kv_low[1].astype(F32), 0)]
    )
    sums = jnp.concatenate([sums[:QUERY_SUM], bias_sums], 0)
    sums = sums + swap_core(sums)
    sums = jnp.concatenate([sums, jnp.zeros((SUM_ROWS - MEMORY_SUM, width), F32)], 0) + mem_sums
    dense_rows = 4 * quarter
    dense = jnp.concatenate(
        [
            attn_grads.reshape(dense_rows, width),
            sums,
            jnp.zeros((-(dense_rows + SUM_ROWS) % 64, width), F32),
        ],
        0,
    )
    dense = gather_dp(scatter_dp(dense.reshape(dp_size, -1, width))).reshape(-1, width)
    attn_grads = dense[:dense_rows].reshape(4, quarter, width)
    sums = dense[dense_rows:]
    inner_bias_grad = lax.dynamic_slice_in_dim(
        sums[6:QUERY_SUM].reshape(-1), chain_index * piece, piece, 0
    )
    grad_qb = lax.dynamic_slice_in_dim(sums[QUERY_SUM], head_index * quarter, quarter, 0)
    grad_vb = lax.dynamic_slice_in_dim(sums[VALUE_SUM], head_index * quarter, quarter, 0)
    grad_memory = sums[MEMORY_SUM : MEMORY_SUM + MEM]

    def both_cores(own):
        other = swap_core(own)
        first = jnp.where(core == 0, own, other).reshape(SEGS, HALF_ROWS, width)
        second = jnp.where(core == 0, other, own).reshape(SEGS, HALF_ROWS, width)
        return jnp.concatenate([first, second], 1).reshape(SEGS * SEG_LEN, width)

    layer_out = both_cores(own_out)
    grad_tokens = both_cores(d_inputs)
    return (
        layer_out,
        grad_tokens,
        grad_memory,
        attn_grads[0].T,
        grad_qb,
        attn_grads[1].T,
        attn_grads[2].T,
        grad_vb,
        attn_grads[3],
        sums[0],
        sums[1],
        sums[2],
        grad_inner,
        inner_bias_grad,
        grad_outer,
        sums[3],
        sums[4],
        sums[5],
    )


def solution(mesh):
    row, col, vec, every = P("dp", None), P(None, "head"), P("head"), P()
    placed = (row, row, every, col, vec, col, col, vec, P("head", None)) + (every,) * 11
    return jax.shard_map(
        on_device,
        mesh=mesh,
        in_specs=placed + (P("dp"),),
        out_specs=(
            row,
            row,
            every,
            col,
            vec,
            col,
            col,
            vec,
            P("head", None),
            every,
            every,
            every,
            P(None, "dp"),
            P("dp"),
            row,
            every,
            every,
            every,
        ),
        check_vma=False,
    )
```

```python
from functools import partial

import jax
import jax.numpy as jnp
from jax import lax
from jax.experimental import pallas as pl
from jax.experimental.pallas import tpu as pltpu
from jax.sharding import PartitionSpec as P

HEAD_DIM = 64
MEM = 10
MEM_PAD = 16
SEG_LEN = 512
SEGS = 3
CHAINED = SEGS - 1
KEYS = SEG_LEN + MEM_PAD
HALF_ROWS = SEG_LEN // 2
EPS = 1e-06
SCALE = HEAD_DIM ** (-0.5)
MASKED = -1000000000.0
LN_TWO = 0.6931471805599453

F32 = jnp.float32
BF16 = jnp.bfloat16


def nn(left, right):
    return jnp.dot(left, right, preferred_element_type=F32)


def nt(left, right):
    return lax.dot_general(left, right, (((1,), (1,)), ((), ())), preferred_element_type=F32)


def tn(left, right):
    return lax.dot_general(left, right, (((0,), (0,)), ((), ())), preferred_element_type=F32)


def norm_fwd(value, gain, shift):
    centered = value - jnp.mean(value, axis=-1, keepdims=True)
    spread = jnp.mean(centered * centered, axis=-1, keepdims=True)
    root = lax.rsqrt(spread + EPS)
    unit = centered * root
    return unit * gain + shift, unit, root


def norm_bwd(d_out, unit, root, gain):
    d_unit = d_out * gain
    mean_one = jnp.mean(d_unit, axis=-1, keepdims=True)
    mean_two = jnp.mean(d_unit * unit, axis=-1, keepdims=True)
    return root * (d_unit - mean_one - unit * mean_two)


def gelu_parts(inner):
    cdf = 0.5 * (1.0 + lax.erf(inner * 0.7071067811865476))
    pdf = jnp.exp(-0.5 * inner * inner) * 0.3989422804014327
    return inner * cdf, cdf + inner * pdf


def column_sum(value):
    return jnp.sum(value, axis=0, keepdims=True)


SIDE, CORE, PART, CHAIN = range(4)


def limit_of(segment, place_ref, sizes_ref, sections_ref, last_ref):
    chain = place_ref[CHAIN]
    end, section = 0, 0
    for group in range(sizes_ref.shape[0]):
        start, end = end, end + sizes_ref[group]
        inside = jnp.logical_and(start <= chain, chain < end)
        section = jnp.where(inside, sections_ref[group], section)
    last = section % (SEGS - 1) + 1
    return jnp.where(segment < last, SEG_LEN, jnp.where(segment == last, last_ref[0], 0))


def key_bias(limit):
    row = lax.broadcasted_iota(jnp.int32, (KEYS, 1), 0)
    beyond = jnp.where((row >= SEG_LEN) & (row < SEG_LEN + MEM), LN_TWO, MASKED)
    return jnp.where(row < limit, 0.0, beyond)


OUT_BIAS, GAIN_ONE, SHIFT_ONE, OUTER_BIAS, GAIN_TWO, SHIFT_TWO, QUERY_BIAS, VALUE_BIAS = range(8)
INNER_BIAS = 8
VECTOR_ROWS = 16


def row_of(vectors, index):
    return vectors[index : index + 1]


def head_mask(width):
    count = width // HEAD_DIM
    shape = (count, MEM_PAD, width)
    head = lax.broadcasted_iota(jnp.int32, shape, 0)
    lane = lax.broadcasted_iota(jnp.int32, shape, 2) // HEAD_DIM
    return (head == lane).astype(F32)


def spread_heads(value, mask):
    count, rows, width = mask.shape
    return (value.astype(F32)[None] * mask).reshape(count * rows, width).astype(BF16)


def gather_heads(value, mask):
    return jnp.sum(value.reshape(mask.shape) * mask, axis=0)


def memory_forward_kernel(
    place_ref,
    sizes_ref,
    sections_ref,
    last_ref,
    tokens_ref,
    memory_ref,
    own_q_ref,
    own_k_ref,
    own_v_ref,
    own_o_ref,
    partner_ref,
    far_refs,
    far_partner_refs,
    vectors_ref,
    inner_hbm,
    outer_hbm,
    weights_hbm,
    keys_hbm,
    values_hbm,
    query_hbm,
    *refs,
):
    saved_hbm, (weights_ref, keys_ref, values_ref, query_ref) = refs[:9], refs[9:13]
    saved, (inner_ref, outer_ref, sems) = refs[13:22], refs[22:]
    (
        low_ref,
        mem_query_ref,
        mem_context_ref,
        mem_probs_ref,
        mem_hidden_ref,
        mem_total_ref,
        mem_slope_ref,
        mem_active_ref,
        mem_normed_ref,
    ) = saved
    copies = [
        pltpu.make_async_copy(inner_hbm, inner_ref, sems.at[0]),
        pltpu.make_async_copy(outer_hbm, outer_ref, sems.at[1]),
    ]
    for copy in copies:
        copy.start()
    side, core, part = place_ref[SIDE], place_ref[CORE], place_ref[PART]
    quarter = own_q_ref.shape[0]
    width = memory_ref.shape[1]

    def span_of(at_side, at_core):
        return pl.ds(pl.multiple_of((2 * at_side + at_core) * quarter, quarter), quarter)

    for which, ref in enumerate((own_q_ref, own_k_ref, own_v_ref, own_o_ref)):
        weights_ref[which, span_of(side, core)] = ref[...]
        weights_ref[which, span_of(side, 1 - core)] = partner_ref[which].astype(BF16)
    for bits in range(4):
        which = part ^ bits
        weights_ref[which, span_of(1 - side, core)] = far_refs[bits][...].astype(BF16)
        weights_ref[which, span_of(1 - side, 1 - core)] = far_partner_refs[bits][...].astype(BF16)
    writes = [pltpu.make_async_copy(weights_ref, weights_hbm, sems.at[2])]
    writes[0].start()
    vectors = vectors_ref[...]
    query_bias = row_of(vectors, QUERY_BIAS)
    value_bias = row_of(vectors, VALUE_BIAS)

    def project(index, carry):
        segment, half = index // 2, index % 2
        span = pl.ds(half * HALF_ROWS, HALF_ROWS)
        rows = tokens_ref[segment, span]
        keys_ref[segment, span] = nt(rows, weights_ref[1]).astype(BF16)
        values_ref[segment, span] = (nt(rows, weights_ref[2]) + value_bias).astype(BF16)

        @pl.when(half == core)
        def _():
            query_ref[segment] = (nt(rows, weights_ref[0]) + query_bias).astype(BF16) * SCALE

        return carry

    lax.fori_loop(0, 2 * SEGS, project, 0)
    token_rows, mem_rows = pl.ds(0, SEG_LEN), pl.ds(SEG_LEN, MEM_PAD)
    pairs = ((keys_ref, keys_hbm), (values_ref, values_hbm))
    writes.append(pltpu.make_async_copy(query_ref, query_hbm, sems.at[3]))
    for index, (ref, hbm) in enumerate(pairs):
        writes.append(
            pltpu.make_async_copy(ref.at[:, token_rows], hbm.at[:, token_rows], sems.at[4 + index])
        )
    for write in writes[1:]:
        write.start()

    mask = head_mask(width)
    now = jnp.concatenate(
        [memory_ref[...].astype(F32), jnp.zeros((MEM_PAD - MEM, width), F32)], 0
    )
    for segment in range(SEGS):
        low = now.astype(BF16)
        low_ref[segment] = low
        keys_ref[segment, SEG_LEN:] = nt(low, weights_ref[1]).astype(BF16)
        values_ref[segment, SEG_LEN:] = (nt(low, weights_ref[2]) + value_bias).astype(BF16)
        if segment == CHAINED:
            break
        query = (nt(low, weights_ref[0]) + query_bias).astype(BF16) * SCALE
        mem_query_ref[segment] = query
        scores = nt(keys_ref[segment], spread_heads(query, mask))
        limit = limit_of(segment, place_ref, sizes_ref, sections_ref, last_ref)
        scores = scores + key_bias(limit)
        weights = jnp.exp(scores - jnp.max(scores, axis=0, keepdims=True))
        probs = weights * (1.0 / jnp.sum(weights, axis=0, keepdims=True))
        mem_probs_ref[segment] = probs
        context = gather_heads(tn(probs.astype(BF16), values_ref[segment]), mask).astype(BF16)
        mem_context_ref[segment] = context
        hidden = now + nn(context, weights_ref[3]) + row_of(vectors, OUT_BIAS)
        mem_hidden_ref[segment] = hidden
        normed, _, _ = norm_fwd(hidden, row_of(vectors, GAIN_ONE), row_of(vectors, SHIFT_ONE))
        mem_normed_ref[segment] = normed.astype(BF16)
        if segment == 0:
            copies[0].wait()
        inner_bias = [row_of(vectors, INNER_BIAS + i) for i in range(inner_ref.shape[1] // width)]
        inner_bias = jnp.concatenate(inner_bias, 1)
        active, slope = gelu_parts(nn(normed.astype(BF16), inner_ref[...]) + inner_bias)
        active = active.astype(BF16)
        mem_slope_ref[segment] = slope
        mem_active_ref[segment] = active
        if segment == 0:
            copies[1].wait()
        total = normed + nn(active, outer_ref[...]) + row_of(vectors, OUTER_BIAS)
        mem_total_ref[segment] = total
        now, _, _ = norm_fwd(total, row_of(vectors, GAIN_TWO), row_of(vectors, SHIFT_TWO))
    for index, (ref, hbm) in enumerate(pairs):
        writes.append(
            pltpu.make_async_copy(ref.at[:, mem_rows], hbm.at[:, mem_rows], sems.at[6 + index])
        )
        writes[-1].start()
    for index, (ref, hbm) in enumerate(zip(saved, saved_hbm)):
        writes.append(pltpu.make_async_copy(ref, hbm, sems.at[8 + index]))
        writes[-1].start()
    for write in writes:
        write.wait()


def memory_forward(
    scalars, tokens, memory, own, partner, far, far_partner, vectors, inner_weight, outer_weight
):
    width = memory.shape[1]
    ff = inner_weight.shape[1]
    head_rows = MEM_PAD * width // HEAD_DIM
    vmem = pl.BlockSpec(memory_space=pltpu.VMEM)

    def like(shape, dtype):
        return jax.ShapeDtypeStruct(shape, dtype)

    saved = [
        ((SEGS, MEM_PAD, width), BF16),
        ((CHAINED, MEM_PAD, width), BF16),
        ((CHAINED, MEM_PAD, width), BF16),
        ((CHAINED, KEYS, head_rows), F32),
        ((CHAINED, MEM_PAD, width), F32),
        ((CHAINED, MEM_PAD, width), F32),
        ((CHAINED, MEM_PAD, ff), F32),
        ((CHAINED, MEM_PAD, ff), BF16),
        ((CHAINED, MEM_PAD, width), BF16),
    ]
    large = [
        ((4, width, width), BF16),
        ((SEGS, KEYS, width), BF16),
        ((SEGS, KEYS, width), BF16),
        ((SEGS, HALF_ROWS, width), BF16),
    ]
    return pl.pallas_call(
        memory_forward_kernel,
        in_specs=[pl.BlockSpec(memory_space=pltpu.SMEM)] * 4
        + [vmem] * 7
        + [[vmem] * 4] * 2
        + [vmem]
        + [pl.BlockSpec(memory_space=pl.ANY)] * 2,
        out_specs=[pl.BlockSpec(memory_space=pltpu.HBM)] * 13,
        out_shape=[pltpu.HBM(*shape) for shape in large + saved],
        scratch_shapes=[pltpu.VMEM(*shape) for shape in large + saved]
        + [
            pltpu.VMEM((width, ff), BF16),
            pltpu.VMEM((ff, width), BF16),
            pltpu.SemaphoreType.DMA((17,)),
        ],
        compiler_params=pltpu.CompilerParams(vmem_limit_bytes=46 << 20),
        cost_estimate=pl.CostEstimate(flops=1000, bytes_accessed=1000, transcendentals=0),
        name="memory_forward",
    )(
        *scalars,
        tokens,
        memory,
        *own,
        partner,
        far,
        far_partner,
        vectors,
        inner_weight,
        outer_weight,
    )


def lane_masks(rows):
    lane = lax.broadcasted_iota(jnp.int32, (rows, 2 * HEAD_DIM), 1)
    first = (lane < HEAD_DIM).astype(F32)
    return first.astype(BF16), (1.0 - first).astype(BF16)


def pair_of(head):
    start = 2 * HEAD_DIM * (head // 2)
    return slice(start, start + 2 * HEAD_DIM)


def attend_kernel(
    place_ref, sizes_ref, sections_ref, last_ref, q_ref, k_ref, v_ref, out_ref, probs_ref
):
    limit = limit_of(pl.program_id(0), place_ref, sizes_ref, sections_ref, last_ref)
    bias = key_bias(limit)
    count = q_ref.shape[2] // HEAD_DIM
    q_masks, k_masks = lane_masks(q_ref.shape[1]), lane_masks(KEYS)

    def score(head):
        cols = pair_of(head)
        return nt(k_ref[0, :, cols], q_ref[0, :, cols] * q_masks[head % 2])

    def finish(head, probs, held):
        cols = pair_of(head)
        part = tn(probs, v_ref[0, :, cols] * k_masks[head % 2])
        if head % 2 == 0:
            return part
        out_ref[0, :, cols] = (held + part).astype(BF16)
        return None

    held = before = None
    later = score(0)
    for head in range(count):
        scores = later + bias
        if head + 1 < count:
            later = score(head + 1)
        if before is not None:
            held = finish(head - 1, before, held)
        weights = jnp.exp(scores - jnp.max(scores, axis=0, keepdims=True))
        before = (weights * (1.0 / jnp.sum(weights, axis=0, keepdims=True))).astype(BF16)
        probs_ref[0, head] = before
    finish(count - 1, before, held)


def attend(scalars, query, keys, values):
    segs, rows, width = query.shape
    wide = width // 2

    def block(length):
        return pl.BlockSpec((1, length, wide), lambda s, h, *_: (s, 0, h))

    return pl.pallas_call(
        attend_kernel,
        grid_spec=pltpu.PrefetchScalarGridSpec(
            num_scalar_prefetch=4,
            grid=(segs, 2),
            in_specs=[block(rows), block(KEYS), block(KEYS)],
            out_specs=[
                block(rows),
                pl.BlockSpec((1, wide // HEAD_DIM, KEYS, rows), lambda s, h, *_: (s, h, 0, 0)),
            ],
        ),
        out_shape=[
            jax.ShapeDtypeStruct(query.shape, BF16),
            jax.ShapeDtypeStruct((segs, width // HEAD_DIM, KEYS, rows), BF16),
        ],
        compiler_params=pltpu.CompilerParams(vmem_limit_bytes=56 << 20),
        cost_estimate=pl.CostEstimate(flops=1000, bytes_accessed=1000, transcendentals=0),
        name="attend",
    )(*scalars, query, keys, values)


def in_step_kernel(*refs):
    pass


def in_step(*values):
    anywhere = [pl.BlockSpec(memory_space=pl.ANY)] * len(values)
    return pl.pallas_call(
        in_step_kernel,
        in_specs=anywhere,
        out_specs=anywhere,
        out_shape=[jax.ShapeDtypeStruct(value.shape, value.dtype) for value in values],
        input_output_aliases={i: i for i in range(len(values))},
        name="in_step",
    )(*values)


def attend_back_kernel(through, place_ref, q_ref, k_ref, v_ref, d_ref, p_ref, *refs):
    dq_ref, own_ref, other_ref, mem_ref = refs[through:][:4]
    first_core = place_ref[CORE] == 0
    count = q_ref.shape[2] // HEAD_DIM
    q_masks, k_masks = lane_masks(q_ref.shape[1]), lane_masks(KEYS)

    def first(head):
        cols = pair_of(head)
        return nt(v_ref[0, :, cols], d_ref[0, :, cols] * q_masks[head % 2])

    def last(head, d_scores, held):
        cols, mask = pair_of(head), q_masks[head % 2]
        dv = nn(p_ref[0, head], d_ref[0, :, cols] * mask)
        dk = nn(d_scores, q_ref[0, :, cols] * mask)
        dq = tn(d_scores, k_ref[0, :, cols] * k_masks[head % 2])
        if head % 2 == 0:
            return dv, dk, dq
        for index, value in enumerate((held[1] + dk, held[0] + dv)):
            low, high = value[:HALF_ROWS], value[HALF_ROWS:SEG_LEN]
            own_ref[index, 0, :, cols] = jnp.where(first_core, low, high)
            other_ref[index, 0, :, cols] = jnp.where(first_core, high, low)
            mem_ref[index, 0, :, cols] = value[SEG_LEN:]
        dq_ref[0, :, cols] = ((held[2] + dq) * SCALE).astype(BF16)
        return None

    held = before = None
    later = first(0)
    for head in range(count):
        d_probs = later
        if head + 1 < count:
            later = first(head + 1)
        if before is not None:
            held = last(head - 1, before, held)
        probs = p_ref[0, head].astype(F32)
        delta = jnp.sum(probs * d_probs, axis=0, keepdims=True)
        before = (probs * (d_probs - delta)).astype(BF16)
    last(count - 1, before, held)


def attend_back(place, query, keys, values, d_context, probs, first, count, held=(), through=()):
    segs, rows, width = query.shape
    wide = width // 2

    def block(length):
        return pl.BlockSpec((1, length, wide), lambda s, h, place: (first + s, 0, h))

    def two(length):
        return pl.BlockSpec((2, 1, length, wide), lambda s, h, place: (0, first + s, 0, h))

    inputs = (query, keys, values, d_context, probs)
    at = 1 + len(inputs)
    aliases = {at + i: i for i in range(len(held))}
    aliases.update({at + len(held) + i: 4 + i for i in range(len(through))})
    return pl.pallas_call(
        partial(attend_back_kernel, len(held) + len(through)),
        grid_spec=pltpu.PrefetchScalarGridSpec(
            num_scalar_prefetch=1,
            grid=(count, 2),
            in_specs=[
                block(rows),
                block(KEYS),
                block(KEYS),
                block(rows),
                pl.BlockSpec(
                    (1, wide // HEAD_DIM, KEYS, rows),
                    lambda s, h, place: (first + s, h, 0, 0),
                ),
            ]
            + [pl.BlockSpec(memory_space=pl.ANY)] * (len(held) + len(through)),
            out_specs=[block(rows), two(HALF_ROWS), two(HALF_ROWS), two(MEM_PAD)]
            + [pl.BlockSpec(memory_space=pl.ANY)] * len(through),
        ),
        out_shape=[
            jax.ShapeDtypeStruct(query.shape, BF16),
            jax.ShapeDtypeStruct((2, segs, HALF_ROWS, width), F32),
            jax.ShapeDtypeStruct((2, segs, HALF_ROWS, width), F32),
            jax.ShapeDtypeStruct((2, segs, MEM_PAD, width), F32),
        ]
        + [jax.ShapeDtypeStruct(value.shape, value.dtype) for value in through],
        input_output_aliases=aliases,
        compiler_params=pltpu.CompilerParams(vmem_limit_bytes=60 << 20),
        cost_estimate=pl.CostEstimate(flops=1000, bytes_accessed=1000, transcendentals=0),
        name="attend_back",
    )(place, *inputs, *held, *through)


SUM_ROWS = 24
QUERY_SUM = 10
VALUE_SUM = 11
MEMORY_SUM = 12


def feed_kernel(
    place_ref,
    sizes_ref,
    sections_ref,
    last_ref,
    rows_ref,
    context_ref,
    cot_ref,
    out_weight_ref,
    inner_ref,
    outer_ref,
    vectors_ref,
    out_ref,
    out_rows_ref,
    d_hidden_ref,
    d_hidden_low_ref,
    d_context_ref,
    sums_ref,
    own_inner_hbm,
    own_outer_hbm,
    other_inner_hbm,
    other_outer_hbm,
    slope_ref,
    active_ref,
    grads_ref,
    sems,
):
    segment = pl.program_id(0)
    side, core = place_ref[SIDE], place_ref[CORE]
    vectors = vectors_ref[...]
    gain_one, gain_two = row_of(vectors, GAIN_ONE), row_of(vectors, GAIN_TWO)
    width = vectors.shape[1]
    half = width // 2
    quarter = width // 4
    chunks = [slice(at, at + width) for at in range(0, inner_ref.shape[1], width)]
    row = lax.broadcasted_iota(jnp.int32, (HALF_ROWS, 1), 0) + core * HALF_ROWS
    valid = row < limit_of(segment, place_ref, sizes_ref, sections_ref, last_ref)

    def of_side(value):
        return jnp.where(side == 0, value[:, :half], value[:, half:])

    def add_grads(which, index, value):
        for row_half in range(2):
            rows = value[quarter * row_half : quarter * (row_half + 1)]
            for part in range(2):
                at = 2 * index + part
                held = jnp.where(segment == 0, 0.0, grads_ref[which, row_half, at])
                grads_ref[which, row_half, at] = held + rows[:, half * part : half * (part + 1)]

    hidden = (
        rows_ref[0].astype(F32)
        + nn(context_ref[0], out_weight_ref[0])
        + row_of(vectors, OUT_BIAS)
    )
    normed, unit_one, root_one = norm_fwd(hidden, gain_one, row_of(vectors, SHIFT_ONE))
    normed_low = normed.astype(BF16)
    total = normed + row_of(vectors, OUTER_BIAS)
    for index, chunk in enumerate(chunks):
        inner = nn(normed_low, inner_ref[:, chunk]) + row_of(vectors, INNER_BIAS + index)
        active, slope = gelu_parts(inner)
        active = active.astype(BF16)
        active_ref[:, chunk] = active
        slope_ref[:, chunk] = slope
        total = total + nn(active, outer_ref[chunk])
    result, unit_two, root_two = norm_fwd(total, gain_two, row_of(vectors, SHIFT_TWO))
    result = jnp.where(valid, result, 0.0)
    out_ref[0] = result
    out_rows_ref[0] = result

    d_result = jnp.where(valid, cot_ref[0].astype(F32), 0.0)
    d_total = norm_bwd(d_result, unit_two, root_two, gain_two)
    d_total_low = d_total.astype(BF16)
    normed_half, d_total_half = of_side(normed_low), of_side(d_total_low)
    d_normed = d_total
    inner_sums = []
    for index, chunk in enumerate(chunks):
        d_inner = (nt(d_total_low, outer_ref[chunk]) * slope_ref[:, chunk]).astype(BF16)
        inner_sums.append(column_sum(d_inner.astype(F32)))
        d_normed = d_normed + nt(d_inner, inner_ref[:, chunk])
        add_grads(0, index, tn(normed_half, d_inner))
        add_grads(1, index, tn(d_total_half, active_ref[:, chunk]))
    final = segment == pl.num_programs(0) - 1
    targets = ((other_inner_hbm, own_inner_hbm), (other_outer_hbm, own_outer_hbm))
    copies = [
        pltpu.make_async_copy(
            grads_ref.at[which, core if own else 1 - core],
            targets[which][own],
            sems.at[which, own],
        )
        for own in range(2)
        for which in range(2)
    ]

    @pl.when(final)
    def _():
        for copy in copies:
            copy.start()

    d_hidden = norm_bwd(d_normed, unit_one, root_one, gain_one)
    d_hidden_ref[0] = d_hidden
    d_hidden_low = d_hidden.astype(BF16)
    d_hidden_low_ref[0] = d_hidden_low
    d_context_ref[0] = nt(d_hidden_low, out_weight_ref[0]).astype(BF16)
    sums = [
        column_sum(d_hidden),
        column_sum(d_normed * unit_one),
        column_sum(d_normed),
        column_sum(d_total),
        column_sum(d_result * unit_two),
        column_sum(d_result),
    ] + inner_sums
    sums = jnp.concatenate(sums + [jnp.zeros((SUM_ROWS - len(sums), width), F32)], 0)

    @pl.when(segment == 0)
    def _():
        sums_ref[...] = sums

    @pl.when(segment > 0)
    def _():
        sums_ref[...] += sums

    @pl.when(final)
    def _():
        for copy in copies:
            copy.wait()


def feed(scalars, tokens, context, cot, weights, inner_weight, outer_weight, vectors):
    width, ff = inner_weight.shape
    chunk = width // 2

    def own_half():
        return pl.BlockSpec((1, HALF_ROWS, width), lambda i, place, *_: (i, place[CORE], 0))

    def segment():
        return pl.BlockSpec((1, HALF_ROWS, width), lambda i, *_: (i, 0, 0))

    def fixed(shape, index=(0, 0)):
        return pl.BlockSpec(shape, lambda i, *_: index, pipeline_mode=pl.Buffered(1))

    like = pltpu.HBM
    per_segment = (SEGS, HALF_ROWS, width)
    grads_shape = (ff // chunk, width // 4, chunk)
    return pl.pallas_call(
        feed_kernel,
        grid_spec=pltpu.PrefetchScalarGridSpec(
            num_scalar_prefetch=4,
            grid=(SEGS,),
            in_specs=[
                own_half(),
                segment(),
                own_half(),
                fixed((1, width, width), (3, 0, 0)),
                fixed((width, ff)),
                fixed((ff, width)),
                fixed(vectors.shape),
            ],
            out_specs=[
                own_half(),
                segment(),
                segment(),
                segment(),
                segment(),
                pl.BlockSpec((SUM_ROWS, width), lambda i, *_: (0, 0)),
            ]
            + [pl.BlockSpec(memory_space=pl.ANY)] * 4,
            scratch_shapes=[
                pltpu.VMEM((HALF_ROWS, ff), F32),
                pltpu.VMEM((HALF_ROWS, ff), BF16),
                pltpu.VMEM((2, 2) + grads_shape, F32),
                pltpu.SemaphoreType.DMA((2, 2)),
            ],
        ),
        out_shape=[
            like((SEGS, SEG_LEN, width), F32),
            like(per_segment, F32),
            like(per_segment, F32),
            like(per_segment, BF16),
            like(per_segment, BF16),
            like((SUM_ROWS, width), F32),
        ]
        + [like(grads_shape, F32)] * 4,
        compiler_params=pltpu.CompilerParams(vmem_limit_bytes=50 << 20),
        cost_estimate=pl.CostEstimate(flops=1000, bytes_accessed=1000, transcendentals=0),
        name="feed",
    )(*scalars, tokens, context, cot, weights, inner_weight, outer_weight, vectors)


BLOCKS = 8
SUM_PART = SUM_ROWS // BLOCKS
SUM_SPACE = 8


def block_rows(width):
    rows = width // 4 // BLOCKS
    return 2 * rows, 2 * rows + SUM_SPACE


def to_blocks(ref, matrices, sums=None):
    rows = (ref.shape[1] - (0 if sums is None else SUM_SPACE)) // 2
    for block in range(BLOCKS):
        for index, matrix in enumerate(matrices):
            ref[block, rows * index : rows * (index + 1)] = matrix(rows * block, rows)
        if sums is not None:
            part = sums[SUM_PART * block : SUM_PART * (block + 1)]
            filler = jnp.zeros((SUM_SPACE - SUM_PART, part.shape[1]), F32)
            ref[block, 2 * rows :] = jnp.concatenate([part, filler], 0)


def memory_backward_kernel(
    packed,
    place_ref,
    kv_mem_ref,
    low_ref,
    mem_query_ref,
    mem_context_ref,
    mem_probs_ref,
    mem_hidden_ref,
    mem_total_ref,
    mem_slope_ref,
    mem_active_ref,
    mem_normed_ref,
    vectors_ref,
    weights_hbm,
    keys_hbm,
    values_hbm,
    inner_hbm,
    outer_hbm,
    kv_rows_ref,
    query_dense_ref,
    dense_ref,
    *refs,
):
    share_refs, refs = refs[:-9], refs[-9:]
    weights_ref, keys_ref, values_ref, inner_ref, outer_ref, grad_ref, d_inner_ref, d_total_ref, sems = refs
    order = [(weights_hbm.at[at], weights_ref.at[at]) for at in (1, 2)]
    order += [(outer_hbm, outer_ref), (inner_hbm, inner_ref)]
    order += [(weights_hbm.at[3], weights_ref.at[3])]
    for segment in reversed(range(CHAINED)):
        order += [(values_hbm.at[segment], values_ref.at[segment])]
        order += [(keys_hbm.at[segment], keys_ref.at[segment])]
        if segment == CHAINED - 1:
            order += [(weights_hbm.at[0], weights_ref.at[0])]
    copies = [
        pltpu.make_async_copy(source, target, sems.at[index])
        for index, (source, target) in enumerate(order)
    ]
    for copy in copies:
        copy.start()
    arrived = iter(copies)

    def wait(count):
        for _ in range(count):
            next(arrived).wait()

    side, core = place_ref[0], place_ref[1]
    width = low_ref.shape[2]
    quarter = width // 4
    vectors = vectors_ref[...]
    gain_one, gain_two = row_of(vectors, GAIN_ONE), row_of(vectors, GAIN_TWO)
    mask = head_mask(width)
    own = pl.ds(core * HALF_ROWS, HALF_ROWS)
    d_memory = None
    sums = None
    queries, hiddens, key_rows, value_rows = [], [], [], []
    for segment in reversed(range(SEGS)):
        d_keys, d_values = kv_mem_ref[0, segment], kv_mem_ref[1, segment]
        if d_memory is None:
            d_next = None
        else:
            normed, unit_one, root_one = norm_fwd(
                mem_hidden_ref[segment], gain_one, row_of(vectors, SHIFT_ONE)
            )
            _, unit_two, root_two = norm_fwd(
                mem_total_ref[segment], gain_two, row_of(vectors, SHIFT_TWO)
            )
            d_total = norm_bwd(d_memory, unit_two, root_two, gain_two)
            d_total_low = d_total.astype(BF16)
            if segment == CHAINED - 1:
                wait(1)
            d_inner = (nt(d_total_low, outer_ref[...]) * mem_slope_ref[segment]).astype(BF16)
            if segment == CHAINED - 1:
                wait(1)
            d_normed = d_total + nt(d_inner, inner_ref[...])
            d_hidden = norm_bwd(d_normed, unit_one, root_one, gain_one)
            d_hidden_low = d_hidden.astype(BF16)
            if segment == CHAINED - 1:
                wait(1)
            d_context = spread_heads(nt(d_hidden_low, weights_ref[3]).astype(BF16), mask)
            query = spread_heads(mem_query_ref[segment], mask)
            probs = mem_probs_ref[segment]
            probs_low = probs.astype(BF16)
            wait(1)
            d_probs = nt(values_ref[segment], d_context)
            delta = jnp.sum(probs * d_probs, axis=0, keepdims=True)
            d_scores = (probs * (d_probs - delta)).astype(BF16)
            wait(1)
            d_query = gather_heads(tn(d_scores, keys_ref[segment]), mask) * SCALE
            d_query = d_query.astype(BF16)
            more_keys = nn(d_scores, query)
            more_values = nn(probs_low, d_context)
            grad_ref[0, :SEG_LEN] = more_keys[:SEG_LEN]
            grad_ref[1, :SEG_LEN] = more_values[:SEG_LEN]
            kv_rows_ref[0, segment] = grad_ref[0, own]
            kv_rows_ref[1, segment] = grad_ref[1, own]
            d_keys = d_keys + more_keys[SEG_LEN:]
            d_values = d_values + more_values[SEG_LEN:]
            if segment == CHAINED - 1:
                wait(1)
            d_next = d_hidden + nn(d_query, weights_ref[0])
            queries.append(d_query)
            hiddens.append(d_hidden_low)
            d_total_ref[segment] = d_total_low
            d_inner_ref[segment] = d_inner
            wide = column_sum(d_inner.astype(F32))
            rows = [
                column_sum(d_hidden),
                column_sum(d_normed * unit_one),
                column_sum(d_normed),
                column_sum(d_total),
                column_sum(d_memory * unit_two),
                column_sum(d_memory),
            ]
            rows += [wide[:, at : at + width] for at in range(0, wide.shape[1], width)]
            rows.append(column_sum(d_query.astype(F32)))
            rows = jnp.concatenate(rows, 0)
            sums = rows if sums is None else sums + rows
        d_keys, d_values = d_keys.astype(BF16), d_values.astype(BF16)
        key_rows.append(d_keys)
        value_rows.append(d_values)
        if segment == CHAINED:
            wait(2)
        d_next = 0.0 if d_next is None else d_next
        d_memory = d_next + nn(d_keys, weights_ref[1]) + nn(d_values, weights_ref[2])
    low = [low_ref[segment] for segment in reversed(range(SEGS))]
    low_all = jnp.concatenate(low, 0)
    low_chained = jnp.concatenate(low[1:], 0)
    context = jnp.concatenate([mem_context_ref[s] for s in reversed(range(CHAINED))], 0)
    pairs = (
        (jnp.concatenate(queries, 0), low_chained),
        (context, jnp.concatenate(hiddens, 0)),
        (jnp.concatenate(key_rows, 0), low_all),
        (jnp.concatenate(value_rows, 0), low_all),
    )
    start = (2 * side + core) * quarter

    def part(index):
        return lambda at, rows: grad_ref[index, pl.ds(pl.multiple_of(start + at, 8), rows)]

    value_sum = column_sum(jnp.concatenate(value_rows, 0).astype(F32))
    filler = jnp.zeros((SUM_ROWS - MEMORY_SUM - MEM, width), F32)
    sums = jnp.concatenate([sums, value_sum, d_memory[:MEM], filler], 0)
    for first, ref, extra in ((0, query_dense_ref, None), (2, dense_ref, sums)):
        for index in range(2):
            grad_ref[index, :width] = tn(*pairs[first + index])
        to_blocks(ref, [part(0), part(1)], extra)
    if not packed:
        share_refs[0][...] = d_inner_ref[...]
        share_refs[1][...] = d_total_ref[...]
        return
    at_fast, at_slow = place_ref[PART] % 2, place_ref[PART] // 2
    half = width // 2
    index = 2 * side + core
    for bits in range(4):
        ref = share_refs[bits]
        base = 2 * (at_slow ^ (bits // 2)) + (at_fast ^ (bits % 2))
        for segment in range(CHAINED):
            rows = slice(MEM_PAD * segment, MEM_PAD * (segment + 1))
            for far in range(2):
                columns = pl.ds(pl.multiple_of((4 * far + base) * half, half), half)
                for which, hidden_ref in enumerate((d_inner_ref, mem_active_ref)):
                    at = which * width + far * half
                    ref[rows, at : at + half] = hidden_ref[segment, :, columns].astype(F32)
            for which, wide_ref in enumerate((mem_normed_ref, d_total_ref)):
                wide = wide_ref[segment]
                piece = wide[:, :quarter]
                for other in range(1, 4):
                    piece = jnp.where(
                        index == other, wide[:, quarter * other : quarter * (other + 1)], piece
                    )
                at = 2 * width + which * SHARE_SPACE
                ref[rows, at : at + quarter] = piece.astype(F32)
                gap = jnp.zeros((MEM_PAD, SHARE_SPACE - quarter), F32)
                ref[rows, at + quarter : at + SHARE_SPACE] = gap


SHARE_SPACE = 256


def memory_backward(
    place, kv_mem, weights, keys, values, saved, vectors, inner_weight, outer_weight, packed
):
    width, ff = inner_weight.shape
    vmem = pl.BlockSpec(memory_space=pltpu.VMEM)
    query_rows, key_rows = block_rows(width)
    if packed:
        shares = [((CHAINED * MEM_PAD, 2 * width + 2 * SHARE_SPACE), F32)] * 4
    else:
        shares = [((CHAINED, MEM_PAD, ff), BF16), ((CHAINED, MEM_PAD, width), BF16)]
    shapes = [
        ((2, CHAINED, HALF_ROWS, width), F32),
        ((BLOCKS, query_rows, width), F32),
        ((BLOCKS, key_rows, width), F32),
    ] + shares
    return pl.pallas_call(
        partial(memory_backward_kernel, packed),
        in_specs=[pl.BlockSpec(memory_space=pltpu.SMEM)]
        + [vmem] * 11
        + [pl.BlockSpec(memory_space=pl.ANY)] * 5,
        out_specs=[vmem] * len(shapes),
        out_shape=[jax.ShapeDtypeStruct(shape, dtype) for shape, dtype in shapes],
        scratch_shapes=[
            pltpu.VMEM(weights.shape, BF16),
            pltpu.VMEM((CHAINED,) + keys.shape[1:], BF16),
            pltpu.VMEM((CHAINED,) + keys.shape[1:], BF16),
            pltpu.VMEM((width, ff), BF16),
            pltpu.VMEM((ff, width), BF16),
            pltpu.VMEM((2, width, width), F32),
            pltpu.VMEM((CHAINED, MEM_PAD, ff), BF16),
            pltpu.VMEM((CHAINED, MEM_PAD, width), BF16),
            pltpu.SemaphoreType.DMA((10,)),
        ],
        compiler_params=pltpu.CompilerParams(vmem_limit_bytes=60 << 20),
        cost_estimate=pl.CostEstimate(flops=1000, bytes_accessed=1000, transcendentals=0),
        name="memory_backward",
    )(place, kv_mem, *saved, vectors, weights, keys, values, inner_weight, outer_weight)


def grads_out(place_ref, grads_ref, own_ref, other_ref, sums=None):
    quarter = grads_ref.shape[1] // 2
    core = place_ref[CORE]
    for ref, at in ((own_ref, core), (other_ref, 1 - core)):

        def part(index, at=at):
            return lambda row, rows: grads_ref[
                index, pl.ds(pl.multiple_of(at * quarter + row, 8), rows)
            ]

        to_blocks(ref, [part(0), part(1)], sums)


def query_grads_kernel(
    place_ref,
    tokens_ref,
    d_hidden_ref,
    d_query_ref,
    context_ref,
    d_hidden_low_ref,
    weights_ref,
    sums_in_ref,
    out_ref,
    own_ref,
    other_ref,
    sums_ref,
    grads_ref,
):
    segment = pl.program_id(0)
    half = out_ref.shape[2] // 2
    d_query = d_query_ref[0]
    out_ref[0] = d_hidden_ref[0] + nn(d_query, weights_ref[0])
    first_side = place_ref[SIDE] == 0

    @pl.when(segment == 0)
    def _():
        grads_ref[...] = jnp.zeros_like(grads_ref)
        sums_ref[...] = sums_in_ref[...]

    pairs = ((d_query, tokens_ref[0]), (context_ref[0], d_hidden_low_ref[0]))
    for index, (cols, against) in enumerate(pairs):
        grads_ref[index] += tn(jnp.where(first_side, cols[:, :half], cols[:, half:]), against)
    sums_ref[QUERY_SUM : QUERY_SUM + 1] += column_sum(d_query.astype(F32))

    @pl.when(segment == pl.num_programs(0) - 1)
    def _():
        grads_out(place_ref, grads_ref, own_ref, other_ref)


def query_grads(place, tokens, d_hidden, d_query, context, d_hidden_low, weights, sums):
    width = tokens.shape[2]

    def own_half():
        return pl.BlockSpec((1, HALF_ROWS, width), lambda i, place: (i, place[CORE], 0))

    def segment():
        return pl.BlockSpec((1, HALF_ROWS, width), lambda i, place: (i, 0, 0))

    def whole(shape):
        return pl.BlockSpec(shape, lambda i, place: (0,) * len(shape))

    shapes = [(BLOCKS, block_rows(width)[0], width)] * 2 + [(SUM_ROWS, width)]
    return pl.pallas_call(
        query_grads_kernel,
        grid_spec=pltpu.PrefetchScalarGridSpec(
            num_scalar_prefetch=1,
            grid=(SEGS,),
            in_specs=[
                own_half(),
                segment(),
                segment(),
                segment(),
                segment(),
                whole((1, width, width)),
                whole((SUM_ROWS, width)),
            ],
            out_specs=[segment()] + [whole(shape) for shape in shapes],
            scratch_shapes=[pltpu.VMEM((2, width // 2, width), F32)],
        ),
        out_shape=[
            jax.ShapeDtypeStruct(shape, F32) for shape in [(SEGS, HALF_ROWS, width)] + shapes
        ],
        compiler_params=pltpu.CompilerParams(vmem_limit_bytes=60 << 20),
        cost_estimate=pl.CostEstimate(flops=1000, bytes_accessed=1000, transcendentals=0),
        name="query_grads",
    )(place, tokens, d_hidden, d_query, context, d_hidden_low, weights, sums)


def input_grads_kernel(
    place_ref,
    tokens_ref,
    d_part_ref,
    kv_own_ref,
    kv_other_ref,
    kv_more_ref,
    key_ref,
    value_ref,
    sums_in_ref,
    out_ref,
    rows_ref,
    own_ref,
    other_ref,
    grads_ref,
    sums_ref,
):
    segment = pl.program_id(0)
    width = out_ref.shape[2]
    half = width // 2
    more = jnp.where(segment < CHAINED, 1.0, 0.0)
    d_keys = (kv_own_ref[0, 0] + kv_other_ref[0, 0] + more * kv_more_ref[0, 0]).astype(BF16)
    d_values = (kv_own_ref[1, 0] + kv_other_ref[1, 0] + more * kv_more_ref[1, 0]).astype(BF16)
    d_inputs = d_part_ref[0] + nn(d_keys, key_ref[0]) + nn(d_values, value_ref[0])
    out_ref[0] = d_inputs
    rows_ref[0] = d_inputs
    first_side = place_ref[SIDE] == 0

    @pl.when(segment == 0)
    def _():
        grads_ref[...] = jnp.zeros_like(grads_ref)
        sums_ref[...] = sums_in_ref[...]

    for index, cols in enumerate((d_keys, d_values)):
        cols = jnp.where(first_side, cols[:, :half], cols[:, half:])
        grads_ref[index] += tn(cols, tokens_ref[0])
    sums_ref[VALUE_SUM : VALUE_SUM + 1] += column_sum(d_values.astype(F32))

    @pl.when(segment == pl.num_programs(0) - 1)
    def _():
        grads_out(place_ref, grads_ref, own_ref, other_ref, sums_ref[...])


def input_grads(place, tokens, d_part, kv_own, kv_other, kv_more, weights, sums):
    width = tokens.shape[2]

    def own_half():
        return pl.BlockSpec((1, HALF_ROWS, width), lambda i, place: (i, place[CORE], 0))

    def segment():
        return pl.BlockSpec((1, HALF_ROWS, width), lambda i, place: (i, 0, 0))

    def two(last):
        return pl.BlockSpec(
            (2, 1, HALF_ROWS, width), lambda i, place: (0, jnp.minimum(i, last), 0, 0)
        )

    def weight(which):
        return pl.BlockSpec((1, width, width), lambda i, place: (which, 0, 0))

    dense = jax.ShapeDtypeStruct((BLOCKS, block_rows(width)[1], width), F32)
    dense_spec = pl.BlockSpec(dense.shape, lambda i, place: (0, 0, 0))
    return pl.pallas_call(
        input_grads_kernel,
        grid_spec=pltpu.PrefetchScalarGridSpec(
            num_scalar_prefetch=1,
            grid=(SEGS,),
            in_specs=[
                own_half(),
                segment(),
                two(SEGS - 1),
                two(SEGS - 1),
                two(CHAINED - 1),
                weight(1),
                weight(2),
                pl.BlockSpec((SUM_ROWS, width), lambda i, place: (0, 0)),
            ],
            out_specs=[own_half(), segment(), dense_spec, dense_spec],
            scratch_shapes=[
                pltpu.VMEM((2, width // 2, width), F32),
                pltpu.VMEM((SUM_ROWS, width), F32),
            ],
        ),
        out_shape=[
            jax.ShapeDtypeStruct((SEGS, SEG_LEN, width), F32),
            jax.ShapeDtypeStruct((SEGS, HALF_ROWS, width), F32),
            dense,
            dense,
        ],
        compiler_params=pltpu.CompilerParams(vmem_limit_bytes=60 << 20),
        cost_estimate=pl.CostEstimate(flops=1000, bytes_accessed=1000, transcendentals=0),
        name="input_grads",
    )(place, tokens, d_part, kv_own, kv_other, kv_more, weights, weights, sums)


def memory_shares_kernel(place_ref, *refs):
    share_refs, refs = refs[:4], refs[4:]
    inner_kept, inner_moved, outer_kept, outer_moved = refs[:4]
    terms, (keep_ref, send_ref, *outs) = refs[4:-6], refs[-6:]
    mine = place_ref[CHAIN] // 4
    quarter = keep_ref.shape[1]
    half = keep_ref.shape[2]
    width = 2 * half
    share = jnp.concatenate([ref[...] for ref in share_refs], 0).astype(BF16)
    normed = share[:, 2 * width : 2 * width + quarter]
    d_total = share[:, 2 * width + SHARE_SPACE : 2 * width + SHARE_SPACE + quarter]
    sides = (
        (inner_kept, inner_moved, normed, share[:, :width]),
        (outer_kept, outer_moved, d_total, share[:, width : 2 * width]),
    )
    for which, (kept_ref, moved_ref, factor, hidden) in enumerate(sides):
        more = tn(factor, hidden)
        parts = [kept_ref[at] + moved_ref[at] + more[:, half * at : half * (at + 1)] for at in (0, 1)]
        keep_ref[which] = jnp.where(mine == 0, parts[0], parts[1])
        send_ref[which] = jnp.where(mine == 0, parts[1], parts[0])
    fast, slow = place_ref[CHAIN] % 2, (place_ref[CHAIN] // 2) % 2
    query, dense = terms[:3], terms[3:]
    for at, out_q, out_d in ((0, outs[0], outs[2]), (1, outs[1], outs[3])):
        out_q[...] = sum((ref[:, slow ^ at] for ref in query[1:]), query[0][:, slow ^ at])
        out_d[...] = sum((ref[:, :, fast ^ at] for ref in dense[1:]), dense[0][:, :, fast ^ at])


def memory_shares(place, shares, inner_kept, inner_moved, outer_kept, outer_moved, query, dense):
    vmem = pl.BlockSpec(memory_space=pltpu.VMEM)
    shape = jax.ShapeDtypeStruct((2,) + inner_kept.shape[1:], F32)
    shapes = [shape] * 2
    for value in (query[0], query[0], dense[0], dense[0]):
        shapes.append(jax.ShapeDtypeStruct((2, 2) + value.shape[3:], F32))
    return pl.pallas_call(
        memory_shares_kernel,
        in_specs=[pl.BlockSpec(memory_space=pltpu.SMEM)] + [vmem] * 14,
        out_specs=[vmem] * 6,
        out_shape=shapes,
        compiler_params=pltpu.CompilerParams(vmem_limit_bytes=60 << 20),
        name="memory_shares",
    )(place, *shares, inner_kept, inner_moved, outer_kept, outer_moved, *query, *dense)


def split_kernel(bits, counts, place_ref, *refs):
    ins, outs = refs[: sum(counts)], refs[sum(counts) :]
    for index, (bit, count) in enumerate(zip(bits, counts)):
        terms, ins = ins[:count], ins[count:]
        if bit is None:
            outs[2 * index][...] = sum((ref[...] for ref in terms[1:]), terms[0][...])
            continue
        mine = (place_ref[CHAIN] >> bit) & 1
        for out, at in ((outs[2 * index], mine), (outs[2 * index + 1], 1 - mine)):
            out[...] = sum((ref[:, at] for ref in terms[1:]), terms[0][:, at])


def split(place, *items):
    terms, bits, counts, shapes, results = [], [], [], [], []
    for bit, axis, values in items:
        shape = values[0].shape
        bits.append(bit)
        counts.append(len(values))
        if bit is None:
            terms += values
            shapes += [shape, (8, 128)]
            results += [shape, (8, 128)]
            continue
        ahead = 1
        for size in shape[:axis]:
            ahead *= size
        terms += [value.reshape((ahead, 2, -1) + shape[-2:]) for value in values]
        half = shape[:axis] + shape[axis + 1 :]
        inner = terms[-1].shape
        shapes += [inner[:1] + inner[2:]] * 2
        results += [half] * 2
    vmem = pl.BlockSpec(memory_space=pltpu.VMEM)
    outs = pl.pallas_call(
        partial(split_kernel, tuple(bits), tuple(counts)),
        in_specs=[pl.BlockSpec(memory_space=pltpu.SMEM)] + [vmem] * len(terms),
        out_specs=[vmem] * len(shapes),
        out_shape=[jax.ShapeDtypeStruct(shape, F32) for shape in shapes],
        compiler_params=pltpu.CompilerParams(vmem_limit_bytes=32 << 20),
        name="split",
    )(place, *terms)
    return [out.reshape(shape) for out, shape in zip(outs, results)]


def join_kernel(bits, place_ref, *refs):
    ins, outs = refs[: 2 * len(bits)], refs[2 * len(bits) :]
    for index, bit in enumerate(bits):
        mine = (place_ref[CHAIN] >> bit) & 1
        outs[index][:, mine] = ins[2 * index][...]
        outs[index][:, 1 - mine] = ins[2 * index + 1][...]


def join(place, *items):
    terms, bits, shapes, results = [], [], [], []
    for bit, axis, own, other in items:
        shape = own.shape
        ahead = 1
        for size in shape[:axis]:
            ahead *= size
        terms += [value.reshape((ahead, -1) + shape[-2:]) for value in (own, other)]
        bits.append(bit)
        inner = terms[-1].shape
        shapes.append(inner[:1] + (2,) + inner[1:])
        results.append(shape[:axis] + (2,) + shape[axis:])
    vmem = pl.BlockSpec(memory_space=pltpu.VMEM)
    outs = pl.pallas_call(
        partial(join_kernel, tuple(bits)),
        in_specs=[pl.BlockSpec(memory_space=pltpu.SMEM)] + [vmem] * len(terms),
        out_specs=[vmem] * len(shapes),
        out_shape=[jax.ShapeDtypeStruct(shape, F32) for shape in shapes],
        compiler_params=pltpu.CompilerParams(vmem_limit_bytes=32 << 20),
        name="join",
    )(place, *terms)
    return [out.reshape(shape) for out, shape in zip(outs, results)]


def final_kernel(place_ref, *refs):
    query_own, query_other, dense_own, dense_other = refs[:4]
    pieces, refs = refs[4:8], refs[8:]
    grad_query, grad_out, grad_key, grad_value, sums_ref, inner_ref, outer_ref, wide_ref = refs
    chain, side, core = place_ref[CHAIN], place_ref[SIDE], place_ref[CORE]
    fast, slow = chain % 2, (chain // 2) % 2

    def put(ref, block, value):
        rows = value.shape[0]
        ref[pl.ds(pl.multiple_of(block * rows, 8), rows)] = value

    rows = query_own.shape[2] // 2
    for far in range(2):
        for near in range(2):
            for source, at in ((query_own, slow), (query_other, 1 - slow)):
                block = 4 * far + 2 * at + near
                put(grad_query, block, source[far, near, :rows])
                put(grad_out, block, source[far, near, rows:])
            for source, at in ((dense_own, fast), (dense_other, 1 - fast)):
                block = 4 * far + 2 * near + at
                put(grad_key, block, source[far, near, :rows])
                put(grad_value, block, source[far, near, rows : 2 * rows])
                put(sums_ref, block, source[far, near, 2 * rows :])
    places = (
        2 * side + core,
        2 * side + 1 - core,
        2 * (1 - side) + core,
        2 * (1 - side) + 1 - core,
    )
    for ref, at in zip(pieces, places):
        put(inner_ref, at, ref[0])
        put(wide_ref, at, ref[1])
    outer_ref[...] = wide_ref[...].T


def final(place, halves, pieces):
    quarter, piece = pieces[0].shape[1:]
    width = 4 * quarter
    vmem = pl.BlockSpec(memory_space=pltpu.VMEM)
    shapes = [(quarter, width)] * 4 + [(BLOCKS * SUM_SPACE, width), (width, piece), (piece, width)]
    return pl.pallas_call(
        final_kernel,
        in_specs=[pl.BlockSpec(memory_space=pltpu.SMEM)] + [vmem] * 8,
        out_specs=[vmem] * len(shapes),
        out_shape=[jax.ShapeDtypeStruct(shape, F32) for shape in shapes],
        scratch_shapes=[pltpu.VMEM((width, piece), F32)],
        compiler_params=pltpu.CompilerParams(vmem_limit_bytes=40 << 20),
        name="final",
    )(place, *halves, *pieces)


def swap_core(value):
    return lax.ppermute(value, "head", [(0, 1), (1, 0), (2, 3), (3, 2)])


def swap_side(value):
    return lax.ppermute(value, "head", [(0, 2), (2, 0), (1, 3), (3, 1)])


def swap_dp(value, bits):
    size = lax.axis_size("dp")
    return lax.ppermute(value, "dp", [(i, i ^ bits) for i in range(size)])


def fetch_far(value):
    part = lax.axis_index("dp") % 4
    mine = swap_side(lax.dynamic_index_in_dim(value, part, 0, False))
    return [mine] + [swap_dp(mine, bits) for bits in (1, 2, 3)]


def on_device(
    tokens,
    cotangent,
    memory,
    query_weight,
    query_bias,
    key_weight,
    value_weight,
    value_bias,
    out_weight,
    out_bias,
    gain_one,
    shift_one,
    inner_weight,
    inner_bias,
    outer_weight,
    outer_bias,
    gain_two,
    shift_two,
    group_sizes,
    group_section,
    last_valid,
):
    width = memory.shape[1]
    ff = inner_weight.shape[1]
    dp_size = lax.axis_size("dp")
    chain_index = lax.axis_index("dp")
    head_index = lax.axis_index("head")
    side = head_index // 2
    core = head_index % 2
    quarter = query_weight.shape[1]
    device = chain_index * 4 + head_index
    divisors, sizes = jnp.array([2, 1, 4, 4], jnp.int32), jnp.array([2, 2, 4, dp_size], jnp.int32)
    place = (device // divisors) % sizes
    scalars = (place, group_sizes, group_section, last_valid)

    own_weights = (query_weight.T, key_weight.T, value_weight.T, out_weight)
    wide_weights = jnp.stack([weight.astype(F32) for weight in own_weights])
    far = fetch_far(wide_weights)
    partner = swap_core(wide_weights)
    far_partner = [swap_core(part) for part in far]
    spread = [
        lax.dynamic_update_slice(jnp.zeros((width,), F32), bias, (head_index * quarter,))
        for bias in (query_bias, value_bias)
    ]
    parts = [out_bias, gain_one, shift_one, outer_bias, gain_two, shift_two] + spread
    filler = jnp.zeros((VECTOR_ROWS * width - len(parts) * width - ff,), F32)
    vectors = jnp.concatenate(parts + [inner_bias, filler]).reshape(VECTOR_ROWS, width)
    row = jnp.arange(VECTOR_ROWS)[:, None]
    split_rows = (row == QUERY_BIAS) | (row == VALUE_BIAS)
    for swap in (swap_core, swap_side):
        vectors = vectors + jnp.where(split_rows, swap(vectors), 0.0)
    token_rows = tokens.reshape(SEGS, SEG_LEN, width)

    weights, keys, values, own_query, *saved = memory_forward(
        scalars,
        token_rows,
        memory,
        own_weights,
        partner,
        far,
        far_partner,
        vectors,
        inner_weight,
        outer_weight,
    )
    context, probs = attend(scalars, own_query, keys, values)
    (
        layer_out,
        out_rows,
        d_hidden,
        d_hidden_low,
        d_context,
        sums,
        own_inner,
        own_outer,
        other_inner,
        other_outer,
    ) = feed(
        scalars,
        token_rows,
        context,
        cotangent.reshape(SEGS, SEG_LEN, width),
        weights,
        inner_weight,
        outer_weight,
        vectors,
    )

    piece = ff // dp_size
    back = partial(attend_back, place, own_query, keys, values, d_context, probs)
    held = back(CHAINED, SEGS - CHAINED)
    fast_path = dp_size == BLOCKS
    run = on_block if fast_path else on_any
    halves = run(
        place,
        scalars,
        back,
        held,
        (own_inner, own_outer, other_inner, other_outer),
        partial(query_grads, place, token_rows, d_hidden),
        (context, d_hidden_low, weights, sums),
        partial(
            memory_backward,
            place,
            weights=weights,
            keys=keys,
            values=values,
            saved=saved,
            vectors=vectors,
            inner_weight=inner_weight,
            outer_weight=outer_weight,
            packed=fast_path,
        ),
        partial(input_grads, place, token_rows, weights=weights),
        saved,
        out_rows,
    )
    grad_query, grad_out, grad_key, grad_value, sums, grad_inner, grad_outer, grad_tokens, others = halves
    sums = sums.reshape(BLOCKS, SUM_SPACE, width)[:, :SUM_PART].reshape(SUM_ROWS, width)

    inner_bias_grad = lax.dynamic_slice_in_dim(
        sums[6:QUERY_SUM].reshape(-1), chain_index * piece, piece, 0
    )
    grad_qb = lax.dynamic_slice_in_dim(sums[QUERY_SUM], head_index * quarter, quarter, 0)
    grad_vb = lax.dynamic_slice_in_dim(sums[VALUE_SUM], head_index * quarter, quarter, 0)
    grad_memory = sums[MEMORY_SUM : MEMORY_SUM + MEM]

    def both_cores(value, other):
        start = (1 - core) * HALF_ROWS
        value = lax.dynamic_update_slice_in_dim(value, other, start, 1)
        return value.reshape(SEGS * SEG_LEN, width)

    return (
        both_cores(layer_out, others[0]),
        both_cores(grad_tokens, others[1]),
        grad_memory,
        grad_query.T,
        grad_qb,
        grad_key.T,
        grad_value.T,
        grad_vb,
        grad_out,
        sums[0],
        sums[1],
        sums[2],
        grad_inner,
        inner_bias_grad,
        grad_outer,
        sums[3],
        sums[4],
        sums[5],
    )


def at_bits(value, bits):
    axis = 0
    for bit in bits:
        if bit is None:
            axis += 1
        else:
            value = lax.dynamic_index_in_dim(value, bit, axis, False)
    return value


def on_block(
    place, scalars, back, held, ffn, query_part, query_args, backward, input_part, saved, out_rows
):
    index = lax.axis_index("dp")
    fast, slow = index & 1, (index >> 1) & 1
    own_inner, own_outer, other_inner, other_outer = ffn
    ffn = in_step(own_inner, own_outer, swap_core(other_inner), swap_core(other_outer), *held)
    ffn, held = ffn[:4], ffn[4:]
    own_inner, own_outer, other_inner, other_outer = (
        value.reshape((2, 2, 2) + value.shape[1:]) for value in ffn
    )
    inner, outer = (own_inner, other_inner), (own_outer, other_outer)

    def total(terms, bits):
        terms = [at_bits(term, bits) for term in terms]
        return sum(terms[1:], terms[0])

    inner_moved = swap_dp(total(inner, (None, 1 - slow, None)), 2)
    outer_moved = swap_dp(total(outer, (None, None, 1 - fast)), 1)
    d_query, kv_own, kv_other, kv_mem = back(0, CHAINED, held)
    d_part, query_own, query_other, sums = query_part(d_query, *query_args)
    weights = query_args[2]
    values = in_step(
        inner_moved, outer_moved, d_part, query_own, query_other, sums, kv_own, kv_other, kv_mem
    )
    inner_moved, outer_moved, d_part, query_own, query_other, sums, kv_own, kv_other, kv_mem = values

    def second(terms, moved, bits, axis, bit):
        def half(at):
            here = [at if place == axis else value for place, value in enumerate(bits)]
            rest = [None if value is None or place != axis else at for place, value in enumerate(here)]
            del rest[[i for i, value in enumerate(bits) if value is not None][0]]
            return total(terms, here) + at_bits(moved, rest)

        return half(bit), half(1 - bit)

    inner_kept, inner_sent = second(inner, inner_moved, (None, slow, None), 2, fast)
    outer_kept, outer_sent = second(outer, outer_moved, (None, None, fast), 1, slow)
    inner_moved, outer_moved = swap_dp(inner_sent, 1), swap_dp(outer_sent, 2)
    kv_mem = kv_mem + swap_core(kv_mem)
    kv_other = swap_core(kv_other)
    query_other = swap_core(query_other)
    kv_more, query_mem, dense_mem, *shares = backward(kv_mem)
    values = in_step(
        inner_kept,
        inner_moved,
        outer_kept,
        outer_moved,
        kv_other,
        query_other,
        kv_more,
        query_mem,
        dense_mem,
        *shares,
    )
    inner_kept, inner_moved, outer_kept, outer_moved, kv_other, query_other, kv_more = values[:7]
    query_mem, dense_mem, *shares = values[7:]

    shares = shares[:1] + [swap_dp(share, bits) for bits, share in enumerate(shares) if bits]
    grad_tokens, token_rows, dense_own, dense_other = input_part(
        d_part, kv_own, kv_other, kv_more, sums=sums
    )
    *shares, dense_own, dense_other = in_step(*shares, dense_own, dense_other)

    def cube(*arrays):
        return [value.reshape((2, 2, 2) + value.shape[1:]) for value in arrays]

    ffn_kept, ffn_sent, q_kept, q_sent, d_kept, d_sent = memory_shares(
        place,
        shares,
        inner_kept,
        inner_moved,
        outer_kept,
        outer_moved,
        cube(query_own, query_other, query_mem),
        cube(dense_own, swap_core(dense_other), dense_mem),
    )
    ffn_moved = swap_dp(ffn_sent, 4)
    q_moved, d_moved = swap_dp(q_sent, 2), swap_dp(d_sent, 1)
    q_kept, q_sent, d_kept, d_sent = split(
        place, (0, 1, [q_kept, q_moved]), (1, 1, [d_kept, d_moved])
    )
    q_moved, d_moved = swap_dp(q_sent, 1), swap_dp(d_sent, 2)
    q_kept, q_sent, d_kept, d_sent, ffn_mine, _ = split(
        place, (2, 0, [q_kept, q_moved]), (2, 0, [d_kept, d_moved]), (None, 0, [ffn_kept, ffn_moved])
    )
    q_moved, d_moved = swap_dp(q_sent, 4), swap_dp(d_sent, 4)
    ffn_far = swap_side(ffn_mine)
    q_mine, _, d_mine, _ = split(place, (None, 0, [q_kept, q_moved]), (None, 0, [d_kept, d_moved]))
    q_mine, d_mine = join(
        place, (2, 0, q_mine, swap_dp(q_mine, 4)), (2, 0, d_mine, swap_dp(d_mine, 4))
    )
    q_mine, d_mine = join(
        place, (0, 1, q_mine, swap_dp(q_mine, 1)), (1, 1, d_mine, swap_dp(d_mine, 2))
    )
    halves = (q_mine, swap_dp(q_mine, 2), d_mine, swap_dp(d_mine, 1))
    pieces = (ffn_mine, swap_core(ffn_mine), ffn_far, swap_core(ffn_far))
    grads = final(place, halves, pieces)
    return *grads, grad_tokens, (swap_core(out_rows), swap_core(token_rows))


def on_any(
    place, scalars, back, held, ffn, query_part, query_args, backward, input_part, saved, out_rows
):
    own_inner, own_outer, other_inner, other_outer = ffn
    dp_size = lax.axis_size("dp")
    quarter = own_inner.shape[1]
    width = 4 * quarter
    head_index = lax.axis_index("head")
    d_query, kv_own, kv_other, kv_mem = back(0, CHAINED, held)
    d_part, query_own, query_other, sums = query_part(d_query, *query_args)
    kv_mem = kv_mem + swap_core(kv_mem)
    kv_more, query_mem, dense_mem, mem_d_inner, mem_d_total = backward(kv_mem)
    grad_tokens, token_rows, dense_own, dense_other = input_part(
        d_part, kv_own, swap_core(kv_other), kv_more, sums=sums
    )
    query = query_own + swap_core(query_other) + query_mem
    dense = dense_own + swap_core(dense_other) + dense_mem
    query, dense = lax.psum((query, dense), "dp")
    mem_active, mem_normed = saved[7], saved[8]

    def whole(own, other, rows, hidden):
        rows = lax.dynamic_slice_in_dim(rows, head_index * quarter, quarter, 2)
        rows = rows.reshape(-1, quarter)
        value = own + swap_core(other)
        value = value.transpose(1, 0, 2).reshape(quarter, -1)
        value = value + tn(rows, hidden.reshape(rows.shape[0], -1))
        value = lax.psum_scatter(value, "dp", scatter_dimension=1, tiled=True)
        return lax.all_gather(value, "head").reshape(width, -1)

    grad_inner = whole(own_inner, other_inner, mem_normed, mem_d_inner)
    grad_outer = whole(own_outer, other_outer, mem_d_total, mem_active).T
    rows = quarter // BLOCKS

    def part(value, index):
        return value[:, rows * index : rows * (index + 1)].reshape(quarter, width)

    sums = dense[:, 2 * rows :].reshape(-1, width)
    grads = (part(query, 0), part(query, 1), part(dense, 0), part(dense, 1), sums)
    others = (swap_core(out_rows), swap_core(token_rows))
    return *grads, grad_inner, grad_outer, grad_tokens, others


def solution(mesh):
    row, col, vec, every = P("dp", None), P(None, "head"), P("head"), P()
    placed = (row, row, every, col, vec, col, col, vec, P("head", None)) + (every,) * 11
    return jax.shard_map(
        on_device,
        mesh=mesh,
        in_specs=placed + (P("dp"),),
        out_specs=(
            row,
            row,
            every,
            col,
            vec,
            col,
            col,
            vec,
            P("head", None),
            every,
            every,
            every,
            P(None, "dp"),
            P("dp"),
            row,
            every,
            every,
            every,
        ),
        check_vma=False,
    )
```

```python
from functools import partial

import jax
import jax.numpy as jnp
from jax import lax
from jax.experimental import pallas as pl
from jax.experimental.pallas import tpu as pltpu
from jax.sharding import PartitionSpec as P

HEAD_DIM = 64
MEM = 10
MEM_PAD = 16
SEG_LEN = 512
SEGS = 3
CHAINED = SEGS - 1
KEYS = SEG_LEN + MEM_PAD
HALF_ROWS = SEG_LEN // 2
EPS = 1e-06
SCALE = HEAD_DIM ** (-0.5)
MASKED = -1000000000.0
LN_TWO = 0.6931471805599453

F32 = jnp.float32
BF16 = jnp.bfloat16


def nn(left, right):
    return jnp.dot(left, right, preferred_element_type=F32)


def nt(left, right):
    return lax.dot_general(left, right, (((1,), (1,)), ((), ())), preferred_element_type=F32)


def tn(left, right):
    return lax.dot_general(left, right, (((0,), (0,)), ((), ())), preferred_element_type=F32)


def norm_fwd(value, gain, shift):
    centered = value - jnp.mean(value, axis=-1, keepdims=True)
    spread = jnp.mean(centered * centered, axis=-1, keepdims=True)
    root = lax.rsqrt(spread + EPS)
    unit = centered * root
    return unit * gain + shift, unit, root


def norm_bwd(d_out, unit, root, gain):
    d_unit = d_out * gain
    mean_one = jnp.mean(d_unit, axis=-1, keepdims=True)
    mean_two = jnp.mean(d_unit * unit, axis=-1, keepdims=True)
    return root * (d_unit - mean_one - unit * mean_two)


def gelu_parts(inner):
    cdf = 0.5 * (1.0 + lax.erf(inner * 0.7071067811865476))
    pdf = jnp.exp(-0.5 * inner * inner) * 0.3989422804014327
    return inner * cdf, cdf + inner * pdf


def column_sum(value):
    return jnp.sum(value, axis=0, keepdims=True)


SHARE_SPACE = 256

SIDE, CORE, PART, CHAIN = range(4)


def limit_of(segment, place_ref, sizes_ref, sections_ref, last_ref):
    chain = place_ref[CHAIN]
    end, section = 0, 0
    for group in range(sizes_ref.shape[0]):
        start, end = end, end + sizes_ref[group]
        inside = jnp.logical_and(start <= chain, chain < end)
        section = jnp.where(inside, sections_ref[group], section)
    last = section % (SEGS - 1) + 1
    return jnp.where(segment < last, SEG_LEN, jnp.where(segment == last, last_ref[0], 0))


def key_bias(limit):
    row = lax.broadcasted_iota(jnp.int32, (KEYS, 1), 0)
    beyond = jnp.where((row >= SEG_LEN) & (row < SEG_LEN + MEM), LN_TWO, MASKED)
    return jnp.where(row < limit, 0.0, beyond)


OUT_BIAS, GAIN_ONE, SHIFT_ONE, OUTER_BIAS, GAIN_TWO, SHIFT_TWO, QUERY_BIAS, VALUE_BIAS = range(8)
INNER_BIAS = 8
VECTOR_ROWS = 16


def row_of(vectors, index):
    return vectors[index : index + 1]


def head_mask(width):
    count = width // HEAD_DIM
    shape = (count, MEM_PAD, width)
    head = lax.broadcasted_iota(jnp.int32, shape, 0)
    lane = lax.broadcasted_iota(jnp.int32, shape, 2) // HEAD_DIM
    return (head == lane).astype(F32)


def spread_heads(value, mask):
    count, rows, width = mask.shape
    return (value.astype(F32)[None] * mask).reshape(count * rows, width).astype(BF16)


def gather_heads(value, mask):
    return jnp.sum(value.reshape(mask.shape) * mask, axis=0)


def pack_vectors_kernel(place_ref, *refs):
    *vector_refs, query_ref, value_ref, inner_ref, out_ref = refs
    width = out_ref.shape[1]
    quarter = query_ref.shape[0]
    out_ref[...] = jnp.zeros_like(out_ref)
    for index, ref in enumerate(vector_refs):
        out_ref[index : index + 1] = ref[...].reshape(1, width)
    index = 2 * place_ref[SIDE] + place_ref[CORE]
    for row, ref in ((QUERY_BIAS, query_ref), (VALUE_BIAS, value_ref)):
        piece = ref[...].reshape(1, quarter)
        for at in range(4):
            columns = slice(quarter * at, quarter * (at + 1))
            out_ref[row : row + 1, columns] = jnp.where(index == at, piece, 0.0)
    for at in range(inner_ref.shape[0] // width):
        piece = inner_ref[width * at : width * (at + 1)].reshape(1, width)
        out_ref[INNER_BIAS + at : INNER_BIAS + at + 1] = piece


def pack_vectors(place, vectors, query_bias, value_bias, inner_bias):
    width = vectors[0].shape[0]
    vmem = pl.BlockSpec(memory_space=pltpu.VMEM)
    return pl.pallas_call(
        pack_vectors_kernel,
        in_specs=[pl.BlockSpec(memory_space=pltpu.SMEM)] + [vmem] * (len(vectors) + 3),
        out_specs=vmem,
        out_shape=jax.ShapeDtypeStruct((VECTOR_ROWS, width), F32),
        name="pack_vectors",
    )(place, *vectors, query_bias, value_bias, inner_bias)


def share_out(place_ref, refs, hidden_ref, wide_ref):
    at_fast, at_slow = place_ref[PART] % 2, place_ref[PART] // 2
    index = 2 * place_ref[SIDE] + place_ref[CORE]
    width = wide_ref.shape[2]
    half, quarter = width // 2, width // 4
    for bits, ref in enumerate(refs):
        base = 2 * (at_slow ^ (bits // 2)) + (at_fast ^ (bits % 2))
        for segment in range(CHAINED):
            rows = slice(MEM_PAD * segment, MEM_PAD * (segment + 1))
            for far in range(2):
                columns = pl.ds(pl.multiple_of((4 * far + base) * half, half), half)
                ref[rows, far * half : (far + 1) * half] = hidden_ref[segment, :, columns].astype(F32)
            wide = wide_ref[segment]
            piece = wide[:, :quarter]
            for other in range(1, 4):
                piece = jnp.where(
                    index == other, wide[:, quarter * other : quarter * (other + 1)], piece
                )
            ref[rows, width : width + quarter] = piece.astype(F32)
            gap = jnp.zeros((MEM_PAD, SHARE_SPACE - quarter), F32)
            ref[rows, width + quarter :] = gap


def memory_forward_kernel(
    places,
    place_ref,
    sizes_ref,
    sections_ref,
    last_ref,
    tokens_ref,
    memory_ref,
    own_q_ref,
    own_k_ref,
    own_v_ref,
    own_o_ref,
    partner_ref,
    vectors_ref,
    *refs,
):
    far_refs, far_partner_refs, refs = (
        refs[: len(places)],
        refs[len(places) : 2 * len(places)],
        refs[2 * len(places) :],
    )
    inner_hbm, outer_hbm, weights_hbm, keys_hbm, values_hbm, query_hbm, *refs = refs
    saved_hbm, (weights_ref, keys_ref, values_ref, query_ref) = refs[:13], refs[13:17]
    saved, (inner_ref, outer_ref, sems) = refs[17:30], refs[30:]
    (
        low_ref,
        mem_query_ref,
        mem_context_ref,
        mem_probs_ref,
        mem_hidden_ref,
        mem_total_ref,
        mem_slope_ref,
        mem_active_ref,
        mem_normed_ref,
        *share_refs,
    ) = saved
    copies = [
        pltpu.make_async_copy(inner_hbm, inner_ref, sems.at[0]),
        pltpu.make_async_copy(outer_hbm, outer_ref, sems.at[1]),
    ]
    for copy in copies:
        copy.start()
    side, core, part = place_ref[SIDE], place_ref[CORE], place_ref[PART]
    quarter = own_q_ref.shape[0]
    width = memory_ref.shape[1]

    def span_of(at_side, at_core, start=0, rows=quarter):
        start = (2 * at_side + at_core) * quarter + start
        return pl.ds(pl.multiple_of(start, 16), rows)

    for which, ref in enumerate((own_q_ref, own_k_ref, own_v_ref, own_o_ref)):
        weights_ref[which, span_of(side, core)] = ref[...]
        weights_ref[which, span_of(side, 1 - core)] = partner_ref[which].astype(BF16)
    for (bits, start), near_ref, other_ref in zip(places, far_refs, far_partner_refs):
        which, rows = part ^ bits, near_ref.shape[0]
        weights_ref[which, span_of(1 - side, core, start, rows)] = near_ref[...].astype(BF16)
        weights_ref[which, span_of(1 - side, 1 - core, start, rows)] = other_ref[...].astype(BF16)
    writes = [pltpu.make_async_copy(weights_ref, weights_hbm, sems.at[2])]
    writes[0].start()
    vectors = vectors_ref[...]
    query_bias = row_of(vectors, QUERY_BIAS)
    value_bias = row_of(vectors, VALUE_BIAS)

    def project(index, carry):
        segment, half = index // 2, index % 2
        span = pl.ds(half * HALF_ROWS, HALF_ROWS)
        rows = tokens_ref[segment, span]
        keys_ref[segment, span] = nt(rows, weights_ref[1]).astype(BF16)
        values_ref[segment, span] = (nt(rows, weights_ref[2]) + value_bias).astype(BF16)

        @pl.when(half == core)
        def _():
            query_ref[segment] = (nt(rows, weights_ref[0]) + query_bias).astype(BF16) * SCALE

        return carry

    lax.fori_loop(0, 2 * SEGS, project, 0)
    token_rows, mem_rows = pl.ds(0, SEG_LEN), pl.ds(SEG_LEN, MEM_PAD)
    pairs = ((keys_ref, keys_hbm), (values_ref, values_hbm))
    writes.append(pltpu.make_async_copy(query_ref, query_hbm, sems.at[3]))
    for index, (ref, hbm) in enumerate(pairs):
        writes.append(
            pltpu.make_async_copy(ref.at[:, token_rows], hbm.at[:, token_rows], sems.at[4 + index])
        )
    for write in writes[1:]:
        write.start()

    mask = head_mask(width)
    now = jnp.concatenate(
        [memory_ref[...].astype(F32), jnp.zeros((MEM_PAD - MEM, width), F32)], 0
    )
    for segment in range(SEGS):
        low = now.astype(BF16)
        low_ref[segment] = low
        keys_ref[segment, SEG_LEN:] = nt(low, weights_ref[1]).astype(BF16)
        values_ref[segment, SEG_LEN:] = (nt(low, weights_ref[2]) + value_bias).astype(BF16)
        if segment == CHAINED:
            break
        query = (nt(low, weights_ref[0]) + query_bias).astype(BF16) * SCALE
        mem_query_ref[segment] = query
        scores = nt(keys_ref[segment], spread_heads(query, mask))
        limit = limit_of(segment, place_ref, sizes_ref, sections_ref, last_ref)
        scores = scores + key_bias(limit)
        weights = jnp.exp(scores - jnp.max(scores, axis=0, keepdims=True))
        probs = weights * (1.0 / jnp.sum(weights, axis=0, keepdims=True))
        mem_probs_ref[segment] = probs
        context = gather_heads(tn(probs.astype(BF16), values_ref[segment]), mask).astype(BF16)
        mem_context_ref[segment] = context
        hidden = now + nn(context, weights_ref[3]) + row_of(vectors, OUT_BIAS)
        mem_hidden_ref[segment] = hidden
        normed, _, _ = norm_fwd(hidden, row_of(vectors, GAIN_ONE), row_of(vectors, SHIFT_ONE))
        mem_normed_ref[segment] = normed.astype(BF16)
        if segment == 0:
            copies[0].wait()
        inner_bias = [row_of(vectors, INNER_BIAS + i) for i in range(inner_ref.shape[1] // width)]
        inner_bias = jnp.concatenate(inner_bias, 1)
        active, slope = gelu_parts(nn(normed.astype(BF16), inner_ref[...]) + inner_bias)
        active = active.astype(BF16)
        mem_slope_ref[segment] = slope
        mem_active_ref[segment] = active
        if segment == 0:
            copies[1].wait()
        total = normed + nn(active, outer_ref[...]) + row_of(vectors, OUTER_BIAS)
        mem_total_ref[segment] = total
        now, _, _ = norm_fwd(total, row_of(vectors, GAIN_TWO), row_of(vectors, SHIFT_TWO))
    for index, (ref, hbm) in enumerate(pairs):
        writes.append(
            pltpu.make_async_copy(ref.at[:, mem_rows], hbm.at[:, mem_rows], sems.at[6 + index])
        )
        writes[-1].start()
    share_out(place_ref, share_refs, mem_active_ref, mem_normed_ref)
    for index, (ref, hbm) in enumerate(zip(saved, saved_hbm)):
        writes.append(pltpu.make_async_copy(ref, hbm, sems.at[8 + index]))
        writes[-1].start()
    for write in writes:
        write.wait()


def memory_forward(
    places, scalars, tokens, memory, own, partner, far, far_partner, vectors, inner_weight, outer_weight
):
    width = memory.shape[1]
    ff = inner_weight.shape[1]
    head_rows = MEM_PAD * width // HEAD_DIM
    vmem = pl.BlockSpec(memory_space=pltpu.VMEM)

    def like(shape, dtype):
        return jax.ShapeDtypeStruct(shape, dtype)

    saved = [
        ((SEGS, MEM_PAD, width), BF16),
        ((CHAINED, MEM_PAD, width), BF16),
        ((CHAINED, MEM_PAD, width), BF16),
        ((CHAINED, KEYS, head_rows), F32),
        ((CHAINED, MEM_PAD, width), F32),
        ((CHAINED, MEM_PAD, width), F32),
        ((CHAINED, MEM_PAD, ff), F32),
        ((CHAINED, MEM_PAD, ff), BF16),
        ((CHAINED, MEM_PAD, width), BF16),
    ] + [((CHAINED * MEM_PAD, width + SHARE_SPACE), F32)] * 4
    large = [
        ((4, width, width), BF16),
        ((SEGS, KEYS, width), BF16),
        ((SEGS, KEYS, width), BF16),
        ((SEGS, HALF_ROWS, width), BF16),
    ]
    return pl.pallas_call(
        partial(memory_forward_kernel, places),
        in_specs=[pl.BlockSpec(memory_space=pltpu.SMEM)] * 4
        + [vmem] * (8 + 2 * len(places))
        + [pl.BlockSpec(memory_space=pl.ANY)] * 2,
        out_specs=[pl.BlockSpec(memory_space=pltpu.HBM)] * 17,
        out_shape=[pltpu.HBM(*shape) for shape in large + saved],
        scratch_shapes=[pltpu.VMEM(*shape) for shape in large + saved]
        + [
            pltpu.VMEM((width, ff), BF16),
            pltpu.VMEM((ff, width), BF16),
            pltpu.SemaphoreType.DMA((21,)),
        ],
        compiler_params=pltpu.CompilerParams(vmem_limit_bytes=46 << 20),
        cost_estimate=pl.CostEstimate(flops=1000, bytes_accessed=1000, transcendentals=0),
        name="memory_forward",
    )(
        *scalars,
        tokens,
        memory,
        *own,
        partner,
        vectors,
        *far,
        *far_partner,
        inner_weight,
        outer_weight,
    )


def lane_masks(rows):
    lane = lax.broadcasted_iota(jnp.int32, (rows, 2 * HEAD_DIM), 1)
    first = (lane < HEAD_DIM).astype(F32)
    return first.astype(BF16), (1.0 - first).astype(BF16)


def pair_of(head):
    start = 2 * HEAD_DIM * (head // 2)
    return slice(start, start + 2 * HEAD_DIM)


def attend_kernel(
    place_ref, sizes_ref, sections_ref, last_ref, q_ref, k_ref, v_ref, out_ref, probs_ref
):
    limit = limit_of(pl.program_id(0), place_ref, sizes_ref, sections_ref, last_ref)
    bias = key_bias(limit)
    count = q_ref.shape[2] // HEAD_DIM
    q_masks, k_masks = lane_masks(q_ref.shape[1]), lane_masks(KEYS)

    def score(head):
        cols = pair_of(head)
        return nt(k_ref[0, :, cols], q_ref[0, :, cols] * q_masks[head % 2])

    def finish(head, probs, held):
        cols = pair_of(head)
        part = tn(probs, v_ref[0, :, cols] * k_masks[head % 2])
        if head % 2 == 0:
            return part
        out_ref[0, :, cols] = (held + part).astype(BF16)
        return None

    held = before = None
    later = score(0)
    for head in range(count):
        scores = later + bias
        if head + 1 < count:
            later = score(head + 1)
        if before is not None:
            held = finish(head - 1, before, held)
        weights = jnp.exp(scores - jnp.max(scores, axis=0, keepdims=True))
        before = (weights * (1.0 / jnp.sum(weights, axis=0, keepdims=True))).astype(BF16)
        probs_ref[0, head] = before
    finish(count - 1, before, held)


def attend(scalars, query, keys, values):
    segs, rows, width = query.shape
    wide = width // 2

    def block(length):
        return pl.BlockSpec((1, length, wide), lambda s, h, *_: (s, 0, h))

    return pl.pallas_call(
        attend_kernel,
        grid_spec=pltpu.PrefetchScalarGridSpec(
            num_scalar_prefetch=4,
            grid=(segs, 2),
            in_specs=[block(rows), block(KEYS), block(KEYS)],
            out_specs=[
                block(rows),
                pl.BlockSpec((1, wide // HEAD_DIM, KEYS, rows), lambda s, h, *_: (s, h, 0, 0)),
            ],
        ),
        out_shape=[
            jax.ShapeDtypeStruct(query.shape, BF16),
            jax.ShapeDtypeStruct((segs, width // HEAD_DIM, KEYS, rows), BF16),
        ],
        compiler_params=pltpu.CompilerParams(vmem_limit_bytes=56 << 20),
        cost_estimate=pl.CostEstimate(flops=1000, bytes_accessed=1000, transcendentals=0),
        name="attend",
    )(*scalars, query, keys, values)


def in_step_kernel(*refs):
    pass


def in_step(*values):
    anywhere = [pl.BlockSpec(memory_space=pl.ANY)] * len(values)
    return pl.pallas_call(
        in_step_kernel,
        in_specs=anywhere,
        out_specs=anywhere,
        out_shape=[jax.ShapeDtypeStruct(value.shape, value.dtype) for value in values],
        input_output_aliases={i: i for i in range(len(values))},
        name="in_step",
    )(*values)


def attend_back_kernel(through, place_ref, q_ref, k_ref, v_ref, d_ref, p_ref, *refs):
    dq_ref, own_ref, other_ref, mem_ref = refs[through:][:4]
    first_core = place_ref[CORE] == 0
    count = q_ref.shape[2] // HEAD_DIM
    q_masks, k_masks = lane_masks(q_ref.shape[1]), lane_masks(KEYS)

    def first(head):
        cols = pair_of(head)
        return nt(v_ref[0, :, cols], d_ref[0, :, cols] * q_masks[head % 2])

    def last(head, d_scores, held):
        cols, mask = pair_of(head), q_masks[head % 2]
        dv = nn(p_ref[0, head], d_ref[0, :, cols] * mask)
        dk = nn(d_scores, q_ref[0, :, cols] * mask)
        dq = tn(d_scores, k_ref[0, :, cols] * k_masks[head % 2])
        if head % 2 == 0:
            return dv, dk, dq
        for index, value in enumerate((held[1] + dk, held[0] + dv)):
            low, high = value[:HALF_ROWS], value[HALF_ROWS:SEG_LEN]
            own_ref[index, 0, :, cols] = jnp.where(first_core, low, high)
            other_ref[index, 0, :, cols] = jnp.where(first_core, high, low)
            mem_ref[index, 0, :, cols] = value[SEG_LEN:]
        dq_ref[0, :, cols] = ((held[2] + dq) * SCALE).astype(BF16)
        return None

    held = before = None
    later = first(0)
    for head in range(count):
        d_probs = later
        if head + 1 < count:
            later = first(head + 1)
        if before is not None:
            held = last(head - 1, before, held)
        probs = p_ref[0, head].astype(F32)
        delta = jnp.sum(probs * d_probs, axis=0, keepdims=True)
        before = (probs * (d_probs - delta)).astype(BF16)
    last(count - 1, before, held)


def attend_back(place, query, keys, values, d_context, probs, first, count, held=(), through=()):
    segs, rows, width = query.shape
    wide = width // 2

    def block(length):
        return pl.BlockSpec((1, length, wide), lambda s, h, place: (first + s, 0, h))

    def two(length):
        return pl.BlockSpec((2, 1, length, wide), lambda s, h, place: (0, first + s, 0, h))

    inputs = (query, keys, values, d_context, probs)
    at = 1 + len(inputs)
    aliases = {at + i: i for i in range(len(held))}
    aliases.update({at + len(held) + i: 4 + i for i in range(len(through))})
    return pl.pallas_call(
        partial(attend_back_kernel, len(held) + len(through)),
        grid_spec=pltpu.PrefetchScalarGridSpec(
            num_scalar_prefetch=1,
            grid=(count, 2),
            in_specs=[
                block(rows),
                block(KEYS),
                block(KEYS),
                block(rows),
                pl.BlockSpec(
                    (1, wide // HEAD_DIM, KEYS, rows),
                    lambda s, h, place: (first + s, h, 0, 0),
                ),
            ]
            + [pl.BlockSpec(memory_space=pl.ANY)] * (len(held) + len(through)),
            out_specs=[block(rows), two(HALF_ROWS), two(HALF_ROWS), two(MEM_PAD)]
            + [pl.BlockSpec(memory_space=pl.ANY)] * len(through),
        ),
        out_shape=[
            jax.ShapeDtypeStruct(query.shape, BF16),
            jax.ShapeDtypeStruct((2, segs, HALF_ROWS, width), F32),
            jax.ShapeDtypeStruct((2, segs, HALF_ROWS, width), F32),
            jax.ShapeDtypeStruct((2, segs, MEM_PAD, width), F32),
        ]
        + [jax.ShapeDtypeStruct(value.shape, value.dtype) for value in through],
        input_output_aliases=aliases,
        compiler_params=pltpu.CompilerParams(vmem_limit_bytes=60 << 20),
        cost_estimate=pl.CostEstimate(flops=1000, bytes_accessed=1000, transcendentals=0),
        name="attend_back",
    )(place, *inputs, *held, *through)


SUM_ROWS = 24
QUERY_SUM = 10
VALUE_SUM = 11
MEMORY_SUM = 12


def feed_kernel(
    place_ref,
    sizes_ref,
    sections_ref,
    last_ref,
    rows_ref,
    context_ref,
    cot_ref,
    out_weight_ref,
    inner_ref,
    outer_ref,
    vectors_ref,
    out_ref,
    out_rows_ref,
    d_hidden_ref,
    d_hidden_low_ref,
    d_context_ref,
    sums_ref,
    own_inner_hbm,
    own_outer_hbm,
    other_inner_hbm,
    other_outer_hbm,
    slope_ref,
    active_ref,
    grads_ref,
    sems,
):
    segment = pl.program_id(0)
    side, core = place_ref[SIDE], place_ref[CORE]
    vectors = vectors_ref[...]
    gain_one, gain_two = row_of(vectors, GAIN_ONE), row_of(vectors, GAIN_TWO)
    width = vectors.shape[1]
    half = width // 2
    quarter = width // 4
    chunks = [slice(at, at + width) for at in range(0, inner_ref.shape[1], width)]
    row = lax.broadcasted_iota(jnp.int32, (HALF_ROWS, 1), 0) + core * HALF_ROWS
    valid = row < limit_of(segment, place_ref, sizes_ref, sections_ref, last_ref)

    def of_side(value):
        return jnp.where(side == 0, value[:, :half], value[:, half:])

    def add_grads(which, index, value):
        for row_half in range(2):
            rows = value[quarter * row_half : quarter * (row_half + 1)]
            for part in range(2):
                at = 2 * index + part
                held = jnp.where(segment == 0, 0.0, grads_ref[which, row_half, at])
                grads_ref[which, row_half, at] = held + rows[:, half * part : half * (part + 1)]

    hidden = (
        rows_ref[0].astype(F32)
        + nn(context_ref[0], out_weight_ref[0])
        + row_of(vectors, OUT_BIAS)
    )
    normed, unit_one, root_one = norm_fwd(hidden, gain_one, row_of(vectors, SHIFT_ONE))
    normed_low = normed.astype(BF16)
    total = normed + row_of(vectors, OUTER_BIAS)
    for index, chunk in enumerate(chunks):
        inner = nn(normed_low, inner_ref[:, chunk]) + row_of(vectors, INNER_BIAS + index)
        active, slope = gelu_parts(inner)
        active = active.astype(BF16)
        active_ref[:, chunk] = active
        slope_ref[:, chunk] = slope
        total = total + nn(active, outer_ref[chunk])
    result, unit_two, root_two = norm_fwd(total, gain_two, row_of(vectors, SHIFT_TWO))
    result = jnp.where(valid, result, 0.0)
    out_ref[0] = result
    out_rows_ref[0] = result

    d_result = jnp.where(valid, cot_ref[0].astype(F32), 0.0)
    d_total = norm_bwd(d_result, unit_two, root_two, gain_two)
    d_total_low = d_total.astype(BF16)
    normed_half, d_total_half = of_side(normed_low), of_side(d_total_low)
    d_normed = d_total
    inner_sums = []
    for index, chunk in enumerate(chunks):
        d_inner = (nt(d_total_low, outer_ref[chunk]) * slope_ref[:, chunk]).astype(BF16)
        inner_sums.append(column_sum(d_inner.astype(F32)))
        d_normed = d_normed + nt(d_inner, inner_ref[:, chunk])
        add_grads(0, index, tn(normed_half, d_inner))
        add_grads(1, index, tn(d_total_half, active_ref[:, chunk]))
    final = segment == pl.num_programs(0) - 1
    targets = ((other_inner_hbm, own_inner_hbm), (other_outer_hbm, own_outer_hbm))
    copies = [
        pltpu.make_async_copy(
            grads_ref.at[which, core if own else 1 - core],
            targets[which][own],
            sems.at[which, own],
        )
        for own in range(2)
        for which in range(2)
    ]

    @pl.when(final)
    def _():
        for copy in copies:
            copy.start()

    d_hidden = norm_bwd(d_normed, unit_one, root_one, gain_one)
    d_hidden_ref[0] = d_hidden
    d_hidden_low = d_hidden.astype(BF16)
    d_hidden_low_ref[0] = d_hidden_low
    d_context_ref[0] = nt(d_hidden_low, out_weight_ref[0]).astype(BF16)
    sums = [
        column_sum(d_hidden),
        column_sum(d_normed * unit_one),
        column_sum(d_normed),
        column_sum(d_total),
        column_sum(d_result * unit_two),
        column_sum(d_result),
    ] + inner_sums
    sums = jnp.concatenate(sums + [jnp.zeros((SUM_ROWS - len(sums), width), F32)], 0)

    @pl.when(segment == 0)
    def _():
        sums_ref[...] = sums

    @pl.when(segment > 0)
    def _():
        sums_ref[...] += sums

    @pl.when(final)
    def _():
        for copy in copies:
            copy.wait()


def feed(scalars, tokens, context, cot, weights, inner_weight, outer_weight, vectors):
    width, ff = inner_weight.shape
    chunk = width // 2

    def own_half():
        return pl.BlockSpec((1, HALF_ROWS, width), lambda i, place, *_: (i, place[CORE], 0))

    def segment():
        return pl.BlockSpec((1, HALF_ROWS, width), lambda i, *_: (i, 0, 0))

    def fixed(shape, index=(0, 0)):
        return pl.BlockSpec(shape, lambda i, *_: index, pipeline_mode=pl.Buffered(1))

    like = pltpu.HBM
    per_segment = (SEGS, HALF_ROWS, width)
    grads_shape = (ff // chunk, width // 4, chunk)
    return pl.pallas_call(
        feed_kernel,
        grid_spec=pltpu.PrefetchScalarGridSpec(
            num_scalar_prefetch=4,
            grid=(SEGS,),
            in_specs=[
                own_half(),
                segment(),
                own_half(),
                fixed((1, width, width), (3, 0, 0)),
                fixed((width, ff)),
                fixed((ff, width)),
                fixed(vectors.shape),
            ],
            out_specs=[
                own_half(),
                segment(),
                segment(),
                segment(),
                segment(),
                pl.BlockSpec((SUM_ROWS, width), lambda i, *_: (0, 0)),
            ]
            + [pl.BlockSpec(memory_space=pl.ANY)] * 4,
            scratch_shapes=[
                pltpu.VMEM((HALF_ROWS, ff), F32),
                pltpu.VMEM((HALF_ROWS, ff), BF16),
                pltpu.VMEM((2, 2) + grads_shape, F32),
                pltpu.SemaphoreType.DMA((2, 2)),
            ],
        ),
        out_shape=[
            like((SEGS, SEG_LEN, width), F32),
            like(per_segment, F32),
            like(per_segment, F32),
            like(per_segment, BF16),
            like(per_segment, BF16),
            like((SUM_ROWS, width), F32),
        ]
        + [like(grads_shape, F32)] * 4,
        compiler_params=pltpu.CompilerParams(vmem_limit_bytes=60 << 20),
        cost_estimate=pl.CostEstimate(flops=1000, bytes_accessed=1000, transcendentals=0),
        name="feed",
    )(*scalars, tokens, context, cot, weights, inner_weight, outer_weight, vectors)


BLOCKS = 8
SUM_PART = SUM_ROWS // BLOCKS
SUM_SPACE = 8


def block_rows(width):
    rows = width // 4 // BLOCKS
    return 2 * rows, 2 * rows + SUM_SPACE


def to_blocks(ref, matrices, sums=None):
    rows = (ref.shape[1] - (0 if sums is None else SUM_SPACE)) // 2
    for block in range(BLOCKS):
        for index, matrix in enumerate(matrices):
            ref[block, rows * index : rows * (index + 1)] = matrix(rows * block, rows)
        if sums is not None:
            part = sums[SUM_PART * block : SUM_PART * (block + 1)]
            filler = jnp.zeros((SUM_SPACE - SUM_PART, part.shape[1]), F32)
            ref[block, 2 * rows :] = jnp.concatenate([part, filler], 0)


def memory_backward_kernel(
    packed,
    place_ref,
    kv_mem_ref,
    kv_mem_other_ref,
    low_ref,
    mem_query_ref,
    mem_context_ref,
    mem_probs_ref,
    mem_hidden_ref,
    mem_total_ref,
    mem_slope_ref,
    mem_active_ref,
    mem_normed_ref,
    vectors_ref,
    weights_hbm,
    keys_hbm,
    values_hbm,
    inner_hbm,
    outer_hbm,
    kv_rows_ref,
    query_dense_ref,
    dense_ref,
    *refs,
):
    share_refs, refs = refs[:-9], refs[-9:]
    weights_ref, keys_ref, values_ref, inner_ref, outer_ref, grad_ref, d_inner_ref, d_total_ref, sems = refs
    order = [(weights_hbm.at[at], weights_ref.at[at]) for at in (1, 2)]
    order += [(outer_hbm, outer_ref), (inner_hbm, inner_ref)]
    order += [(weights_hbm.at[3], weights_ref.at[3])]
    for segment in reversed(range(CHAINED)):
        order += [(values_hbm.at[segment], values_ref.at[segment])]
        order += [(keys_hbm.at[segment], keys_ref.at[segment])]
        if segment == CHAINED - 1:
            order += [(weights_hbm.at[0], weights_ref.at[0])]
    copies = [
        pltpu.make_async_copy(source, target, sems.at[index])
        for index, (source, target) in enumerate(order)
    ]
    for copy in copies:
        copy.start()
    arrived = iter(copies)

    def wait(count):
        for _ in range(count):
            next(arrived).wait()

    side, core = place_ref[0], place_ref[1]
    width = low_ref.shape[2]
    quarter = width // 4
    vectors = vectors_ref[...]
    gain_one, gain_two = row_of(vectors, GAIN_ONE), row_of(vectors, GAIN_TWO)
    mask = head_mask(width)
    own = pl.ds(core * HALF_ROWS, HALF_ROWS)
    d_memory = None
    sums = None
    queries, hiddens, key_rows, value_rows = [], [], [], []
    for segment in reversed(range(SEGS)):
        d_keys = kv_mem_ref[0, segment] + kv_mem_other_ref[0, segment]
        d_values = kv_mem_ref[1, segment] + kv_mem_other_ref[1, segment]
        if d_memory is None:
            d_next = None
        else:
            normed, unit_one, root_one = norm_fwd(
                mem_hidden_ref[segment], gain_one, row_of(vectors, SHIFT_ONE)
            )
            _, unit_two, root_two = norm_fwd(
                mem_total_ref[segment], gain_two, row_of(vectors, SHIFT_TWO)
            )
            d_total = norm_bwd(d_memory, unit_two, root_two, gain_two)
            d_total_low = d_total.astype(BF16)
            if segment == CHAINED - 1:
                wait(1)
            d_inner = (nt(d_total_low, outer_ref[...]) * mem_slope_ref[segment]).astype(BF16)
            if segment == CHAINED - 1:
                wait(1)
            d_normed = d_total + nt(d_inner, inner_ref[...])
            d_hidden = norm_bwd(d_normed, unit_one, root_one, gain_one)
            d_hidden_low = d_hidden.astype(BF16)
            if segment == CHAINED - 1:
                wait(1)
            d_context = spread_heads(nt(d_hidden_low, weights_ref[3]).astype(BF16), mask)
            query = spread_heads(mem_query_ref[segment], mask)
            probs = mem_probs_ref[segment]
            probs_low = probs.astype(BF16)
            wait(1)
            d_probs = nt(values_ref[segment], d_context)
            delta = jnp.sum(probs * d_probs, axis=0, keepdims=True)
            d_scores = (probs * (d_probs - delta)).astype(BF16)
            wait(1)
            d_query = gather_heads(tn(d_scores, keys_ref[segment]), mask) * SCALE
            d_query = d_query.astype(BF16)
            more_keys = nn(d_scores, query)
            more_values = nn(probs_low, d_context)
            grad_ref[0, :SEG_LEN] = more_keys[:SEG_LEN]
            grad_ref[1, :SEG_LEN] = more_values[:SEG_LEN]
            kv_rows_ref[0, segment] = grad_ref[0, own]
            kv_rows_ref[1, segment] = grad_ref[1, own]
            d_keys = d_keys + more_keys[SEG_LEN:]
            d_values = d_values + more_values[SEG_LEN:]
            if segment == CHAINED - 1:
                wait(1)
            d_next = d_hidden + nn(d_query, weights_ref[0])
            queries.append(d_query)
            hiddens.append(d_hidden_low)
            d_total_ref[segment] = d_total_low
            d_inner_ref[segment] = d_inner
            wide = column_sum(d_inner.astype(F32))
            rows = [
                column_sum(d_hidden),
                column_sum(d_normed * unit_one),
                column_sum(d_normed),
                column_sum(d_total),
                column_sum(d_memory * unit_two),
                column_sum(d_memory),
            ]
            rows += [wide[:, at : at + width] for at in range(0, wide.shape[1], width)]
            rows.append(column_sum(d_query.astype(F32)))
            rows = jnp.concatenate(rows, 0)
            sums = rows if sums is None else sums + rows
        d_keys, d_values = d_keys.astype(BF16), d_values.astype(BF16)
        key_rows.append(d_keys)
        value_rows.append(d_values)
        if segment == CHAINED:
            wait(2)
        d_next = 0.0 if d_next is None else d_next
        d_memory = d_next + nn(d_keys, weights_ref[1]) + nn(d_values, weights_ref[2])
    low = [low_ref[segment] for segment in reversed(range(SEGS))]
    low_all = jnp.concatenate(low, 0)
    low_chained = jnp.concatenate(low[1:], 0)
    context = jnp.concatenate([mem_context_ref[s] for s in reversed(range(CHAINED))], 0)
    pairs = (
        (jnp.concatenate(queries, 0), low_chained),
        (context, jnp.concatenate(hiddens, 0)),
        (jnp.concatenate(key_rows, 0), low_all),
        (jnp.concatenate(value_rows, 0), low_all),
    )
    start = (2 * side + core) * quarter

    def part(index):
        return lambda at, rows: grad_ref[index, pl.ds(pl.multiple_of(start + at, 8), rows)]

    value_sum = column_sum(jnp.concatenate(value_rows, 0).astype(F32))
    filler = jnp.zeros((SUM_ROWS - MEMORY_SUM - MEM, width), F32)
    sums = jnp.concatenate([sums, value_sum, d_memory[:MEM], filler], 0)
    for first, ref, extra in ((0, query_dense_ref, None), (2, dense_ref, sums)):
        for index in range(2):
            grad_ref[index, :width] = tn(*pairs[first + index])
        to_blocks(ref, [part(0), part(1)], extra)
    if not packed:
        share_refs[0][...] = d_inner_ref[...]
        share_refs[1][...] = d_total_ref[...]
        return
    share_out(place_ref, share_refs, d_inner_ref, d_total_ref)


def memory_backward(
    place, kv_mem, weights, keys, values, saved, vectors, inner_weight, outer_weight, packed
):
    width, ff = inner_weight.shape
    vmem = pl.BlockSpec(memory_space=pltpu.VMEM)
    query_rows, key_rows = block_rows(width)
    if packed:
        shares = [((CHAINED * MEM_PAD, width + SHARE_SPACE), F32)] * 4
    else:
        shares = [((CHAINED, MEM_PAD, ff), BF16), ((CHAINED, MEM_PAD, width), BF16)]
    shapes = [
        ((2, CHAINED, HALF_ROWS, width), F32),
        ((BLOCKS, query_rows, width), F32),
        ((BLOCKS, key_rows, width), F32),
    ] + shares
    return pl.pallas_call(
        partial(memory_backward_kernel, packed),
        in_specs=[pl.BlockSpec(memory_space=pltpu.SMEM)]
        + [vmem] * 12
        + [pl.BlockSpec(memory_space=pl.ANY)] * 5,
        out_specs=[vmem] * len(shapes),
        out_shape=[jax.ShapeDtypeStruct(shape, dtype) for shape, dtype in shapes],
        scratch_shapes=[
            pltpu.VMEM(weights.shape, BF16),
            pltpu.VMEM((CHAINED,) + keys.shape[1:], BF16),
            pltpu.VMEM((CHAINED,) + keys.shape[1:], BF16),
            pltpu.VMEM((width, ff), BF16),
            pltpu.VMEM((ff, width), BF16),
            pltpu.VMEM((2, width, width), F32),
            pltpu.VMEM((CHAINED, MEM_PAD, ff), BF16),
            pltpu.VMEM((CHAINED, MEM_PAD, width), BF16),
            pltpu.SemaphoreType.DMA((10,)),
        ],
        compiler_params=pltpu.CompilerParams(vmem_limit_bytes=60 << 20),
        cost_estimate=pl.CostEstimate(flops=1000, bytes_accessed=1000, transcendentals=0),
        name="memory_backward",
    )(place, *kv_mem, *saved, vectors, weights, keys, values, inner_weight, outer_weight)


def grads_out(place_ref, grads_ref, own_ref, other_ref, sums=None):
    quarter = grads_ref.shape[1] // 2
    core = place_ref[CORE]
    for ref, at in ((own_ref, core), (other_ref, 1 - core)):

        def part(index, at=at):
            return lambda row, rows: grads_ref[
                index, pl.ds(pl.multiple_of(at * quarter + row, 8), rows)
            ]

        to_blocks(ref, [part(0), part(1)], sums)


def query_grads_kernel(
    place_ref,
    tokens_ref,
    d_hidden_ref,
    d_query_ref,
    context_ref,
    d_hidden_low_ref,
    weights_ref,
    sums_in_ref,
    out_ref,
    own_ref,
    other_ref,
    sums_ref,
    grads_ref,
):
    segment = pl.program_id(0)
    half = out_ref.shape[2] // 2
    d_query = d_query_ref[0]
    out_ref[0] = d_hidden_ref[0] + nn(d_query, weights_ref[0])
    first_side = place_ref[SIDE] == 0

    @pl.when(segment == 0)
    def _():
        grads_ref[...] = jnp.zeros_like(grads_ref)
        sums_ref[...] = sums_in_ref[...]

    pairs = ((d_query, tokens_ref[0]), (context_ref[0], d_hidden_low_ref[0]))
    for index, (cols, against) in enumerate(pairs):
        grads_ref[index] += tn(jnp.where(first_side, cols[:, :half], cols[:, half:]), against)
    sums_ref[QUERY_SUM : QUERY_SUM + 1] += column_sum(d_query.astype(F32))

    @pl.when(segment == pl.num_programs(0) - 1)
    def _():
        grads_out(place_ref, grads_ref, own_ref, other_ref)


def query_grads(place, tokens, d_hidden, d_query, context, d_hidden_low, weights, sums):
    width = tokens.shape[2]

    def own_half():
        return pl.BlockSpec((1, HALF_ROWS, width), lambda i, place: (i, place[CORE], 0))

    def segment():
        return pl.BlockSpec((1, HALF_ROWS, width), lambda i, place: (i, 0, 0))

    def whole(shape):
        return pl.BlockSpec(shape, lambda i, place: (0,) * len(shape))

    shapes = [(BLOCKS, block_rows(width)[0], width)] * 2 + [(SUM_ROWS, width)]
    return pl.pallas_call(
        query_grads_kernel,
        grid_spec=pltpu.PrefetchScalarGridSpec(
            num_scalar_prefetch=1,
            grid=(SEGS,),
            in_specs=[
                own_half(),
                segment(),
                segment(),
                segment(),
                segment(),
                whole((1, width, width)),
                whole((SUM_ROWS, width)),
            ],
            out_specs=[segment()] + [whole(shape) for shape in shapes],
            scratch_shapes=[pltpu.VMEM((2, width // 2, width), F32)],
        ),
        out_shape=[
            jax.ShapeDtypeStruct(shape, F32) for shape in [(SEGS, HALF_ROWS, width)] + shapes
        ],
        compiler_params=pltpu.CompilerParams(vmem_limit_bytes=60 << 20),
        cost_estimate=pl.CostEstimate(flops=1000, bytes_accessed=1000, transcendentals=0),
        name="query_grads",
    )(place, tokens, d_hidden, d_query, context, d_hidden_low, weights, sums)


def input_grads_kernel(
    place_ref,
    tokens_ref,
    d_part_ref,
    kv_own_ref,
    kv_other_ref,
    kv_more_ref,
    key_ref,
    value_ref,
    sums_in_ref,
    out_ref,
    rows_ref,
    own_ref,
    other_ref,
    grads_ref,
    sums_ref,
):
    segment = pl.program_id(0)
    width = out_ref.shape[2]
    half = width // 2
    more = jnp.where(segment < CHAINED, 1.0, 0.0)
    d_keys = (kv_own_ref[0, 0] + kv_other_ref[0, 0] + more * kv_more_ref[0, 0]).astype(BF16)
    d_values = (kv_own_ref[1, 0] + kv_other_ref[1, 0] + more * kv_more_ref[1, 0]).astype(BF16)
    d_inputs = d_part_ref[0] + nn(d_keys, key_ref[0]) + nn(d_values, value_ref[0])
    out_ref[0] = d_inputs
    rows_ref[0] = d_inputs
    first_side = place_ref[SIDE] == 0

    @pl.when(segment == 0)
    def _():
        grads_ref[...] = jnp.zeros_like(grads_ref)
        sums_ref[...] = sums_in_ref[...]

    for index, cols in enumerate((d_keys, d_values)):
        cols = jnp.where(first_side, cols[:, :half], cols[:, half:])
        grads_ref[index] += tn(cols, tokens_ref[0])
    sums_ref[VALUE_SUM : VALUE_SUM + 1] += column_sum(d_values.astype(F32))

    @pl.when(segment == pl.num_programs(0) - 1)
    def _():
        grads_out(place_ref, grads_ref, own_ref, other_ref, sums_ref[...])


def input_grads(place, tokens, d_part, kv_own, kv_other, kv_more, weights, sums):
    width = tokens.shape[2]

    def own_half():
        return pl.BlockSpec((1, HALF_ROWS, width), lambda i, place: (i, place[CORE], 0))

    def segment():
        return pl.BlockSpec((1, HALF_ROWS, width), lambda i, place: (i, 0, 0))

    def two(last):
        return pl.BlockSpec(
            (2, 1, HALF_ROWS, width), lambda i, place: (0, jnp.minimum(i, last), 0, 0)
        )

    def weight(which):
        return pl.BlockSpec((1, width, width), lambda i, place: (which, 0, 0))

    dense = jax.ShapeDtypeStruct((BLOCKS, block_rows(width)[1], width), F32)
    dense_spec = pl.BlockSpec(dense.shape, lambda i, place: (0, 0, 0))
    return pl.pallas_call(
        input_grads_kernel,
        grid_spec=pltpu.PrefetchScalarGridSpec(
            num_scalar_prefetch=1,
            grid=(SEGS,),
            in_specs=[
                own_half(),
                segment(),
                two(SEGS - 1),
                two(SEGS - 1),
                two(CHAINED - 1),
                weight(1),
                weight(2),
                pl.BlockSpec((SUM_ROWS, width), lambda i, place: (0, 0)),
            ],
            out_specs=[own_half(), segment(), dense_spec, dense_spec],
            scratch_shapes=[
                pltpu.VMEM((2, width // 2, width), F32),
                pltpu.VMEM((SUM_ROWS, width), F32),
            ],
        ),
        out_shape=[
            jax.ShapeDtypeStruct((SEGS, SEG_LEN, width), F32),
            jax.ShapeDtypeStruct((SEGS, HALF_ROWS, width), F32),
            dense,
            dense,
        ],
        compiler_params=pltpu.CompilerParams(vmem_limit_bytes=60 << 20),
        cost_estimate=pl.CostEstimate(flops=1000, bytes_accessed=1000, transcendentals=0),
        name="input_grads",
    )(place, tokens, d_part, kv_own, kv_other, kv_more, weights, weights, sums)


def memory_shares_kernel(place_ref, *refs):
    early_refs, late_refs, refs = refs[:4], refs[4:8], refs[8:]
    inner_kept, inner_moved, outer_kept, outer_moved, keep_ref, send_ref = refs
    mine = place_ref[CHAIN] // 4
    quarter = keep_ref.shape[1]
    half = keep_ref.shape[2]
    width = 2 * half
    early, late = (
        jnp.concatenate([ref[...] for ref in share], 0).astype(BF16)
        for share in (early_refs, late_refs)
    )
    active, normed = early[:, :width], early[:, width : width + quarter]
    d_inner, d_total = late[:, :width], late[:, width : width + quarter]
    sides = (
        (inner_kept, inner_moved, normed, d_inner),
        (outer_kept, outer_moved, d_total, active),
    )
    for which, (kept_ref, moved_ref, factor, hidden) in enumerate(sides):
        more = tn(factor, hidden)
        parts = [kept_ref[at] + moved_ref[at] + more[:, half * at : half * (at + 1)] for at in (0, 1)]
        keep_ref[which] = jnp.where(mine == 0, parts[0], parts[1])
        send_ref[which] = jnp.where(mine == 0, parts[1], parts[0])


def memory_shares(place, early, late, inner_kept, inner_moved, outer_kept, outer_moved):
    vmem = pl.BlockSpec(memory_space=pltpu.VMEM)
    shape = jax.ShapeDtypeStruct((2,) + inner_kept.shape[1:], F32)
    return pl.pallas_call(
        memory_shares_kernel,
        in_specs=[pl.BlockSpec(memory_space=pltpu.SMEM)] + [vmem] * 12,
        out_specs=[vmem] * 2,
        out_shape=[shape, shape],
        compiler_params=pltpu.CompilerParams(vmem_limit_bytes=60 << 20),
        name="memory_shares",
    )(place, *early, *late, inner_kept, inner_moved, outer_kept, outer_moved)


def split_kernel(bits, counts, place_ref, *refs):
    ins, outs = refs[: sum(counts)], refs[sum(counts) :]
    for index, (bit, count) in enumerate(zip(bits, counts)):
        terms, ins = ins[:count], ins[count:]
        if bit is None:
            outs[2 * index][...] = sum((ref[...] for ref in terms[1:]), terms[0][...])
            continue
        mine = (place_ref[CHAIN] >> bit) & 1
        for out, at in ((outs[2 * index], mine), (outs[2 * index + 1], 1 - mine)):
            out[...] = sum((ref[:, at] for ref in terms[1:]), terms[0][:, at])


def split(place, *items, limit=32):
    terms, bits, counts, shapes, results = [], [], [], [], []
    for bit, axis, values in items:
        shape = values[0].shape
        bits.append(bit)
        counts.append(len(values))
        if bit is None:
            terms += values
            shapes += [shape, (8, 128)]
            results += [shape, (8, 128)]
            continue
        ahead = 1
        for size in shape[:axis]:
            ahead *= size
        terms += [value.reshape((ahead, 2, -1) + shape[-2:]) for value in values]
        half = shape[:axis] + shape[axis + 1 :]
        inner = terms[-1].shape
        shapes += [inner[:1] + inner[2:]] * 2
        results += [half] * 2
    vmem = pl.BlockSpec(memory_space=pltpu.VMEM)
    outs = pl.pallas_call(
        partial(split_kernel, tuple(bits), tuple(counts)),
        in_specs=[pl.BlockSpec(memory_space=pltpu.SMEM)] + [vmem] * len(terms),
        out_specs=[vmem] * len(shapes),
        out_shape=[jax.ShapeDtypeStruct(shape, F32) for shape in shapes],
        compiler_params=pltpu.CompilerParams(vmem_limit_bytes=limit << 20),
        name="split",
    )(place, *terms)
    return [out.reshape(shape) for out, shape in zip(outs, results)]


def join_kernel(bits, place_ref, *refs):
    ins, outs = refs[: 2 * len(bits)], refs[2 * len(bits) :]
    for index, bit in enumerate(bits):
        mine = (place_ref[CHAIN] >> bit) & 1
        outs[index][:, mine] = ins[2 * index][...]
        outs[index][:, 1 - mine] = ins[2 * index + 1][...]


def join(place, *items):
    terms, bits, shapes, results = [], [], [], []
    for bit, axis, own, other in items:
        shape = own.shape
        ahead = 1
        for size in shape[:axis]:
            ahead *= size
        terms += [value.reshape((ahead, -1) + shape[-2:]) for value in (own, other)]
        bits.append(bit)
        inner = terms[-1].shape
        shapes.append(inner[:1] + (2,) + inner[1:])
        results.append(shape[:axis] + (2,) + shape[axis:])
    vmem = pl.BlockSpec(memory_space=pltpu.VMEM)
    outs = pl.pallas_call(
        partial(join_kernel, tuple(bits)),
        in_specs=[pl.BlockSpec(memory_space=pltpu.SMEM)] + [vmem] * len(terms),
        out_specs=[vmem] * len(shapes),
        out_shape=[jax.ShapeDtypeStruct(shape, F32) for shape in shapes],
        compiler_params=pltpu.CompilerParams(vmem_limit_bytes=32 << 20),
        name="join",
    )(place, *terms)
    return [out.reshape(shape) for out, shape in zip(outs, results)]


def feed_final_kernel(place_ref, *refs):
    pieces, (inner_ref, outer_ref, wide_ref) = refs[:4], refs[4:]
    side, core = place_ref[SIDE], place_ref[CORE]
    quarter = pieces[0].shape[1]
    places = (
        2 * side + core,
        2 * side + 1 - core,
        2 * (1 - side) + core,
        2 * (1 - side) + 1 - core,
    )
    for ref, at in zip(pieces, places):
        rows = pl.ds(pl.multiple_of(at * quarter, 8), quarter)
        inner_ref[rows] = ref[0]
        wide_ref[rows] = ref[1]
    outer_ref[...] = wide_ref[...].T


def feed_final(place, pieces):
    quarter, piece = pieces[0].shape[1:]
    vmem = pl.BlockSpec(memory_space=pltpu.VMEM)
    shapes = [(4 * quarter, piece), (piece, 4 * quarter)]
    return pl.pallas_call(
        feed_final_kernel,
        in_specs=[pl.BlockSpec(memory_space=pltpu.SMEM)] + [vmem] * 4,
        out_specs=[vmem] * 2,
        out_shape=[jax.ShapeDtypeStruct(shape, F32) for shape in shapes],
        scratch_shapes=[pltpu.VMEM((4 * quarter, piece), F32)],
        compiler_params=pltpu.CompilerParams(vmem_limit_bytes=32 << 20),
        name="feed_final",
    )(place, *pieces)


def final_kernel(place_ref, query_own, query_other, dense_own, dense_other, *refs):
    grad_query, grad_out, grad_key, grad_value, memory_ref, *refs = refs
    *vector_refs, query_bias_ref, value_bias_ref, inner_bias_ref, sums_ref = refs
    chain = place_ref[CHAIN]
    fast, slow = chain % 2, (chain // 2) % 2

    def put(ref, block, value):
        rows = value.shape[0]
        ref[pl.ds(pl.multiple_of(block * rows, 8), rows)] = value

    rows = query_own.shape[2] // 2
    for far in range(2):
        for near in range(2):
            for source, at in ((query_own, slow), (query_other, 1 - slow)):
                block = 4 * far + 2 * at + near
                put(grad_query, block, source[far, near, :rows])
                put(grad_out, block, source[far, near, rows:])
            for source, at in ((dense_own, fast), (dense_other, 1 - fast)):
                block = 4 * far + 2 * near + at
                put(grad_key, block, source[far, near, :rows])
                put(grad_value, block, source[far, near, rows : 2 * rows])
                put(sums_ref, block, source[far, near, 2 * rows :])
    width = sums_ref.shape[1]
    quarter, piece = query_bias_ref.shape[0], inner_bias_ref.shape[0]

    def row(index):
        at = SUM_SPACE * (index // SUM_PART) + index % SUM_PART
        return sums_ref[at : at + 1]

    for index, ref in enumerate(vector_refs):
        ref[...] = row(index).reshape(width)
    own = 2 * place_ref[SIDE] + place_ref[CORE]
    for ref, index in ((query_bias_ref, QUERY_SUM), (value_bias_ref, VALUE_SUM)):
        whole = row(index)
        value = whole[:, :quarter]
        for other in range(1, 4):
            value = jnp.where(own == other, whole[:, quarter * other : quarter * (other + 1)], value)
        ref[...] = value.reshape(quarter)
    count = width // piece
    value = jnp.zeros((1, piece), F32)
    for index in range(QUERY_SUM - len(vector_refs)):
        whole = row(len(vector_refs) + index)
        for part in range(count):
            here = chain == count * index + part
            value = jnp.where(here, whole[:, piece * part : piece * (part + 1)], value)
    inner_bias_ref[...] = value.reshape(piece)
    for index in range(MEM):
        memory_ref[index : index + 1] = row(MEMORY_SUM + index)


def final(place, halves, piece):
    width = halves[0].shape[3]
    quarter = width // 4
    vmem = pl.BlockSpec(memory_space=pltpu.VMEM)
    shapes = [(quarter, width)] * 4 + [(MEM, width)] + [(width,)] * 6
    shapes += [(quarter,), (quarter,), (piece,)]
    return pl.pallas_call(
        final_kernel,
        in_specs=[pl.BlockSpec(memory_space=pltpu.SMEM)] + [vmem] * 4,
        out_specs=[vmem] * len(shapes),
        out_shape=[jax.ShapeDtypeStruct(shape, F32) for shape in shapes],
        scratch_shapes=[pltpu.VMEM((BLOCKS * SUM_SPACE, width), F32)],
        compiler_params=pltpu.CompilerParams(vmem_limit_bytes=32 << 20),
        name="final",
    )(place, *halves)


def swap_core(value):
    return lax.ppermute(value, "head", [(0, 1), (1, 0), (2, 3), (3, 2)])


def swap_side(value):
    return lax.ppermute(value, "head", [(0, 2), (2, 0), (1, 3), (3, 1)])


def swap_dp(value, bits):
    size = lax.axis_size("dp")
    return lax.ppermute(value, "dp", [(i, i ^ bits) for i in range(size)])


def fetch_far(value):
    part = lax.axis_index("dp") % 4
    mine = lax.dynamic_index_in_dim(value, part, 0, False)
    rows = mine.shape[0]
    half, quarter = rows // 2, rows // 4
    pieces = []
    for start in (0, half):
        own = swap_side(mine[start : start + half])
        fast, slow = swap_dp(own, 1), swap_dp(own, 2)
        pieces += [(0, start, own), (1, start, fast), (2, start, slow)]
        pieces.append((3, start, swap_dp(slow[:quarter], 1)))
        pieces.append((3, start + quarter, swap_dp(fast[quarter:], 2)))
    return pieces


def on_device(
    tokens,
    cotangent,
    memory,
    query_weight,
    query_bias,
    key_weight,
    value_weight,
    value_bias,
    out_weight,
    out_bias,
    gain_one,
    shift_one,
    inner_weight,
    inner_bias,
    outer_weight,
    outer_bias,
    gain_two,
    shift_two,
    group_sizes,
    group_section,
    last_valid,
):
    width = memory.shape[1]
    ff = inner_weight.shape[1]
    dp_size = lax.axis_size("dp")
    chain_index = lax.axis_index("dp")
    head_index = lax.axis_index("head")
    side = head_index // 2
    core = head_index % 2
    quarter = query_weight.shape[1]
    device = chain_index * 4 + head_index
    divisors, sizes = jnp.array([2, 1, 4, 4], jnp.int32), jnp.array([2, 2, 4, dp_size], jnp.int32)
    place = (device // divisors) % sizes
    scalars = (place, group_sizes, group_section, last_valid)

    own_weights = (query_weight.T, key_weight.T, value_weight.T, out_weight)
    wide_weights = jnp.stack([weight.astype(F32) for weight in own_weights])
    far = fetch_far(wide_weights)
    partner = swap_core(wide_weights)
    places, far = [piece[:2] for piece in far], [piece[2] for piece in far]
    far_partner = [swap_core(piece) for piece in far]
    vectors = pack_vectors(
        place,
        (out_bias, gain_one, shift_one, outer_bias, gain_two, shift_two),
        query_bias,
        value_bias,
        inner_bias,
    )
    row = jnp.arange(VECTOR_ROWS)[:, None]
    split_rows = (row == QUERY_BIAS) | (row == VALUE_BIAS)
    for swap in (swap_core, swap_side):
        vectors = vectors + jnp.where(split_rows, swap(vectors), 0.0)
    token_rows = tokens.reshape(SEGS, SEG_LEN, width)

    weights, keys, values, own_query, *saved = memory_forward(
        places,
        scalars,
        token_rows,
        memory,
        own_weights,
        partner,
        far,
        far_partner,
        vectors,
        inner_weight,
        outer_weight,
    )
    context, probs = attend(scalars, own_query, keys, values)
    (
        layer_out,
        out_rows,
        d_hidden,
        d_hidden_low,
        d_context,
        sums,
        own_inner,
        own_outer,
        other_inner,
        other_outer,
    ) = feed(
        scalars,
        token_rows,
        context,
        cotangent.reshape(SEGS, SEG_LEN, width),
        weights,
        inner_weight,
        outer_weight,
        vectors,
    )

    piece = ff // dp_size
    back = partial(attend_back, place, own_query, keys, values, d_context, probs)
    held = back(CHAINED, SEGS - CHAINED)
    fast_path = dp_size == BLOCKS
    run = on_block if fast_path else on_any
    results = run(
        place,
        scalars,
        back,
        held,
        (own_inner, own_outer, other_inner, other_outer),
        partial(query_grads, place, token_rows, d_hidden),
        (context, d_hidden_low, weights, sums),
        partial(
            memory_backward,
            place,
            weights=weights,
            keys=keys,
            values=values,
            saved=saved[:9],
            vectors=vectors,
            inner_weight=inner_weight,
            outer_weight=outer_weight,
            packed=fast_path,
        ),
        partial(input_grads, place, token_rows, weights=weights),
        saved,
        out_rows,
    )
    grads, smalls, grad_inner, grad_outer, grad_tokens, others = results
    grad_query, grad_out, grad_key, grad_value = grads
    grad_memory, *grad_vectors, grad_qb, grad_vb, inner_bias_grad = smalls

    def both_cores(value, other):
        start = (1 - core) * HALF_ROWS
        value = lax.dynamic_update_slice_in_dim(value, other, start, 1)
        return value.reshape(SEGS * SEG_LEN, width)

    return (
        both_cores(layer_out, others[0]),
        both_cores(grad_tokens, others[1]),
        grad_memory,
        grad_query.T,
        grad_qb,
        grad_key.T,
        grad_value.T,
        grad_vb,
        grad_out,
        *grad_vectors[:3],
        grad_inner,
        inner_bias_grad,
        grad_outer,
        *grad_vectors[3:],
    )


def at_bits(value, bits):
    axis = 0
    for bit in bits:
        if bit is None:
            axis += 1
        else:
            value = lax.dynamic_index_in_dim(value, bit, axis, False)
    return value


def on_block(
    place, scalars, back, held, ffn, query_part, query_args, backward, input_part, saved, out_rows
):
    index = lax.axis_index("dp")
    fast, slow = index & 1, (index >> 1) & 1
    own_inner, own_outer, other_inner, other_outer = ffn
    early = saved[9:]
    early = early[:1] + [swap_dp(share, bits) for bits, share in enumerate(early) if bits]
    ffn = in_step(
        own_inner, own_outer, swap_core(other_inner), swap_core(other_outer), *early, *held
    )
    ffn, early, held = ffn[:4], ffn[4:8], ffn[8:]
    own_inner, own_outer, other_inner, other_outer = (
        value.reshape((2, 2, 2) + value.shape[1:]) for value in ffn
    )
    inner, outer = (own_inner, other_inner), (own_outer, other_outer)

    def total(terms, bits):
        terms = [at_bits(term, bits) for term in terms]
        return sum(terms[1:], terms[0])

    inner_moved = swap_dp(total(inner, (None, 1 - slow, None)), 2)
    outer_moved = swap_dp(total(outer, (None, None, 1 - fast)), 1)
    d_query, kv_own, kv_other, kv_mem = back(0, CHAINED, held)
    d_part, query_own, query_other, sums = query_part(d_query, *query_args)
    weights = query_args[2]
    values = in_step(
        inner_moved,
        outer_moved,
        d_part,
        query_own,
        query_other,
        sums,
        kv_own,
        kv_other,
        kv_mem,
        swap_core(kv_mem),
    )
    inner_moved, outer_moved, d_part, query_own, query_other, sums, kv_own, kv_other = values[:8]
    kv_mem = values[8:]

    def second(terms, moved, bits, axis, bit):
        def half(at):
            here = [at if place == axis else value for place, value in enumerate(bits)]
            rest = [None if value is None or place != axis else at for place, value in enumerate(here)]
            del rest[[i for i, value in enumerate(bits) if value is not None][0]]
            return total(terms, here) + at_bits(moved, rest)

        return half(bit), half(1 - bit)

    inner_kept, inner_sent = second(inner, inner_moved, (None, slow, None), 2, fast)
    outer_kept, outer_sent = second(outer, outer_moved, (None, None, fast), 1, slow)
    inner_moved, outer_moved = swap_dp(inner_sent, 1), swap_dp(outer_sent, 2)
    kv_other = swap_core(kv_other)
    query_other = swap_core(query_other)
    kv_more, query_mem, dense_mem, *late = backward(kv_mem)

    def cube(*arrays):
        return [value.reshape((2, 2, 2) + value.shape[1:]) for value in arrays]

    q_kept, q_sent = split(place, (1, 1, cube(query_own, query_other, query_mem)), limit=60)
    values = in_step(
        inner_kept,
        inner_moved,
        outer_kept,
        outer_moved,
        kv_other,
        kv_more,
        q_kept,
        q_sent,
        dense_mem,
        *late,
    )
    inner_kept, inner_moved, outer_kept, outer_moved, kv_other, kv_more = values[:6]
    q_kept, q_sent, dense_mem, *late = values[6:]
    q_moved = swap_dp(q_sent, 2)
    late = late[:1] + [swap_dp(share, bits) for bits, share in enumerate(late) if bits]
    grad_tokens, token_rows, dense_own, dense_other = input_part(
        d_part, kv_own, kv_other, kv_more, sums=sums
    )
    q_moved, *late, dense_own, dense_other = in_step(q_moved, *late, dense_own, dense_other)

    ffn_kept, ffn_sent = memory_shares(place, early, late, inner_kept, inner_moved, outer_kept, outer_moved)
    ffn_kept, ffn_sent, dense_own, dense_other = in_step(
        ffn_kept, ffn_sent, dense_own, swap_core(dense_other)
    )
    ffn_moved = swap_dp(ffn_sent, 4)
    d_kept, d_sent = split(place, (0, 2, cube(dense_own, dense_other, dense_mem)), limit=60)
    d_moved = swap_dp(d_sent, 1)
    q_kept, q_sent, d_kept, d_sent = split(
        place, (0, 1, [q_kept, q_moved]), (1, 1, [d_kept, d_moved])
    )
    q_moved, d_moved = swap_dp(q_sent, 1), swap_dp(d_sent, 2)
    q_part, _, d_part, _, ffn_mine, _ = split(
        place,
        (None, 0, [q_kept, q_moved]),
        (None, 0, [d_kept, d_moved]),
        (None, 0, [ffn_kept, ffn_moved]),
    )
    q_moved, d_moved = swap_dp(q_part, 4), swap_dp(d_part, 4)
    ffn_far = swap_side(ffn_mine)
    q_mine, _, d_mine, _ = split(place, (None, 0, [q_part, q_moved]), (None, 0, [d_part, d_moved]))
    q_moved, d_moved = swap_dp(q_mine, 1), swap_dp(d_mine, 2)
    pieces = (ffn_mine, swap_core(ffn_mine), ffn_far, swap_core(ffn_far))
    grad_inner, grad_outer = feed_final(place, pieces)
    q_mine, d_mine = join(place, (0, 1, q_mine, q_moved), (1, 1, d_mine, d_moved))
    halves = (q_mine, swap_dp(q_mine, 2), d_mine, swap_dp(d_mine, 1))
    grads = final(place, halves, grad_inner.shape[1])
    others = (swap_core(out_rows), swap_core(token_rows))
    return grads[:4], grads[4:], grad_inner, grad_outer, grad_tokens, others


def on_any(
    place, scalars, back, held, ffn, query_part, query_args, backward, input_part, saved, out_rows
):
    own_inner, own_outer, other_inner, other_outer = ffn
    dp_size = lax.axis_size("dp")
    quarter = own_inner.shape[1]
    width = 4 * quarter
    head_index = lax.axis_index("head")
    d_query, kv_own, kv_other, kv_mem = back(0, CHAINED, held)
    d_part, query_own, query_other, sums = query_part(d_query, *query_args)
    kv_mem = (kv_mem, swap_core(kv_mem))
    kv_more, query_mem, dense_mem, mem_d_inner, mem_d_total = backward(kv_mem)
    grad_tokens, token_rows, dense_own, dense_other = input_part(
        d_part, kv_own, swap_core(kv_other), kv_more, sums=sums
    )
    query = query_own + swap_core(query_other) + query_mem
    dense = dense_own + swap_core(dense_other) + dense_mem
    query, dense = lax.psum((query, dense), "dp")
    mem_active, mem_normed = saved[7], saved[8]

    def whole(own, other, rows, hidden):
        rows = lax.dynamic_slice_in_dim(rows, head_index * quarter, quarter, 2)
        rows = rows.reshape(-1, quarter)
        value = own + swap_core(other)
        value = value.transpose(1, 0, 2).reshape(quarter, -1)
        value = value + tn(rows, hidden.reshape(rows.shape[0], -1))
        value = lax.psum_scatter(value, "dp", scatter_dimension=1, tiled=True)
        return lax.all_gather(value, "head").reshape(width, -1)

    grad_inner = whole(own_inner, other_inner, mem_normed, mem_d_inner)
    grad_outer = whole(own_outer, other_outer, mem_d_total, mem_active).T
    rows = quarter // BLOCKS

    def part(value, index):
        return value[:, rows * index : rows * (index + 1)].reshape(quarter, width)

    sums = dense[:, 2 * rows : 2 * rows + SUM_PART].reshape(SUM_ROWS, width)
    piece = grad_inner.shape[1]
    at = lax.axis_index("dp") * piece
    smalls = (
        sums[MEMORY_SUM : MEMORY_SUM + MEM],
        *sums[:6],
        lax.dynamic_slice_in_dim(sums[QUERY_SUM], head_index * quarter, quarter, 0),
        lax.dynamic_slice_in_dim(sums[VALUE_SUM], head_index * quarter, quarter, 0),
        lax.dynamic_slice_in_dim(sums[6:QUERY_SUM].reshape(-1), at, piece, 0),
    )
    grads = (part(query, 0), part(query, 1), part(dense, 0), part(dense, 1))
    others = (swap_core(out_rows), swap_core(token_rows))
    return grads, smalls, grad_inner, grad_outer, grad_tokens, others


def solution(mesh):
    row, col, vec, every = P("dp", None), P(None, "head"), P("head"), P()
    placed = (row, row, every, col, vec, col, col, vec, P("head", None)) + (every,) * 11
    return jax.shard_map(
        on_device,
        mesh=mesh,
        in_specs=placed + (P("dp"),),
        out_specs=(
            row,
            row,
            every,
            col,
            vec,
            col,
            col,
            vec,
            P("head", None),
            every,
            every,
            every,
            P(None, "dp"),
            P("dp"),
            row,
            every,
            every,
            every,
        ),
        check_vma=False,
    )
```

```python
from functools import partial

import jax
import jax.numpy as jnp
from jax import lax
from jax.experimental import pallas as pl
from jax.experimental.pallas import tpu as pltpu
from jax.sharding import PartitionSpec as P

HEAD_DIM = 64
MEM = 10
MEM_PAD = 16
SEG_LEN = 512
SEGS = 3
CHAINED = SEGS - 1
KEYS = SEG_LEN + MEM_PAD
HALF_ROWS = SEG_LEN // 2
EPS = 1e-06
SCALE = HEAD_DIM ** (-0.5)
MASKED = -1000000000.0
LN_TWO = 0.6931471805599453

F32 = jnp.float32
BF16 = jnp.bfloat16


def nn(left, right):
    return jnp.dot(left, right, preferred_element_type=F32)


def nt(left, right):
    return lax.dot_general(left, right, (((1,), (1,)), ((), ())), preferred_element_type=F32)


def tn(left, right):
    return lax.dot_general(left, right, (((0,), (0,)), ((), ())), preferred_element_type=F32)


def norm_fwd(value, gain, shift):
    centered = value - jnp.mean(value, axis=-1, keepdims=True)
    spread = jnp.mean(centered * centered, axis=-1, keepdims=True)
    root = lax.rsqrt(spread + EPS)
    unit = centered * root
    return unit * gain + shift, unit, root


def norm_bwd(d_out, unit, root, gain):
    d_unit = d_out * gain
    mean_one = jnp.mean(d_unit, axis=-1, keepdims=True)
    mean_two = jnp.mean(d_unit * unit, axis=-1, keepdims=True)
    return root * (d_unit - mean_one - unit * mean_two)


def gelu_parts(inner):
    cdf = 0.5 * (1.0 + lax.erf(inner * 0.7071067811865476))
    pdf = jnp.exp(-0.5 * inner * inner) * 0.3989422804014327
    return inner * cdf, cdf + inner * pdf


def column_sum(value):
    return jnp.sum(value, axis=0, keepdims=True)


SHARE_SPACE = 256

SIDE, CORE, PART, CHAIN = range(4)


def limit_of(segment, place_ref, sizes_ref, sections_ref, last_ref):
    chain = place_ref[CHAIN]
    end, section = 0, 0
    for group in range(sizes_ref.shape[0]):
        start, end = end, end + sizes_ref[group]
        inside = jnp.logical_and(start <= chain, chain < end)
        section = jnp.where(inside, sections_ref[group], section)
    last = section % (SEGS - 1) + 1
    return jnp.where(segment < last, SEG_LEN, jnp.where(segment == last, last_ref[0], 0))


def key_bias(limit):
    row = lax.broadcasted_iota(jnp.int32, (KEYS, 1), 0)
    beyond = jnp.where((row >= SEG_LEN) & (row < SEG_LEN + MEM), LN_TWO, MASKED)
    return jnp.where(row < limit, 0.0, beyond)


OUT_BIAS, GAIN_ONE, SHIFT_ONE, OUTER_BIAS, GAIN_TWO, SHIFT_TWO, QUERY_BIAS, VALUE_BIAS = range(8)
INNER_BIAS = 8
VECTOR_ROWS = 16


def row_of(vectors, index):
    return vectors[index : index + 1]


def head_mask(width):
    count = width // HEAD_DIM
    shape = (count, MEM_PAD, width)
    head = lax.broadcasted_iota(jnp.int32, shape, 0)
    lane = lax.broadcasted_iota(jnp.int32, shape, 2) // HEAD_DIM
    return (head == lane).astype(F32)


def spread_heads(value, mask):
    count, rows, width = mask.shape
    return (value.astype(F32)[None] * mask).reshape(count * rows, width).astype(BF16)


def gather_heads(value, mask):
    return jnp.sum(value.reshape(mask.shape) * mask, axis=0)


def pack_vectors_kernel(place_ref, *refs):
    *vector_refs, query_ref, value_ref, inner_ref, out_ref = refs
    width = out_ref.shape[1]
    quarter = query_ref.shape[0]
    out_ref[...] = jnp.zeros_like(out_ref)
    for index, ref in enumerate(vector_refs):
        out_ref[index : index + 1] = ref[...].reshape(1, width)
    index = 2 * place_ref[SIDE] + place_ref[CORE]
    for row, ref in ((QUERY_BIAS, query_ref), (VALUE_BIAS, value_ref)):
        piece = ref[...].reshape(1, quarter)
        for at in range(4):
            columns = slice(quarter * at, quarter * (at + 1))
            out_ref[row : row + 1, columns] = jnp.where(index == at, piece, 0.0)
    for at in range(inner_ref.shape[0] // width):
        piece = inner_ref[width * at : width * (at + 1)].reshape(1, width)
        out_ref[INNER_BIAS + at : INNER_BIAS + at + 1] = piece


def pack_vectors(place, vectors, query_bias, value_bias, inner_bias):
    width = vectors[0].shape[0]
    vmem = pl.BlockSpec(memory_space=pltpu.VMEM)
    return pl.pallas_call(
        pack_vectors_kernel,
        in_specs=[pl.BlockSpec(memory_space=pltpu.SMEM)] + [vmem] * (len(vectors) + 3),
        out_specs=vmem,
        out_shape=jax.ShapeDtypeStruct((VECTOR_ROWS, width), F32),
        name="pack_vectors",
    )(place, *vectors, query_bias, value_bias, inner_bias)


def share_out(place_ref, refs, hidden_ref, wide_ref):
    at_fast, at_slow = place_ref[PART] % 2, place_ref[PART] // 2
    index = 2 * place_ref[SIDE] + place_ref[CORE]
    width = wide_ref.shape[2]
    half, quarter = width // 2, width // 4
    for bits, ref in enumerate(refs):
        base = 2 * (at_slow ^ (bits // 2)) + (at_fast ^ (bits % 2))
        for segment in range(CHAINED):
            rows = slice(MEM_PAD * segment, MEM_PAD * (segment + 1))
            for far in range(2):
                columns = pl.ds(pl.multiple_of((4 * far + base) * half, half), half)
                ref[rows, far * half : (far + 1) * half] = hidden_ref[segment, :, columns].astype(F32)
            wide = wide_ref[segment]
            piece = wide[:, :quarter]
            for other in range(1, 4):
                piece = jnp.where(
                    index == other, wide[:, quarter * other : quarter * (other + 1)], piece
                )
            ref[rows, width : width + quarter] = piece.astype(F32)
            gap = jnp.zeros((MEM_PAD, SHARE_SPACE - quarter), F32)
            ref[rows, width + quarter :] = gap


def memory_forward_kernel(
    places,
    place_ref,
    sizes_ref,
    sections_ref,
    last_ref,
    tokens_ref,
    memory_ref,
    own_q_ref,
    own_k_ref,
    own_v_ref,
    own_o_ref,
    partner_ref,
    vectors_ref,
    *refs,
):
    far_refs, far_partner_refs, refs = (
        refs[: len(places)],
        refs[len(places) : 2 * len(places)],
        refs[2 * len(places) :],
    )
    inner_hbm, outer_hbm, weights_hbm, keys_hbm, values_hbm, query_hbm, *refs = refs
    saved_hbm, (weights_ref, keys_ref, values_ref, query_ref) = refs[:13], refs[13:17]
    saved, (inner_ref, outer_ref, sems) = refs[17:30], refs[30:]
    (
        low_ref,
        mem_query_ref,
        mem_context_ref,
        mem_probs_ref,
        mem_hidden_ref,
        mem_total_ref,
        mem_slope_ref,
        mem_active_ref,
        mem_normed_ref,
        *share_refs,
    ) = saved
    copies = [
        pltpu.make_async_copy(inner_hbm, inner_ref, sems.at[0]),
        pltpu.make_async_copy(outer_hbm, outer_ref, sems.at[1]),
    ]
    for copy in copies:
        copy.start()
    side, core, part = place_ref[SIDE], place_ref[CORE], place_ref[PART]
    quarter = own_q_ref.shape[0]
    width = memory_ref.shape[1]

    def span_of(at_side, at_core, start=0, rows=quarter):
        start = (2 * at_side + at_core) * quarter + start
        return pl.ds(pl.multiple_of(start, 16), rows)

    for which, ref in enumerate((own_q_ref, own_k_ref, own_v_ref, own_o_ref)):
        weights_ref[which, span_of(side, core)] = ref[...]
        weights_ref[which, span_of(side, 1 - core)] = partner_ref[which].astype(BF16)
    for (bits, start), near_ref, other_ref in zip(places, far_refs, far_partner_refs):
        which, rows = part ^ bits, near_ref.shape[0]
        weights_ref[which, span_of(1 - side, core, start, rows)] = near_ref[...].astype(BF16)
        weights_ref[which, span_of(1 - side, 1 - core, start, rows)] = other_ref[...].astype(BF16)
    writes = [pltpu.make_async_copy(weights_ref, weights_hbm, sems.at[2])]
    writes[0].start()
    vectors = vectors_ref[...]
    query_bias = row_of(vectors, QUERY_BIAS)
    value_bias = row_of(vectors, VALUE_BIAS)

    def project(index, carry):
        segment, half = index // 2, index % 2
        span = pl.ds(half * HALF_ROWS, HALF_ROWS)
        rows = tokens_ref[segment, span]
        keys_ref[segment, span] = nt(rows, weights_ref[1]).astype(BF16)
        values_ref[segment, span] = (nt(rows, weights_ref[2]) + value_bias).astype(BF16)

        @pl.when(half == core)
        def _():
            query_ref[segment] = (nt(rows, weights_ref[0]) + query_bias).astype(BF16) * SCALE

        return carry

    lax.fori_loop(0, 2 * SEGS, project, 0)
    token_rows, mem_rows = pl.ds(0, SEG_LEN), pl.ds(SEG_LEN, MEM_PAD)
    pairs = ((keys_ref, keys_hbm), (values_ref, values_hbm))
    writes.append(pltpu.make_async_copy(query_ref, query_hbm, sems.at[3]))
    for index, (ref, hbm) in enumerate(pairs):
        writes.append(
            pltpu.make_async_copy(ref.at[:, token_rows], hbm.at[:, token_rows], sems.at[4 + index])
        )
    for write in writes[1:]:
        write.start()

    mask = head_mask(width)
    now = jnp.concatenate(
        [memory_ref[...].astype(F32), jnp.zeros((MEM_PAD - MEM, width), F32)], 0
    )
    for segment in range(SEGS):
        low = now.astype(BF16)
        low_ref[segment] = low
        keys_ref[segment, SEG_LEN:] = nt(low, weights_ref[1]).astype(BF16)
        values_ref[segment, SEG_LEN:] = (nt(low, weights_ref[2]) + value_bias).astype(BF16)
        if segment == CHAINED:
            break
        query = (nt(low, weights_ref[0]) + query_bias).astype(BF16) * SCALE
        mem_query_ref[segment] = query
        scores = nt(keys_ref[segment], spread_heads(query, mask))
        limit = limit_of(segment, place_ref, sizes_ref, sections_ref, last_ref)
        scores = scores + key_bias(limit)
        weights = jnp.exp(scores - jnp.max(scores, axis=0, keepdims=True))
        probs = weights * (1.0 / jnp.sum(weights, axis=0, keepdims=True))
        mem_probs_ref[segment] = probs
        context = gather_heads(tn(probs.astype(BF16), values_ref[segment]), mask).astype(BF16)
        mem_context_ref[segment] = context
        hidden = now + nn(context, weights_ref[3]) + row_of(vectors, OUT_BIAS)
        mem_hidden_ref[segment] = hidden
        normed, _, _ = norm_fwd(hidden, row_of(vectors, GAIN_ONE), row_of(vectors, SHIFT_ONE))
        mem_normed_ref[segment] = normed.astype(BF16)
        if segment == 0:
            copies[0].wait()
        inner_bias = [row_of(vectors, INNER_BIAS + i) for i in range(inner_ref.shape[1] // width)]
        inner_bias = jnp.concatenate(inner_bias, 1)
        active, slope = gelu_parts(nn(normed.astype(BF16), inner_ref[...]) + inner_bias)
        active = active.astype(BF16)
        mem_slope_ref[segment] = slope
        mem_active_ref[segment] = active
        if segment == 0:
            copies[1].wait()
        total = normed + nn(active, outer_ref[...]) + row_of(vectors, OUTER_BIAS)
        mem_total_ref[segment] = total
        now, _, _ = norm_fwd(total, row_of(vectors, GAIN_TWO), row_of(vectors, SHIFT_TWO))
    for index, (ref, hbm) in enumerate(pairs):
        writes.append(
            pltpu.make_async_copy(ref.at[:, mem_rows], hbm.at[:, mem_rows], sems.at[6 + index])
        )
        writes[-1].start()
    share_out(place_ref, share_refs, mem_active_ref, mem_normed_ref)
    for index, (ref, hbm) in enumerate(zip(saved, saved_hbm)):
        writes.append(pltpu.make_async_copy(ref, hbm, sems.at[8 + index]))
        writes[-1].start()
    for write in writes:
        write.wait()


def memory_forward(
    places, scalars, tokens, memory, own, partner, far, far_partner, vectors, inner_weight, outer_weight
):
    width = memory.shape[1]
    ff = inner_weight.shape[1]
    head_rows = MEM_PAD * width // HEAD_DIM
    vmem = pl.BlockSpec(memory_space=pltpu.VMEM)

    def like(shape, dtype):
        return jax.ShapeDtypeStruct(shape, dtype)

    saved = [
        ((SEGS, MEM_PAD, width), BF16),
        ((CHAINED, MEM_PAD, width), BF16),
        ((CHAINED, MEM_PAD, width), BF16),
        ((CHAINED, KEYS, head_rows), F32),
        ((CHAINED, MEM_PAD, width), F32),
        ((CHAINED, MEM_PAD, width), F32),
        ((CHAINED, MEM_PAD, ff), F32),
        ((CHAINED, MEM_PAD, ff), BF16),
        ((CHAINED, MEM_PAD, width), BF16),
    ] + [((CHAINED * MEM_PAD, width + SHARE_SPACE), F32)] * 4
    large = [
        ((4, width, width), BF16),
        ((SEGS, KEYS, width), BF16),
        ((SEGS, KEYS, width), BF16),
        ((SEGS, HALF_ROWS, width), BF16),
    ]
    return pl.pallas_call(
        partial(memory_forward_kernel, places),
        in_specs=[pl.BlockSpec(memory_space=pltpu.SMEM)] * 4
        + [vmem] * (8 + 2 * len(places))
        + [pl.BlockSpec(memory_space=pl.ANY)] * 2,
        out_specs=[pl.BlockSpec(memory_space=pltpu.HBM)] * 17,
        out_shape=[pltpu.HBM(*shape) for shape in large + saved],
        scratch_shapes=[pltpu.VMEM(*shape) for shape in large + saved]
        + [
            pltpu.VMEM((width, ff), BF16),
            pltpu.VMEM((ff, width), BF16),
            pltpu.SemaphoreType.DMA((21,)),
        ],
        compiler_params=pltpu.CompilerParams(vmem_limit_bytes=60 << 20),
        cost_estimate=pl.CostEstimate(flops=1000, bytes_accessed=1000, transcendentals=0),
        name="memory_forward",
    )(
        *scalars,
        tokens,
        memory,
        *own,
        partner,
        vectors,
        *far,
        *far_partner,
        inner_weight,
        outer_weight,
    )


def lane_masks(rows):
    lane = lax.broadcasted_iota(jnp.int32, (rows, 2 * HEAD_DIM), 1)
    first = (lane < HEAD_DIM).astype(F32)
    return first.astype(BF16), (1.0 - first).astype(BF16)


def pair_of(head):
    start = 2 * HEAD_DIM * (head // 2)
    return slice(start, start + 2 * HEAD_DIM)


def attend_kernel(
    place_ref, sizes_ref, sections_ref, last_ref, q_ref, k_ref, v_ref, out_ref, probs_ref
):
    limit = limit_of(pl.program_id(0), place_ref, sizes_ref, sections_ref, last_ref)
    bias = key_bias(limit)
    count = q_ref.shape[2] // HEAD_DIM
    q_masks, k_masks = lane_masks(q_ref.shape[1]), lane_masks(KEYS)

    def score(head):
        cols = pair_of(head)
        return nt(k_ref[0, :, cols], q_ref[0, :, cols] * q_masks[head % 2])

    def finish(head, probs, held):
        cols = pair_of(head)
        part = tn(probs, v_ref[0, :, cols] * k_masks[head % 2])
        if head % 2 == 0:
            return part
        out_ref[0, :, cols] = (held + part).astype(BF16)
        return None

    held = before = None
    later = score(0)
    for head in range(count):
        scores = later + bias
        if head + 1 < count:
            later = score(head + 1)
        if before is not None:
            held = finish(head - 1, before, held)
        weights = jnp.exp(scores - jnp.max(scores, axis=0, keepdims=True))
        before = (weights * (1.0 / jnp.sum(weights, axis=0, keepdims=True))).astype(BF16)
        probs_ref[0, head] = before
    finish(count - 1, before, held)


def attend(scalars, query, keys, values):
    segs, rows, width = query.shape
    wide = width // 2

    def block(length):
        return pl.BlockSpec((1, length, wide), lambda s, h, *_: (s, 0, h))

    return pl.pallas_call(
        attend_kernel,
        grid_spec=pltpu.PrefetchScalarGridSpec(
            num_scalar_prefetch=4,
            grid=(segs, 2),
            in_specs=[block(rows), block(KEYS), block(KEYS)],
            out_specs=[
                block(rows),
                pl.BlockSpec((1, wide // HEAD_DIM, KEYS, rows), lambda s, h, *_: (s, h, 0, 0)),
            ],
        ),
        out_shape=[
            jax.ShapeDtypeStruct(query.shape, BF16),
            jax.ShapeDtypeStruct((segs, width // HEAD_DIM, KEYS, rows), BF16),
        ],
        compiler_params=pltpu.CompilerParams(vmem_limit_bytes=60 << 20),
        cost_estimate=pl.CostEstimate(flops=1000, bytes_accessed=1000, transcendentals=0),
        name="attend",
    )(*scalars, query, keys, values)


def in_step_kernel(*refs):
    pass


def in_step(*values):
    anywhere = [pl.BlockSpec(memory_space=pl.ANY)] * len(values)
    return pl.pallas_call(
        in_step_kernel,
        in_specs=anywhere,
        out_specs=anywhere,
        out_shape=[jax.ShapeDtypeStruct(value.shape, value.dtype) for value in values],
        input_output_aliases={i: i for i in range(len(values))},
        name="in_step",
    )(*values)


def attend_back_kernel(through, place_ref, q_ref, k_ref, v_ref, d_ref, p_ref, *refs):
    dq_ref, own_ref, other_ref, mem_ref = refs[through:][:4]
    first_core = place_ref[CORE] == 0
    count = q_ref.shape[2] // HEAD_DIM
    q_masks, k_masks = lane_masks(q_ref.shape[1]), lane_masks(KEYS)

    def first(head):
        cols = pair_of(head)
        return nt(v_ref[0, :, cols], d_ref[0, :, cols] * q_masks[head % 2])

    def last(head, d_scores, held):
        cols, mask = pair_of(head), q_masks[head % 2]
        dv = nn(p_ref[0, head], d_ref[0, :, cols] * mask)
        dk = nn(d_scores, q_ref[0, :, cols] * mask)
        dq = tn(d_scores, k_ref[0, :, cols] * k_masks[head % 2])
        if head % 2 == 0:
            return dv, dk, dq
        for index, value in enumerate((held[1] + dk, held[0] + dv)):
            low, high = value[:HALF_ROWS], value[HALF_ROWS:SEG_LEN]
            own_ref[index, 0, :, cols] = jnp.where(first_core, low, high)
            other_ref[index, 0, :, cols] = jnp.where(first_core, high, low)
            mem_ref[index, 0, :, cols] = value[SEG_LEN:]
        dq_ref[0, :, cols] = ((held[2] + dq) * SCALE).astype(BF16)
        return None

    held = before = None
    later = first(0)
    for head in range(count):
        d_probs = later
        if head + 1 < count:
            later = first(head + 1)
        if before is not None:
            held = last(head - 1, before, held)
        probs = p_ref[0, head].astype(F32)
        delta = jnp.sum(probs * d_probs, axis=0, keepdims=True)
        before = (probs * (d_probs - delta)).astype(BF16)
    last(count - 1, before, held)


def attend_back(place, query, keys, values, d_context, probs, first, count, held=(), through=()):
    segs, rows, width = query.shape
    wide = width // 2

    def block(length):
        return pl.BlockSpec((1, length, wide), lambda s, h, place: (first + s, 0, h))

    def two(length):
        return pl.BlockSpec((2, 1, length, wide), lambda s, h, place: (0, first + s, 0, h))

    inputs = (query, keys, values, d_context, probs)
    at = 1 + len(inputs)
    aliases = {at + i: i for i in range(len(held))}
    aliases.update({at + len(held) + i: 4 + i for i in range(len(through))})
    return pl.pallas_call(
        partial(attend_back_kernel, len(held) + len(through)),
        grid_spec=pltpu.PrefetchScalarGridSpec(
            num_scalar_prefetch=1,
            grid=(count, 2),
            in_specs=[
                block(rows),
                block(KEYS),
                block(KEYS),
                block(rows),
                pl.BlockSpec(
                    (1, wide // HEAD_DIM, KEYS, rows),
                    lambda s, h, place: (first + s, h, 0, 0),
                ),
            ]
            + [pl.BlockSpec(memory_space=pl.ANY)] * (len(held) + len(through)),
            out_specs=[block(rows), two(HALF_ROWS), two(HALF_ROWS), two(MEM_PAD)]
            + [pl.BlockSpec(memory_space=pl.ANY)] * len(through),
        ),
        out_shape=[
            jax.ShapeDtypeStruct(query.shape, BF16),
            jax.ShapeDtypeStruct((2, segs, HALF_ROWS, width), F32),
            jax.ShapeDtypeStruct((2, segs, HALF_ROWS, width), F32),
            jax.ShapeDtypeStruct((2, segs, MEM_PAD, width), F32),
        ]
        + [jax.ShapeDtypeStruct(value.shape, value.dtype) for value in through],
        input_output_aliases=aliases,
        compiler_params=pltpu.CompilerParams(vmem_limit_bytes=60 << 20),
        cost_estimate=pl.CostEstimate(flops=1000, bytes_accessed=1000, transcendentals=0),
        name="attend_back",
    )(place, *inputs, *held, *through)


SUM_ROWS = 24
QUERY_SUM = 10
VALUE_SUM = 11
MEMORY_SUM = 12


def feed_kernel(
    place_ref,
    sizes_ref,
    sections_ref,
    last_ref,
    rows_ref,
    context_ref,
    cot_ref,
    out_weight_ref,
    inner_ref,
    outer_ref,
    vectors_ref,
    out_ref,
    out_rows_ref,
    d_hidden_ref,
    d_hidden_low_ref,
    d_context_ref,
    sums_ref,
    own_inner_hbm,
    own_outer_hbm,
    other_inner_hbm,
    other_outer_hbm,
    slope_ref,
    active_ref,
    grads_ref,
    sems,
):
    segment = pl.program_id(0)
    side, core = place_ref[SIDE], place_ref[CORE]
    vectors = vectors_ref[...]
    gain_one, gain_two = row_of(vectors, GAIN_ONE), row_of(vectors, GAIN_TWO)
    width = vectors.shape[1]
    half = width // 2
    quarter = width // 4
    chunks = [slice(at, at + width) for at in range(0, inner_ref.shape[1], width)]
    row = lax.broadcasted_iota(jnp.int32, (HALF_ROWS, 1), 0) + core * HALF_ROWS
    valid = row < limit_of(segment, place_ref, sizes_ref, sections_ref, last_ref)

    def of_side(value):
        return jnp.where(side == 0, value[:, :half], value[:, half:])

    def add_grads(which, index, value):
        for row_half in range(2):
            rows = value[quarter * row_half : quarter * (row_half + 1)]
            for part in range(2):
                at = 2 * index + part
                held = jnp.where(segment == 0, 0.0, grads_ref[which, row_half, at])
                grads_ref[which, row_half, at] = held + rows[:, half * part : half * (part + 1)]

    hidden = (
        rows_ref[0].astype(F32)
        + nn(context_ref[0], out_weight_ref[0])
        + row_of(vectors, OUT_BIAS)
    )
    normed, unit_one, root_one = norm_fwd(hidden, gain_one, row_of(vectors, SHIFT_ONE))
    normed_low = normed.astype(BF16)
    total = normed + row_of(vectors, OUTER_BIAS)
    for index, chunk in enumerate(chunks):
        inner = nn(normed_low, inner_ref[:, chunk]) + row_of(vectors, INNER_BIAS + index)
        active, slope = gelu_parts(inner)
        active = active.astype(BF16)
        active_ref[:, chunk] = active
        slope_ref[:, chunk] = slope
        total = total + nn(active, outer_ref[chunk])
    result, unit_two, root_two = norm_fwd(total, gain_two, row_of(vectors, SHIFT_TWO))
    result = jnp.where(valid, result, 0.0)
    out_ref[0] = result
    out_rows_ref[0] = result

    d_result = jnp.where(valid, cot_ref[0].astype(F32), 0.0)
    d_total = norm_bwd(d_result, unit_two, root_two, gain_two)
    d_total_low = d_total.astype(BF16)
    normed_half, d_total_half = of_side(normed_low), of_side(d_total_low)
    d_normed = d_total
    inner_sums = []
    for index, chunk in enumerate(chunks):
        d_inner = (nt(d_total_low, outer_ref[chunk]) * slope_ref[:, chunk]).astype(BF16)
        inner_sums.append(column_sum(d_inner.astype(F32)))
        d_normed = d_normed + nt(d_inner, inner_ref[:, chunk])
        add_grads(0, index, tn(normed_half, d_inner))
        add_grads(1, index, tn(d_total_half, active_ref[:, chunk]))
    final = segment == pl.num_programs(0) - 1
    targets = ((other_inner_hbm, own_inner_hbm), (other_outer_hbm, own_outer_hbm))
    copies = [
        pltpu.make_async_copy(
            grads_ref.at[which, core if own else 1 - core],
            targets[which][own],
            sems.at[which, own],
        )
        for own in range(2)
        for which in range(2)
    ]

    @pl.when(final)
    def _():
        for copy in copies:
            copy.start()

    d_hidden = norm_bwd(d_normed, unit_one, root_one, gain_one)
    d_hidden_ref[0] = d_hidden
    d_hidden_low = d_hidden.astype(BF16)
    d_hidden_low_ref[0] = d_hidden_low
    d_context_ref[0] = nt(d_hidden_low, out_weight_ref[0]).astype(BF16)
    sums = [
        column_sum(d_hidden),
        column_sum(d_normed * unit_one),
        column_sum(d_normed),
        column_sum(d_total),
        column_sum(d_result * unit_two),
        column_sum(d_result),
    ] + inner_sums
    sums = jnp.concatenate(sums + [jnp.zeros((SUM_ROWS - len(sums), width), F32)], 0)

    @pl.when(segment == 0)
    def _():
        sums_ref[...] = sums

    @pl.when(segment > 0)
    def _():
        sums_ref[...] += sums

    @pl.when(final)
    def _():
        for copy in copies:
            copy.wait()


def feed(scalars, tokens, context, cot, weights, inner_weight, outer_weight, vectors):
    width, ff = inner_weight.shape
    chunk = width // 2

    def own_half():
        return pl.BlockSpec((1, HALF_ROWS, width), lambda i, place, *_: (i, place[CORE], 0))

    def segment():
        return pl.BlockSpec((1, HALF_ROWS, width), lambda i, *_: (i, 0, 0))

    def fixed(shape, index=(0, 0)):
        return pl.BlockSpec(shape, lambda i, *_: index, pipeline_mode=pl.Buffered(1))

    like = pltpu.HBM
    per_segment = (SEGS, HALF_ROWS, width)
    grads_shape = (ff // chunk, width // 4, chunk)
    return pl.pallas_call(
        feed_kernel,
        grid_spec=pltpu.PrefetchScalarGridSpec(
            num_scalar_prefetch=4,
            grid=(SEGS,),
            in_specs=[
                own_half(),
                segment(),
                own_half(),
                fixed((1, width, width), (3, 0, 0)),
                fixed((width, ff)),
                fixed((ff, width)),
                fixed(vectors.shape),
            ],
            out_specs=[
                own_half(),
                segment(),
                segment(),
                segment(),
                segment(),
                pl.BlockSpec((SUM_ROWS, width), lambda i, *_: (0, 0)),
            ]
            + [pl.BlockSpec(memory_space=pl.ANY)] * 4,
            scratch_shapes=[
                pltpu.VMEM((HALF_ROWS, ff), F32),
                pltpu.VMEM((HALF_ROWS, ff), BF16),
                pltpu.VMEM((2, 2) + grads_shape, F32),
                pltpu.SemaphoreType.DMA((2, 2)),
            ],
        ),
        out_shape=[
            like((SEGS, SEG_LEN, width), F32),
            like(per_segment, F32),
            like(per_segment, F32),
            like(per_segment, BF16),
            like(per_segment, BF16),
            like((SUM_ROWS, width), F32),
        ]
        + [like(grads_shape, F32)] * 4,
        compiler_params=pltpu.CompilerParams(vmem_limit_bytes=60 << 20),
        cost_estimate=pl.CostEstimate(flops=1000, bytes_accessed=1000, transcendentals=0),
        name="feed",
    )(*scalars, tokens, context, cot, weights, inner_weight, outer_weight, vectors)


BLOCKS = 8
SUM_PART = SUM_ROWS // BLOCKS
SUM_SPACE = 8


def block_rows(width):
    rows = width // 4 // BLOCKS
    return 2 * rows, 2 * rows + SUM_SPACE


def to_blocks(ref, matrices, sums=None):
    rows = (ref.shape[1] - (0 if sums is None else SUM_SPACE)) // 2
    for block in range(BLOCKS):
        for index, matrix in enumerate(matrices):
            ref[block, rows * index : rows * (index + 1)] = matrix(rows * block, rows)
        if sums is not None:
            part = sums[SUM_PART * block : SUM_PART * (block + 1)]
            filler = jnp.zeros((SUM_SPACE - SUM_PART, part.shape[1]), F32)
            ref[block, 2 * rows :] = jnp.concatenate([part, filler], 0)


def memory_backward_kernel(
    packed,
    place_ref,
    kv_mem_ref,
    kv_mem_other_ref,
    low_ref,
    mem_query_ref,
    mem_context_ref,
    mem_probs_ref,
    mem_hidden_ref,
    mem_total_ref,
    mem_slope_ref,
    mem_active_ref,
    mem_normed_ref,
    vectors_ref,
    weights_hbm,
    keys_hbm,
    values_hbm,
    inner_hbm,
    outer_hbm,
    kv_rows_ref,
    query_dense_ref,
    dense_ref,
    *refs,
):
    share_refs, refs = refs[:-9], refs[-9:]
    weights_ref, keys_ref, values_ref, inner_ref, outer_ref, grad_ref, d_inner_ref, d_total_ref, sems = refs
    order = [(weights_hbm.at[at], weights_ref.at[at]) for at in (1, 2)]
    order += [(outer_hbm, outer_ref), (inner_hbm, inner_ref)]
    order += [(weights_hbm.at[3], weights_ref.at[3])]
    for segment in reversed(range(CHAINED)):
        order += [(values_hbm.at[segment], values_ref.at[segment])]
        order += [(keys_hbm.at[segment], keys_ref.at[segment])]
        if segment == CHAINED - 1:
            order += [(weights_hbm.at[0], weights_ref.at[0])]
    copies = [
        pltpu.make_async_copy(source, target, sems.at[index])
        for index, (source, target) in enumerate(order)
    ]
    for copy in copies:
        copy.start()
    arrived = iter(copies)

    def wait(count):
        for _ in range(count):
            next(arrived).wait()

    side, core = place_ref[0], place_ref[1]
    width = low_ref.shape[2]
    quarter = width // 4
    vectors = vectors_ref[...]
    gain_one, gain_two = row_of(vectors, GAIN_ONE), row_of(vectors, GAIN_TWO)
    mask = head_mask(width)
    own = pl.ds(core * HALF_ROWS, HALF_ROWS)
    d_memory = None
    sums = None
    queries, hiddens, key_rows, value_rows = [], [], [], []
    for segment in reversed(range(SEGS)):
        d_keys = kv_mem_ref[0, segment] + kv_mem_other_ref[0, segment]
        d_values = kv_mem_ref[1, segment] + kv_mem_other_ref[1, segment]
        if d_memory is None:
            d_next = None
        else:
            normed, unit_one, root_one = norm_fwd(
                mem_hidden_ref[segment], gain_one, row_of(vectors, SHIFT_ONE)
            )
            _, unit_two, root_two = norm_fwd(
                mem_total_ref[segment], gain_two, row_of(vectors, SHIFT_TWO)
            )
            d_total = norm_bwd(d_memory, unit_two, root_two, gain_two)
            d_total_low = d_total.astype(BF16)
            if segment == CHAINED - 1:
                wait(1)
            d_inner = (nt(d_total_low, outer_ref[...]) * mem_slope_ref[segment]).astype(BF16)
            if segment == CHAINED - 1:
                wait(1)
            d_normed = d_total + nt(d_inner, inner_ref[...])
            d_hidden = norm_bwd(d_normed, unit_one, root_one, gain_one)
            d_hidden_low = d_hidden.astype(BF16)
            if segment == CHAINED - 1:
                wait(1)
            d_context = spread_heads(nt(d_hidden_low, weights_ref[3]).astype(BF16), mask)
            query = spread_heads(mem_query_ref[segment], mask)
            probs = mem_probs_ref[segment]
            probs_low = probs.astype(BF16)
            wait(1)
            d_probs = nt(values_ref[segment], d_context)
            delta = jnp.sum(probs * d_probs, axis=0, keepdims=True)
            d_scores = (probs * (d_probs - delta)).astype(BF16)
            wait(1)
            d_query = gather_heads(tn(d_scores, keys_ref[segment]), mask) * SCALE
            d_query = d_query.astype(BF16)
            more_keys = nn(d_scores, query)
            more_values = nn(probs_low, d_context)
            grad_ref[0, :SEG_LEN] = more_keys[:SEG_LEN]
            grad_ref[1, :SEG_LEN] = more_values[:SEG_LEN]
            kv_rows_ref[0, segment] = grad_ref[0, own]
            kv_rows_ref[1, segment] = grad_ref[1, own]
            d_keys = d_keys + more_keys[SEG_LEN:]
            d_values = d_values + more_values[SEG_LEN:]
            if segment == CHAINED - 1:
                wait(1)
            d_next = d_hidden + nn(d_query, weights_ref[0])
            queries.append(d_query)
            hiddens.append(d_hidden_low)
            d_total_ref[segment] = d_total_low
            d_inner_ref[segment] = d_inner
            wide = column_sum(d_inner.astype(F32))
            rows = [
                column_sum(d_hidden),
                column_sum(d_normed * unit_one),
                column_sum(d_normed),
                column_sum(d_total),
                column_sum(d_memory * unit_two),
                column_sum(d_memory),
            ]
            rows += [wide[:, at : at + width] for at in range(0, wide.shape[1], width)]
            rows.append(column_sum(d_query.astype(F32)))
            rows = jnp.concatenate(rows, 0)
            sums = rows if sums is None else sums + rows
        d_keys, d_values = d_keys.astype(BF16), d_values.astype(BF16)
        key_rows.append(d_keys)
        value_rows.append(d_values)
        if segment == CHAINED:
            wait(2)
        d_next = 0.0 if d_next is None else d_next
        d_memory = d_next + nn(d_keys, weights_ref[1]) + nn(d_values, weights_ref[2])
    low = [low_ref[segment] for segment in reversed(range(SEGS))]
    low_all = jnp.concatenate(low, 0)
    low_chained = jnp.concatenate(low[1:], 0)
    context = jnp.concatenate([mem_context_ref[s] for s in reversed(range(CHAINED))], 0)
    pairs = (
        (jnp.concatenate(queries, 0), low_chained),
        (context, jnp.concatenate(hiddens, 0)),
        (jnp.concatenate(key_rows, 0), low_all),
        (jnp.concatenate(value_rows, 0), low_all),
    )
    start = (2 * side + core) * quarter

    def part(index):
        return lambda at, rows: grad_ref[index, pl.ds(pl.multiple_of(start + at, 8), rows)]

    value_sum = column_sum(jnp.concatenate(value_rows, 0).astype(F32))
    filler = jnp.zeros((SUM_ROWS - MEMORY_SUM - MEM, width), F32)
    sums = jnp.concatenate([sums, value_sum, d_memory[:MEM], filler], 0)
    for first, ref, extra in ((0, query_dense_ref, None), (2, dense_ref, sums)):
        for index in range(2):
            grad_ref[index, :width] = tn(*pairs[first + index])
        to_blocks(ref, [part(0), part(1)], extra)
    if not packed:
        share_refs[0][...] = d_inner_ref[...]
        share_refs[1][...] = d_total_ref[...]
        return
    share_out(place_ref, share_refs, d_inner_ref, d_total_ref)


def memory_backward(
    place, kv_mem, weights, keys, values, saved, vectors, inner_weight, outer_weight, packed
):
    width, ff = inner_weight.shape
    vmem = pl.BlockSpec(memory_space=pltpu.VMEM)
    query_rows, key_rows = block_rows(width)
    if packed:
        shares = [((CHAINED * MEM_PAD, width + SHARE_SPACE), F32)] * 4
    else:
        shares = [((CHAINED, MEM_PAD, ff), BF16), ((CHAINED, MEM_PAD, width), BF16)]
    shapes = [
        ((2, CHAINED, HALF_ROWS, width), F32),
        ((BLOCKS, query_rows, width), F32),
        ((BLOCKS, key_rows, width), F32),
    ] + shares
    return pl.pallas_call(
        partial(memory_backward_kernel, packed),
        in_specs=[pl.BlockSpec(memory_space=pltpu.SMEM)]
        + [vmem] * 12
        + [pl.BlockSpec(memory_space=pl.ANY)] * 5,
        out_specs=[vmem] * len(shapes),
        out_shape=[jax.ShapeDtypeStruct(shape, dtype) for shape, dtype in shapes],
        scratch_shapes=[
            pltpu.VMEM(weights.shape, BF16),
            pltpu.VMEM((CHAINED,) + keys.shape[1:], BF16),
            pltpu.VMEM((CHAINED,) + keys.shape[1:], BF16),
            pltpu.VMEM((width, ff), BF16),
            pltpu.VMEM((ff, width), BF16),
            pltpu.VMEM((2, width, width), F32),
            pltpu.VMEM((CHAINED, MEM_PAD, ff), BF16),
            pltpu.VMEM((CHAINED, MEM_PAD, width), BF16),
            pltpu.SemaphoreType.DMA((10,)),
        ],
        compiler_params=pltpu.CompilerParams(vmem_limit_bytes=60 << 20),
        cost_estimate=pl.CostEstimate(flops=1000, bytes_accessed=1000, transcendentals=0),
        name="memory_backward",
    )(place, *kv_mem, *saved, vectors, weights, keys, values, inner_weight, outer_weight)


def grads_out(place_ref, grads_ref, own_ref, other_ref, sums=None):
    quarter = grads_ref.shape[1] // 2
    core = place_ref[CORE]
    for ref, at in ((own_ref, core), (other_ref, 1 - core)):

        def part(index, at=at):
            return lambda row, rows: grads_ref[
                index, pl.ds(pl.multiple_of(at * quarter + row, 8), rows)
            ]

        to_blocks(ref, [part(0), part(1)], sums)


def query_grads_kernel(
    place_ref,
    tokens_ref,
    d_hidden_ref,
    d_query_ref,
    context_ref,
    d_hidden_low_ref,
    weights_ref,
    sums_in_ref,
    out_ref,
    own_ref,
    other_ref,
    sums_ref,
    grads_ref,
):
    segment = pl.program_id(0)
    half = out_ref.shape[2] // 2
    d_query = d_query_ref[0]
    out_ref[0] = d_hidden_ref[0] + nn(d_query, weights_ref[0])
    first_side = place_ref[SIDE] == 0

    @pl.when(segment == 0)
    def _():
        grads_ref[...] = jnp.zeros_like(grads_ref)
        sums_ref[...] = sums_in_ref[...]

    pairs = ((d_query, tokens_ref[0]), (context_ref[0], d_hidden_low_ref[0]))
    for index, (cols, against) in enumerate(pairs):
        grads_ref[index] += tn(jnp.where(first_side, cols[:, :half], cols[:, half:]), against)
    sums_ref[QUERY_SUM : QUERY_SUM + 1] += column_sum(d_query.astype(F32))

    @pl.when(segment == pl.num_programs(0) - 1)
    def _():
        grads_out(place_ref, grads_ref, own_ref, other_ref)


def query_grads(place, tokens, d_hidden, d_query, context, d_hidden_low, weights, sums):
    width = tokens.shape[2]

    def own_half():
        return pl.BlockSpec((1, HALF_ROWS, width), lambda i, place: (i, place[CORE], 0))

    def segment():
        return pl.BlockSpec((1, HALF_ROWS, width), lambda i, place: (i, 0, 0))

    def whole(shape):
        return pl.BlockSpec(shape, lambda i, place: (0,) * len(shape))

    shapes = [(BLOCKS, block_rows(width)[0], width)] * 2 + [(SUM_ROWS, width)]
    return pl.pallas_call(
        query_grads_kernel,
        grid_spec=pltpu.PrefetchScalarGridSpec(
            num_scalar_prefetch=1,
            grid=(SEGS,),
            in_specs=[
                own_half(),
                segment(),
                segment(),
                segment(),
                segment(),
                whole((1, width, width)),
                whole((SUM_ROWS, width)),
            ],
            out_specs=[segment()] + [whole(shape) for shape in shapes],
            scratch_shapes=[pltpu.VMEM((2, width // 2, width), F32)],
        ),
        out_shape=[
            jax.ShapeDtypeStruct(shape, F32) for shape in [(SEGS, HALF_ROWS, width)] + shapes
        ],
        compiler_params=pltpu.CompilerParams(vmem_limit_bytes=60 << 20),
        cost_estimate=pl.CostEstimate(flops=1000, bytes_accessed=1000, transcendentals=0),
        name="query_grads",
    )(place, tokens, d_hidden, d_query, context, d_hidden_low, weights, sums)


def input_grads_kernel(
    place_ref,
    tokens_ref,
    d_part_ref,
    kv_own_ref,
    kv_other_ref,
    kv_more_ref,
    key_ref,
    value_ref,
    sums_in_ref,
    out_ref,
    rows_ref,
    own_ref,
    other_ref,
    grads_ref,
    sums_ref,
):
    segment = pl.program_id(0)
    width = out_ref.shape[2]
    half = width // 2
    more = jnp.where(segment < CHAINED, 1.0, 0.0)
    d_keys = (kv_own_ref[0, 0] + kv_other_ref[0, 0] + more * kv_more_ref[0, 0]).astype(BF16)
    d_values = (kv_own_ref[1, 0] + kv_other_ref[1, 0] + more * kv_more_ref[1, 0]).astype(BF16)
    d_inputs = d_part_ref[0] + nn(d_keys, key_ref[0]) + nn(d_values, value_ref[0])
    out_ref[0] = d_inputs
    rows_ref[0] = d_inputs
    first_side = place_ref[SIDE] == 0

    @pl.when(segment == 0)
    def _():
        grads_ref[...] = jnp.zeros_like(grads_ref)
        sums_ref[...] = sums_in_ref[...]

    for index, cols in enumerate((d_keys, d_values)):
        cols = jnp.where(first_side, cols[:, :half], cols[:, half:])
        grads_ref[index] += tn(cols, tokens_ref[0])
    sums_ref[VALUE_SUM : VALUE_SUM + 1] += column_sum(d_values.astype(F32))

    @pl.when(segment == pl.num_programs(0) - 1)
    def _():
        grads_out(place_ref, grads_ref, own_ref, other_ref, sums_ref[...])


def input_grads(place, tokens, d_part, kv_own, kv_other, kv_more, weights, sums):
    width = tokens.shape[2]

    def own_half():
        return pl.BlockSpec((1, HALF_ROWS, width), lambda i, place: (i, place[CORE], 0))

    def segment():
        return pl.BlockSpec((1, HALF_ROWS, width), lambda i, place: (i, 0, 0))

    def two(last):
        return pl.BlockSpec(
            (2, 1, HALF_ROWS, width), lambda i, place: (0, jnp.minimum(i, last), 0, 0)
        )

    def weight(which):
        return pl.BlockSpec((1, width, width), lambda i, place: (which, 0, 0))

    dense = jax.ShapeDtypeStruct((BLOCKS, block_rows(width)[1], width), F32)
    dense_spec = pl.BlockSpec(dense.shape, lambda i, place: (0, 0, 0))
    return pl.pallas_call(
        input_grads_kernel,
        grid_spec=pltpu.PrefetchScalarGridSpec(
            num_scalar_prefetch=1,
            grid=(SEGS,),
            in_specs=[
                own_half(),
                segment(),
                two(SEGS - 1),
                two(SEGS - 1),
                two(CHAINED - 1),
                weight(1),
                weight(2),
                pl.BlockSpec((SUM_ROWS, width), lambda i, place: (0, 0)),
            ],
            out_specs=[own_half(), segment(), dense_spec, dense_spec],
            scratch_shapes=[
                pltpu.VMEM((2, width // 2, width), F32),
                pltpu.VMEM((SUM_ROWS, width), F32),
            ],
        ),
        out_shape=[
            jax.ShapeDtypeStruct((SEGS, SEG_LEN, width), F32),
            jax.ShapeDtypeStruct((SEGS, HALF_ROWS, width), F32),
            dense,
            dense,
        ],
        compiler_params=pltpu.CompilerParams(vmem_limit_bytes=60 << 20),
        cost_estimate=pl.CostEstimate(flops=1000, bytes_accessed=1000, transcendentals=0),
        name="input_grads",
    )(place, tokens, d_part, kv_own, kv_other, kv_more, weights, weights, sums)


def memory_shares_kernel(place_ref, *refs):
    early_refs, late_refs, refs = refs[:4], refs[4:8], refs[8:]
    inner_kept, inner_moved, outer_kept, outer_moved, keep_ref, send_ref = refs
    mine = place_ref[CHAIN] // 4
    quarter = keep_ref.shape[1]
    half = keep_ref.shape[2]
    width = 2 * half
    early, late = (
        jnp.concatenate([ref[...] for ref in share], 0).astype(BF16)
        for share in (early_refs, late_refs)
    )
    active, normed = early[:, :width], early[:, width : width + quarter]
    d_inner, d_total = late[:, :width], late[:, width : width + quarter]
    sides = (
        (inner_kept, inner_moved, normed, d_inner),
        (outer_kept, outer_moved, d_total, active),
    )
    for which, (kept_ref, moved_ref, factor, hidden) in enumerate(sides):
        more = tn(factor, hidden)
        parts = [kept_ref[at] + moved_ref[at] + more[:, half * at : half * (at + 1)] for at in (0, 1)]
        keep_ref[which] = jnp.where(mine == 0, parts[0], parts[1])
        send_ref[which] = jnp.where(mine == 0, parts[1], parts[0])


def memory_shares(place, early, late, inner_kept, inner_moved, outer_kept, outer_moved):
    vmem = pl.BlockSpec(memory_space=pltpu.VMEM)
    shape = jax.ShapeDtypeStruct((2,) + inner_kept.shape[1:], F32)
    return pl.pallas_call(
        memory_shares_kernel,
        in_specs=[pl.BlockSpec(memory_space=pltpu.SMEM)] + [vmem] * 12,
        out_specs=[vmem] * 2,
        out_shape=[shape, shape],
        compiler_params=pltpu.CompilerParams(vmem_limit_bytes=60 << 20),
        name="memory_shares",
    )(place, *early, *late, inner_kept, inner_moved, outer_kept, outer_moved)


def split_kernel(bits, counts, unused, place_ref, *refs):
    ins, outs = refs[: sum(counts)], refs[sum(counts) + unused :]
    for index, (bit, count) in enumerate(zip(bits, counts)):
        terms, ins = ins[:count], ins[count:]
        if bit is None:
            outs[2 * index][...] = sum((ref[...] for ref in terms[1:]), terms[0][...])
            continue
        mine = (place_ref[CHAIN] >> bit) & 1
        for out, at in ((outs[2 * index], mine), (outs[2 * index + 1], 1 - mine)):
            out[...] = sum((ref[:, at] for ref in terms[1:]), terms[0][:, at])


def split(place, *items, limit=32, after=()):
    terms, bits, counts, shapes, results = [], [], [], [], []
    for bit, axis, values in items:
        shape = values[0].shape
        bits.append(bit)
        counts.append(len(values))
        if bit is None:
            terms += values
            shapes += [shape, (8, 128)]
            results += [shape, (8, 128)]
            continue
        ahead = 1
        for size in shape[:axis]:
            ahead *= size
        terms += [value.reshape((ahead, 2, -1) + shape[-2:]) for value in values]
        half = shape[:axis] + shape[axis + 1 :]
        inner = terms[-1].shape
        shapes += [inner[:1] + inner[2:]] * 2
        results += [half] * 2
    vmem = pl.BlockSpec(memory_space=pltpu.VMEM)
    outs = pl.pallas_call(
        partial(split_kernel, tuple(bits), tuple(counts), len(after)),
        in_specs=[pl.BlockSpec(memory_space=pltpu.SMEM)]
        + [vmem] * len(terms)
        + [pl.BlockSpec(memory_space=pl.ANY)] * len(after),
        out_specs=[vmem] * len(shapes),
        out_shape=[jax.ShapeDtypeStruct(shape, F32) for shape in shapes],
        compiler_params=pltpu.CompilerParams(vmem_limit_bytes=limit << 20),
        name="split",
    )(place, *terms, *after)
    return [out.reshape(shape) for out, shape in zip(outs, results)]


def join_kernel(bits, unused, place_ref, *refs):
    ins, outs = refs[: 2 * len(bits)], refs[2 * len(bits) + unused :]
    for index, bit in enumerate(bits):
        mine = (place_ref[CHAIN] >> bit) & 1
        outs[index][:, mine] = ins[2 * index][...]
        outs[index][:, 1 - mine] = ins[2 * index + 1][...]


def join(place, *items, after=()):
    terms, bits, shapes, results = [], [], [], []
    for bit, axis, own, other in items:
        shape = own.shape
        ahead = 1
        for size in shape[:axis]:
            ahead *= size
        terms += [value.reshape((ahead, -1) + shape[-2:]) for value in (own, other)]
        bits.append(bit)
        inner = terms[-1].shape
        shapes.append(inner[:1] + (2,) + inner[1:])
        results.append(shape[:axis] + (2,) + shape[axis:])
    vmem = pl.BlockSpec(memory_space=pltpu.VMEM)
    outs = pl.pallas_call(
        partial(join_kernel, tuple(bits), len(after)),
        in_specs=[pl.BlockSpec(memory_space=pltpu.SMEM)]
        + [vmem] * len(terms)
        + [pl.BlockSpec(memory_space=pl.ANY)] * len(after),
        out_specs=[vmem] * len(shapes),
        out_shape=[jax.ShapeDtypeStruct(shape, F32) for shape in shapes],
        compiler_params=pltpu.CompilerParams(vmem_limit_bytes=32 << 20),
        name="join",
    )(place, *terms, *after)
    return [out.reshape(shape) for out, shape in zip(outs, results)]


def feed_final_kernel(place_ref, *refs):
    pieces, (inner_ref, outer_ref, wide_ref) = refs[:4], refs[4:]
    side, core = place_ref[SIDE], place_ref[CORE]
    quarter = pieces[0].shape[1]
    places = (
        2 * side + core,
        2 * side + 1 - core,
        2 * (1 - side) + core,
        2 * (1 - side) + 1 - core,
    )
    for ref, at in zip(pieces, places):
        rows = pl.ds(pl.multiple_of(at * quarter, 8), quarter)
        inner_ref[rows] = ref[0]
        wide_ref[rows] = ref[1]
    outer_ref[...] = wide_ref[...].T


def feed_final(place, pieces):
    quarter, piece = pieces[0].shape[1:]
    vmem = pl.BlockSpec(memory_space=pltpu.VMEM)
    shapes = [(4 * quarter, piece), (piece, 4 * quarter)]
    return pl.pallas_call(
        feed_final_kernel,
        in_specs=[pl.BlockSpec(memory_space=pltpu.SMEM)] + [vmem] * 4,
        out_specs=[vmem] * 2,
        out_shape=[jax.ShapeDtypeStruct(shape, F32) for shape in shapes],
        scratch_shapes=[pltpu.VMEM((4 * quarter, piece), F32)],
        compiler_params=pltpu.CompilerParams(vmem_limit_bytes=32 << 20),
        name="feed_final",
    )(place, *pieces)


def final_kernel(place_ref, query_own, query_other, dense_own, dense_other, *refs):
    grad_query, grad_out, grad_key, grad_value, memory_ref, *refs = refs
    *vector_refs, query_bias_ref, value_bias_ref, inner_bias_ref, sums_ref = refs
    chain = place_ref[CHAIN]
    fast = chain % 2

    def put(ref, block, value):
        rows = value.shape[0]
        ref[pl.ds(pl.multiple_of(block * rows, 8), rows)] = value

    rows = query_own.shape[2] // 2
    for far in range(2):
        for near in range(2):
            for source, at in ((query_own, fast), (query_other, 1 - fast)):
                block = 4 * far + 2 * near + at
                put(grad_query, block, source[far, near, :rows])
                put(grad_out, block, source[far, near, rows:])
            for source, at in ((dense_own, fast), (dense_other, 1 - fast)):
                block = 4 * far + 2 * near + at
                put(grad_key, block, source[far, near, :rows])
                put(grad_value, block, source[far, near, rows : 2 * rows])
                put(sums_ref, block, source[far, near, 2 * rows :])
    width = sums_ref.shape[1]
    quarter, piece = query_bias_ref.shape[0], inner_bias_ref.shape[0]

    def row(index):
        at = SUM_SPACE * (index // SUM_PART) + index % SUM_PART
        return sums_ref[at : at + 1]

    for index, ref in enumerate(vector_refs):
        ref[...] = row(index).reshape(width)
    own = 2 * place_ref[SIDE] + place_ref[CORE]
    for ref, index in ((query_bias_ref, QUERY_SUM), (value_bias_ref, VALUE_SUM)):
        whole = row(index)
        value = whole[:, :quarter]
        for other in range(1, 4):
            value = jnp.where(own == other, whole[:, quarter * other : quarter * (other + 1)], value)
        ref[...] = value.reshape(quarter)
    count = width // piece
    value = jnp.zeros((1, piece), F32)
    for index in range(QUERY_SUM - len(vector_refs)):
        whole = row(len(vector_refs) + index)
        for part in range(count):
            here = chain == count * index + part
            value = jnp.where(here, whole[:, piece * part : piece * (part + 1)], value)
    inner_bias_ref[...] = value.reshape(piece)
    for index in range(MEM):
        memory_ref[index : index + 1] = row(MEMORY_SUM + index)


def final(place, halves, piece):
    width = halves[0].shape[3]
    quarter = width // 4
    vmem = pl.BlockSpec(memory_space=pltpu.VMEM)
    shapes = [(quarter, width)] * 4 + [(MEM, width)] + [(width,)] * 6
    shapes += [(quarter,), (quarter,), (piece,)]
    return pl.pallas_call(
        final_kernel,
        in_specs=[pl.BlockSpec(memory_space=pltpu.SMEM)] + [vmem] * 4,
        out_specs=[vmem] * len(shapes),
        out_shape=[jax.ShapeDtypeStruct(shape, F32) for shape in shapes],
        scratch_shapes=[pltpu.VMEM((BLOCKS * SUM_SPACE, width), F32)],
        compiler_params=pltpu.CompilerParams(vmem_limit_bytes=32 << 20),
        name="final",
    )(place, *halves)


def swap_core(value):
    return lax.ppermute(value, "head", [(0, 1), (1, 0), (2, 3), (3, 2)])


def swap_side(value):
    return lax.ppermute(value, "head", [(0, 2), (2, 0), (1, 3), (3, 1)])


def swap_dp(value, bits):
    size = lax.axis_size("dp")
    return lax.ppermute(value, "dp", [(i, i ^ bits) for i in range(size)])


def fetch_far(value):
    part = lax.axis_index("dp") % 4
    mine = lax.dynamic_index_in_dim(value, part, 0, False)
    rows = mine.shape[0]
    half, quarter = rows // 2, rows // 4
    pieces = []
    for start in (0, half):
        own = swap_side(mine[start : start + half])
        fast, slow = swap_dp(own, 1), swap_dp(own, 2)
        pieces += [(0, start, own), (1, start, fast), (2, start, slow)]
        pieces.append((3, start, swap_dp(slow[:quarter], 1)))
        pieces.append((3, start + quarter, swap_dp(fast[quarter:], 2)))
    return pieces


def on_device(
    tokens,
    cotangent,
    memory,
    query_weight,
    query_bias,
    key_weight,
    value_weight,
    value_bias,
    out_weight,
    out_bias,
    gain_one,
    shift_one,
    inner_weight,
    inner_bias,
    outer_weight,
    outer_bias,
    gain_two,
    shift_two,
    group_sizes,
    group_section,
    last_valid,
):
    width = memory.shape[1]
    ff = inner_weight.shape[1]
    dp_size = lax.axis_size("dp")
    chain_index = lax.axis_index("dp")
    head_index = lax.axis_index("head")
    side = head_index // 2
    core = head_index % 2
    quarter = query_weight.shape[1]
    device = chain_index * 4 + head_index
    divisors, sizes = jnp.array([2, 1, 4, 4], jnp.int32), jnp.array([2, 2, 4, dp_size], jnp.int32)
    place = (device // divisors) % sizes
    scalars = (place, group_sizes, group_section, last_valid)

    own_weights = (query_weight.T, key_weight.T, value_weight.T, out_weight)
    wide_weights = jnp.stack([weight.astype(F32) for weight in own_weights])
    far = fetch_far(wide_weights)
    partner = swap_core(wide_weights)
    places, far = [piece[:2] for piece in far], [piece[2] for piece in far]
    far_partner = [swap_core(piece) for piece in far]
    vectors = pack_vectors(
        place,
        (out_bias, gain_one, shift_one, outer_bias, gain_two, shift_two),
        query_bias,
        value_bias,
        inner_bias,
    )
    row = jnp.arange(VECTOR_ROWS)[:, None]
    split_rows = (row == QUERY_BIAS) | (row == VALUE_BIAS)
    for swap in (swap_core, swap_side):
        vectors = vectors + jnp.where(split_rows, swap(vectors), 0.0)
    token_rows = tokens.reshape(SEGS, SEG_LEN, width)

    weights, keys, values, own_query, *saved = memory_forward(
        places,
        scalars,
        token_rows,
        memory,
        own_weights,
        partner,
        far,
        far_partner,
        vectors,
        inner_weight,
        outer_weight,
    )
    context, probs = attend(scalars, own_query, keys, values)
    (
        layer_out,
        out_rows,
        d_hidden,
        d_hidden_low,
        d_context,
        sums,
        own_inner,
        own_outer,
        other_inner,
        other_outer,
    ) = feed(
        scalars,
        token_rows,
        context,
        cotangent.reshape(SEGS, SEG_LEN, width),
        weights,
        inner_weight,
        outer_weight,
        vectors,
    )

    piece = ff // dp_size
    back = partial(attend_back, place, own_query, keys, values, d_context, probs)
    held = back(CHAINED, SEGS - CHAINED)
    fast_path = dp_size == BLOCKS
    run = on_block if fast_path else on_any
    results = run(
        place,
        scalars,
        back,
        held,
        (own_inner, own_outer, other_inner, other_outer),
        partial(query_grads, place, token_rows, d_hidden),
        (context, d_hidden_low, weights, sums),
        partial(
            memory_backward,
            place,
            weights=weights,
            keys=keys,
            values=values,
            saved=saved[:9],
            vectors=vectors,
            inner_weight=inner_weight,
            outer_weight=outer_weight,
            packed=fast_path,
        ),
        partial(input_grads, place, token_rows, weights=weights),
        saved,
        out_rows,
    )
    grads, smalls, grad_inner, grad_outer, grad_tokens, others = results
    grad_query, grad_out, grad_key, grad_value = grads
    grad_memory, *grad_vectors, grad_qb, grad_vb, inner_bias_grad = smalls

    def both_cores(value, other):
        start = (1 - core) * HALF_ROWS
        value = lax.dynamic_update_slice_in_dim(value, other, start, 1)
        return value.reshape(SEGS * SEG_LEN, width)

    return (
        both_cores(layer_out, others[0]),
        both_cores(grad_tokens, others[1]),
        grad_memory,
        grad_query.T,
        grad_qb,
        grad_key.T,
        grad_value.T,
        grad_vb,
        grad_out,
        *grad_vectors[:3],
        grad_inner,
        inner_bias_grad,
        grad_outer,
        *grad_vectors[3:],
    )


def at_bits(value, bits):
    axis = 0
    for bit in bits:
        if bit is None:
            axis += 1
        else:
            value = lax.dynamic_index_in_dim(value, bit, axis, False)
    return value


def on_block(
    place, scalars, back, held, ffn, query_part, query_args, backward, input_part, saved, out_rows
):
    index = lax.axis_index("dp")
    fast, slow = index & 1, (index >> 1) & 1
    own_inner, own_outer, other_inner, other_outer = ffn
    early = saved[9:]
    early = early[:1] + [swap_dp(share, bits) for bits, share in enumerate(early) if bits]
    ffn = in_step(
        own_inner, own_outer, swap_core(other_inner), swap_core(other_outer), *early, *held
    )
    ffn, early, held = ffn[:4], ffn[4:8], ffn[8:]
    own_inner, own_outer, other_inner, other_outer = (
        value.reshape((2, 2, 2) + value.shape[1:]) for value in ffn
    )
    inner, outer = (own_inner, other_inner), (own_outer, other_outer)

    def total(terms, bits):
        terms = [at_bits(term, bits) for term in terms]
        return sum(terms[1:], terms[0])

    inner_moved = swap_dp(total(inner, (None, 1 - slow, None)), 2)
    outer_moved = swap_dp(total(outer, (None, None, 1 - fast)), 1)
    d_query, kv_own, kv_other, kv_mem = back(0, CHAINED, held)
    d_part, query_own, query_other, sums = query_part(d_query, *query_args)
    weights = query_args[2]
    values = in_step(
        inner_moved,
        outer_moved,
        d_part,
        query_own,
        query_other,
        sums,
        kv_own,
        kv_other,
        kv_mem,
        swap_core(kv_mem),
    )
    inner_moved, outer_moved, d_part, query_own, query_other, sums, kv_own, kv_other = values[:8]
    kv_mem = values[8:]

    def second(terms, moved, bits, axis, bit):
        def half(at):
            here = [at if place == axis else value for place, value in enumerate(bits)]
            rest = [None if value is None or place != axis else at for place, value in enumerate(here)]
            del rest[[i for i, value in enumerate(bits) if value is not None][0]]
            return total(terms, here) + at_bits(moved, rest)

        return half(bit), half(1 - bit)

    inner_kept, inner_sent = second(inner, inner_moved, (None, slow, None), 2, fast)
    outer_kept, outer_sent = second(outer, outer_moved, (None, None, fast), 1, slow)
    inner_moved, outer_moved = swap_dp(inner_sent, 1), swap_dp(outer_sent, 2)
    kv_other = swap_core(kv_other)
    query_other = swap_core(query_other)
    kv_more, query_mem, dense_mem, *late = backward(kv_mem)

    def cube(*arrays):
        return [value.reshape((2, 2, 2) + value.shape[1:]) for value in arrays]

    q_kept, q_sent = split(place, (0, 2, cube(query_own, query_other, query_mem)), limit=60)
    values = in_step(
        inner_kept,
        inner_moved,
        outer_kept,
        outer_moved,
        kv_other,
        kv_more,
        q_kept,
        q_sent,
        dense_mem,
        *late,
    )
    inner_kept, inner_moved, outer_kept, outer_moved, kv_other, kv_more = values[:6]
    q_kept, q_sent, dense_mem, *late = values[6:]
    q_moved = swap_dp(q_sent, 1)
    late = late[:1] + [swap_dp(share, bits) for bits, share in enumerate(late) if bits]
    grad_tokens, token_rows, dense_own, dense_other = input_part(
        d_part, kv_own, kv_other, kv_more, sums=sums
    )
    q_moved, *late, dense_own, dense_other = in_step(q_moved, *late, dense_own, dense_other)

    ffn_kept, ffn_sent = memory_shares(place, early, late, inner_kept, inner_moved, outer_kept, outer_moved)
    ffn_kept, ffn_sent, dense_own, dense_other = in_step(
        ffn_kept, ffn_sent, dense_own, swap_core(dense_other)
    )
    ffn_moved = swap_dp(ffn_sent, 4)
    q_kept, q_sent = split(place, (1, 1, [q_kept, q_moved]))
    q_moved = swap_dp(q_sent, 2)
    d_kept, d_sent = split(place, (0, 2, cube(dense_own, dense_other, dense_mem)), limit=60)
    d_moved = swap_dp(d_sent, 1)
    q_part, _, d_kept, d_sent = split(
        place, (None, 0, [q_kept, q_moved]), (1, 1, [d_kept, d_moved])
    )
    q_moved, d_moved = swap_dp(q_part, 4), swap_dp(d_sent, 2)
    d_part, _, ffn_mine, _ = split(
        place, (None, 0, [d_kept, d_moved]), (None, 0, [ffn_kept, ffn_moved])
    )
    d_moved = swap_dp(d_part, 4)
    ffn_far = swap_side(ffn_mine)
    q_mine, _ = split(place, (None, 0, [q_part, q_moved]))
    (q_mine,) = join(place, (1, 1, q_mine, swap_dp(q_mine, 2)))
    d_mine, _ = split(place, (None, 0, [d_part, d_moved]), after=(q_mine,))
    q_moved = swap_dp(q_mine, 1)
    (d_mine,) = join(place, (1, 1, d_mine, swap_dp(d_mine, 2)), after=(q_moved,))
    pieces = (ffn_mine, swap_core(ffn_mine), ffn_far, swap_core(ffn_far))
    grad_inner, grad_outer = feed_final(place, pieces)
    halves = (q_mine, q_moved, d_mine, swap_dp(d_mine, 1))
    grads = final(place, halves, grad_inner.shape[1])
    others = (swap_core(out_rows), swap_core(token_rows))
    return grads[:4], grads[4:], grad_inner, grad_outer, grad_tokens, others


def on_any(
    place, scalars, back, held, ffn, query_part, query_args, backward, input_part, saved, out_rows
):
    own_inner, own_outer, other_inner, other_outer = ffn
    dp_size = lax.axis_size("dp")
    quarter = own_inner.shape[1]
    width = 4 * quarter
    head_index = lax.axis_index("head")
    d_query, kv_own, kv_other, kv_mem = back(0, CHAINED, held)
    d_part, query_own, query_other, sums = query_part(d_query, *query_args)
    kv_mem = (kv_mem, swap_core(kv_mem))
    kv_more, query_mem, dense_mem, mem_d_inner, mem_d_total = backward(kv_mem)
    grad_tokens, token_rows, dense_own, dense_other = input_part(
        d_part, kv_own, swap_core(kv_other), kv_more, sums=sums
    )
    query = query_own + swap_core(query_other) + query_mem
    dense = dense_own + swap_core(dense_other) + dense_mem
    query, dense = lax.psum((query, dense), "dp")
    mem_active, mem_normed = saved[7], saved[8]

    def whole(own, other, rows, hidden):
        rows = lax.dynamic_slice_in_dim(rows, head_index * quarter, quarter, 2)
        rows = rows.reshape(-1, quarter)
        value = own + swap_core(other)
        value = value.transpose(1, 0, 2).reshape(quarter, -1)
        value = value + tn(rows, hidden.reshape(rows.shape[0], -1))
        value = lax.psum_scatter(value, "dp", scatter_dimension=1, tiled=True)
        return lax.all_gather(value, "head").reshape(width, -1)

    grad_inner = whole(own_inner, other_inner, mem_normed, mem_d_inner)
    grad_outer = whole(own_outer, other_outer, mem_d_total, mem_active).T
    rows = quarter // BLOCKS

    def part(value, index):
        return value[:, rows * index : rows * (index + 1)].reshape(quarter, width)

    sums = dense[:, 2 * rows : 2 * rows + SUM_PART].reshape(SUM_ROWS, width)
    piece = grad_inner.shape[1]
    at = lax.axis_index("dp") * piece
    smalls = (
        sums[MEMORY_SUM : MEMORY_SUM + MEM],
        *sums[:6],
        lax.dynamic_slice_in_dim(sums[QUERY_SUM], head_index * quarter, quarter, 0),
        lax.dynamic_slice_in_dim(sums[VALUE_SUM], head_index * quarter, quarter, 0),
        lax.dynamic_slice_in_dim(sums[6:QUERY_SUM].reshape(-1), at, piece, 0),
    )
    grads = (part(query, 0), part(query, 1), part(dense, 0), part(dense, 1))
    others = (swap_core(out_rows), swap_core(token_rows))
    return grads, smalls, grad_inner, grad_outer, grad_tokens, others


def solution(mesh):
    row, col, vec, every = P("dp", None), P(None, "head"), P("head"), P()
    placed = (row, row, every, col, vec, col, col, vec, P("head", None)) + (every,) * 11
    return jax.shard_map(
        on_device,
        mesh=mesh,
        in_specs=placed + (P("dp"),),
        out_specs=(
            row,
            row,
            every,
            col,
            vec,
            col,
            col,
            vec,
            P("head", None),
            every,
            every,
            every,
            P(None, "dp"),
            P("dp"),
            row,
            every,
            every,
            every,
        ),
        check_vma=False,
    )
```

```python
from functools import partial

import jax
import jax.numpy as jnp
from jax import lax
from jax.experimental import pallas as pl
from jax.experimental.pallas import tpu as pltpu
from jax.sharding import PartitionSpec as P

HEAD_DIM = 64
MEM = 10
MEM_PAD = 16
SEG_LEN = 512
SEGS = 3
CHAINED = SEGS - 1
KEYS = SEG_LEN + MEM_PAD
HALF_ROWS = SEG_LEN // 2
EPS = 1e-06
SCALE = HEAD_DIM ** (-0.5)
MASKED = -1000000000.0
LN_TWO = 0.6931471805599453

F32 = jnp.float32
BF16 = jnp.bfloat16


def nn(left, right):
    return jnp.dot(left, right, preferred_element_type=F32)


def nt(left, right):
    return lax.dot_general(left, right, (((1,), (1,)), ((), ())), preferred_element_type=F32)


def tn(left, right):
    return lax.dot_general(left, right, (((0,), (0,)), ((), ())), preferred_element_type=F32)


def norm_fwd(value, gain, shift):
    centered = value - jnp.mean(value, axis=-1, keepdims=True)
    spread = jnp.mean(centered * centered, axis=-1, keepdims=True)
    root = lax.rsqrt(spread + EPS)
    unit = centered * root
    return unit * gain + shift, unit, root


def norm_bwd(d_out, unit, root, gain):
    d_unit = d_out * gain
    mean_one = jnp.mean(d_unit, axis=-1, keepdims=True)
    mean_two = jnp.mean(d_unit * unit, axis=-1, keepdims=True)
    return root * (d_unit - mean_one - unit * mean_two)


def gelu_parts(inner):
    cdf = 0.5 * (1.0 + lax.erf(inner * 0.7071067811865476))
    pdf = jnp.exp(-0.5 * inner * inner) * 0.3989422804014327
    return inner * cdf, cdf + inner * pdf


def column_sum(value):
    return jnp.sum(value, axis=0, keepdims=True)


SHARE_SPACE = 256

SIDE, CORE, PART, CHAIN = range(4)


def limit_of(segment, place_ref, sizes_ref, sections_ref, last_ref):
    chain = place_ref[CHAIN]
    end, section = 0, 0
    for group in range(sizes_ref.shape[0]):
        start, end = end, end + sizes_ref[group]
        inside = jnp.logical_and(start <= chain, chain < end)
        section = jnp.where(inside, sections_ref[group], section)
    last = section % (SEGS - 1) + 1
    return jnp.where(segment < last, SEG_LEN, jnp.where(segment == last, last_ref[0], 0))


def key_bias(limit):
    row = lax.broadcasted_iota(jnp.int32, (KEYS, 1), 0)
    beyond = jnp.where((row >= SEG_LEN) & (row < SEG_LEN + MEM), LN_TWO, MASKED)
    return jnp.where(row < limit, 0.0, beyond)


OUT_BIAS, GAIN_ONE, SHIFT_ONE, OUTER_BIAS, GAIN_TWO, SHIFT_TWO, QUERY_BIAS, VALUE_BIAS = range(8)
INNER_BIAS = 8
VECTOR_ROWS = 16


def row_of(vectors, index):
    return vectors[index : index + 1]


def head_mask(width):
    count = width // HEAD_DIM
    shape = (count, MEM_PAD, width)
    head = lax.broadcasted_iota(jnp.int32, shape, 0)
    lane = lax.broadcasted_iota(jnp.int32, shape, 2) // HEAD_DIM
    return (head == lane).astype(F32)


def spread_heads(value, mask):
    count, rows, width = mask.shape
    return (value.astype(F32)[None] * mask).reshape(count * rows, width).astype(BF16)


def gather_heads(value, mask):
    return jnp.sum(value.reshape(mask.shape) * mask, axis=0)


def pack_vectors_kernel(place_ref, *refs):
    *vector_refs, query_ref, value_ref, inner_ref, out_ref = refs
    width = out_ref.shape[1]
    quarter = query_ref.shape[0]
    out_ref[...] = jnp.zeros_like(out_ref)
    for index, ref in enumerate(vector_refs):
        out_ref[index : index + 1] = ref[...].reshape(1, width)
    index = 2 * place_ref[SIDE] + place_ref[CORE]
    for row, ref in ((QUERY_BIAS, query_ref), (VALUE_BIAS, value_ref)):
        piece = ref[...].reshape(1, quarter)
        for at in range(4):
            columns = slice(quarter * at, quarter * (at + 1))
            out_ref[row : row + 1, columns] = jnp.where(index == at, piece, 0.0)
    for at in range(inner_ref.shape[0] // width):
        piece = inner_ref[width * at : width * (at + 1)].reshape(1, width)
        out_ref[INNER_BIAS + at : INNER_BIAS + at + 1] = piece


def pack_vectors(place, vectors, query_bias, value_bias, inner_bias):
    width = vectors[0].shape[0]
    vmem = pl.BlockSpec(memory_space=pltpu.VMEM)
    return pl.pallas_call(
        pack_vectors_kernel,
        in_specs=[pl.BlockSpec(memory_space=pltpu.SMEM)] + [vmem] * (len(vectors) + 3),
        out_specs=vmem,
        out_shape=jax.ShapeDtypeStruct((VECTOR_ROWS, width), F32),
        name="pack_vectors",
    )(place, *vectors, query_bias, value_bias, inner_bias)


def share_out(place_ref, refs, hidden_ref, wide_ref):
    at_fast, at_slow = place_ref[PART] % 2, place_ref[PART] // 2
    index = 2 * place_ref[SIDE] + place_ref[CORE]
    width = wide_ref.shape[2]
    half, quarter = width // 2, width // 4
    for bits, ref in enumerate(refs):
        base = 2 * (at_slow ^ (bits // 2)) + (at_fast ^ (bits % 2))
        for segment in range(CHAINED):
            rows = slice(MEM_PAD * segment, MEM_PAD * (segment + 1))
            for far in range(2):
                columns = pl.ds(pl.multiple_of((4 * far + base) * half, half), half)
                ref[rows, far * half : (far + 1) * half] = hidden_ref[segment, :, columns].astype(F32)
            wide = wide_ref[segment]
            piece = wide[:, :quarter]
            for other in range(1, 4):
                piece = jnp.where(
                    index == other, wide[:, quarter * other : quarter * (other + 1)], piece
                )
            ref[rows, width : width + quarter] = piece.astype(F32)
            gap = jnp.zeros((MEM_PAD, SHARE_SPACE - quarter), F32)
            ref[rows, width + quarter :] = gap


def memory_forward_kernel(
    places,
    place_ref,
    sizes_ref,
    sections_ref,
    last_ref,
    tokens_ref,
    memory_ref,
    own_q_ref,
    own_k_ref,
    own_v_ref,
    own_o_ref,
    partner_ref,
    vectors_ref,
    *refs,
):
    far_refs, far_partner_refs, refs = (
        refs[: len(places)],
        refs[len(places) : 2 * len(places)],
        refs[2 * len(places) :],
    )
    inner_hbm, outer_hbm, weights_hbm, keys_hbm, values_hbm, query_hbm, *refs = refs
    saved_hbm, (weights_ref, keys_ref, values_ref, query_ref) = refs[:13], refs[13:17]
    saved, (inner_ref, outer_ref, sems) = refs[17:30], refs[30:]
    (
        low_ref,
        mem_query_ref,
        mem_context_ref,
        mem_probs_ref,
        mem_hidden_ref,
        mem_total_ref,
        mem_slope_ref,
        mem_active_ref,
        mem_normed_ref,
        *share_refs,
    ) = saved
    copies = [
        pltpu.make_async_copy(inner_hbm, inner_ref, sems.at[0]),
        pltpu.make_async_copy(outer_hbm, outer_ref, sems.at[1]),
    ]
    for copy in copies:
        copy.start()
    side, core, part = place_ref[SIDE], place_ref[CORE], place_ref[PART]
    quarter = own_q_ref.shape[0]
    width = memory_ref.shape[1]

    def span_of(at_side, at_core, start=0, rows=quarter):
        start = (2 * at_side + at_core) * quarter + start
        return pl.ds(pl.multiple_of(start, 16), rows)

    for which, ref in enumerate((own_q_ref, own_k_ref, own_v_ref, own_o_ref)):
        weights_ref[which, span_of(side, core)] = ref[...]
        weights_ref[which, span_of(side, 1 - core)] = partner_ref[which].astype(BF16)
    for (bits, start), near_ref, other_ref in zip(places, far_refs, far_partner_refs):
        which, rows = part ^ bits, near_ref.shape[0]
        weights_ref[which, span_of(1 - side, core, start, rows)] = near_ref[...].astype(BF16)
        weights_ref[which, span_of(1 - side, 1 - core, start, rows)] = other_ref[...].astype(BF16)
    writes = [pltpu.make_async_copy(weights_ref, weights_hbm, sems.at[2])]
    writes[0].start()
    vectors = vectors_ref[...]
    query_bias = row_of(vectors, QUERY_BIAS)
    value_bias = row_of(vectors, VALUE_BIAS)

    def project(index, carry):
        segment, half = index // 2, index % 2
        span = pl.ds(half * HALF_ROWS, HALF_ROWS)
        rows = tokens_ref[segment, span]
        keys_ref[segment, span] = nt(rows, weights_ref[1]).astype(BF16)
        values_ref[segment, span] = (nt(rows, weights_ref[2]) + value_bias).astype(BF16)

        @pl.when(half == core)
        def _():
            query_ref[segment] = (nt(rows, weights_ref[0]) + query_bias).astype(BF16) * SCALE

        return carry

    lax.fori_loop(0, 2 * SEGS, project, 0)
    token_rows, mem_rows = pl.ds(0, SEG_LEN), pl.ds(SEG_LEN, MEM_PAD)
    pairs = ((keys_ref, keys_hbm), (values_ref, values_hbm))
    writes.append(pltpu.make_async_copy(query_ref, query_hbm, sems.at[3]))
    for index, (ref, hbm) in enumerate(pairs):
        writes.append(
            pltpu.make_async_copy(ref.at[:, token_rows], hbm.at[:, token_rows], sems.at[4 + index])
        )
    for write in writes[1:]:
        write.start()

    mask = head_mask(width)
    now = memory_ref[...]
    for segment in range(SEGS):
        low = now.astype(BF16)
        low_ref[segment] = low
        keys_ref[segment, SEG_LEN:] = nt(low, weights_ref[1]).astype(BF16)
        values_ref[segment, SEG_LEN:] = (nt(low, weights_ref[2]) + value_bias).astype(BF16)
        if segment == CHAINED:
            break
        query = (nt(low, weights_ref[0]) + query_bias).astype(BF16) * SCALE
        mem_query_ref[segment] = query
        scores = nt(keys_ref[segment], spread_heads(query, mask))
        limit = limit_of(segment, place_ref, sizes_ref, sections_ref, last_ref)
        scores = scores + key_bias(limit)
        weights = jnp.exp(scores - jnp.max(scores, axis=0, keepdims=True))
        probs = weights * (1.0 / jnp.sum(weights, axis=0, keepdims=True))
        mem_probs_ref[segment] = probs
        context = gather_heads(tn(probs.astype(BF16), values_ref[segment]), mask).astype(BF16)
        mem_context_ref[segment] = context
        hidden = now + nn(context, weights_ref[3]) + row_of(vectors, OUT_BIAS)
        mem_hidden_ref[segment] = hidden
        normed, _, _ = norm_fwd(hidden, row_of(vectors, GAIN_ONE), row_of(vectors, SHIFT_ONE))
        mem_normed_ref[segment] = normed.astype(BF16)
        if segment == 0:
            copies[0].wait()
        inner_bias = [row_of(vectors, INNER_BIAS + i) for i in range(inner_ref.shape[1] // width)]
        inner_bias = jnp.concatenate(inner_bias, 1)
        active, slope = gelu_parts(nn(normed.astype(BF16), inner_ref[...]) + inner_bias)
        active = active.astype(BF16)
        mem_slope_ref[segment] = slope
        mem_active_ref[segment] = active
        if segment == 0:
            copies[1].wait()
        total = normed + nn(active, outer_ref[...]) + row_of(vectors, OUTER_BIAS)
        mem_total_ref[segment] = total
        now, _, _ = norm_fwd(total, row_of(vectors, GAIN_TWO), row_of(vectors, SHIFT_TWO))
    for index, (ref, hbm) in enumerate(pairs):
        writes.append(
            pltpu.make_async_copy(ref.at[:, mem_rows], hbm.at[:, mem_rows], sems.at[6 + index])
        )
        writes[-1].start()
    share_out(place_ref, share_refs, mem_active_ref, mem_normed_ref)
    for index, (ref, hbm) in enumerate(zip(saved, saved_hbm)):
        writes.append(pltpu.make_async_copy(ref, hbm, sems.at[8 + index]))
        writes[-1].start()
    for write in writes:
        write.wait()


def memory_forward(
    places, scalars, tokens, memory, own, partner, far, far_partner, vectors, inner_weight, outer_weight
):
    width = memory.shape[1]
    ff = inner_weight.shape[1]
    head_rows = MEM_PAD * width // HEAD_DIM
    vmem = pl.BlockSpec(memory_space=pltpu.VMEM)

    def like(shape, dtype):
        return jax.ShapeDtypeStruct(shape, dtype)

    saved = [
        ((SEGS, MEM_PAD, width), BF16),
        ((CHAINED, MEM_PAD, width), BF16),
        ((CHAINED, MEM_PAD, width), BF16),
        ((CHAINED, KEYS, head_rows), F32),
        ((CHAINED, MEM_PAD, width), F32),
        ((CHAINED, MEM_PAD, width), F32),
        ((CHAINED, MEM_PAD, ff), F32),
        ((CHAINED, MEM_PAD, ff), BF16),
        ((CHAINED, MEM_PAD, width), BF16),
    ] + [((CHAINED * MEM_PAD, width + SHARE_SPACE), F32)] * 4
    large = [
        ((4, width, width), BF16),
        ((SEGS, KEYS, width), BF16),
        ((SEGS, KEYS, width), BF16),
        ((SEGS, HALF_ROWS, width), BF16),
    ]
    return pl.pallas_call(
        partial(memory_forward_kernel, places),
        in_specs=[pl.BlockSpec(memory_space=pltpu.SMEM)] * 4
        + [vmem] * (8 + 2 * len(places))
        + [pl.BlockSpec(memory_space=pl.ANY)] * 2,
        out_specs=[pl.BlockSpec(memory_space=pltpu.HBM)] * 17,
        out_shape=[pltpu.HBM(*shape) for shape in large + saved],
        scratch_shapes=[pltpu.VMEM(*shape) for shape in large + saved]
        + [
            pltpu.VMEM((width, ff), BF16),
            pltpu.VMEM((ff, width), BF16),
            pltpu.SemaphoreType.DMA((21,)),
        ],
        compiler_params=pltpu.CompilerParams(vmem_limit_bytes=60 << 20),
        cost_estimate=pl.CostEstimate(flops=1000, bytes_accessed=1000, transcendentals=0),
        name="memory_forward",
    )(
        *scalars,
        tokens,
        memory,
        *own,
        partner,
        vectors,
        *far,
        *far_partner,
        inner_weight,
        outer_weight,
    )


def lane_masks(rows):
    lane = lax.broadcasted_iota(jnp.int32, (rows, 2 * HEAD_DIM), 1)
    first = (lane < HEAD_DIM).astype(F32)
    return first.astype(BF16), (1.0 - first).astype(BF16)


def pair_of(head):
    start = 2 * HEAD_DIM * (head // 2)
    return slice(start, start + 2 * HEAD_DIM)


def attend_kernel(
    place_ref, sizes_ref, sections_ref, last_ref, q_ref, k_ref, v_ref, out_ref, probs_ref
):
    limit = limit_of(pl.program_id(0), place_ref, sizes_ref, sections_ref, last_ref)
    bias = key_bias(limit)
    count = q_ref.shape[2] // HEAD_DIM
    q_masks, k_masks = lane_masks(q_ref.shape[1]), lane_masks(KEYS)

    def score(head):
        cols = pair_of(head)
        return nt(k_ref[0, :, cols], q_ref[0, :, cols] * q_masks[head % 2])

    def finish(head, probs, held):
        cols = pair_of(head)
        part = tn(probs, v_ref[0, :, cols] * k_masks[head % 2])
        if head % 2 == 0:
            return part
        out_ref[0, :, cols] = (held + part).astype(BF16)
        return None

    held = before = None
    later = score(0)
    for head in range(count):
        scores = later + bias
        if head + 1 < count:
            later = score(head + 1)
        if before is not None:
            held = finish(head - 1, before, held)
        weights = jnp.exp(scores - jnp.max(scores, axis=0, keepdims=True))
        before = (weights * (1.0 / jnp.sum(weights, axis=0, keepdims=True))).astype(BF16)
        probs_ref[0, head] = before
    finish(count - 1, before, held)


def attend(scalars, query, keys, values):
    segs, rows, width = query.shape
    wide = width // 2

    def block(length):
        return pl.BlockSpec((1, length, wide), lambda s, h, *_: (s, 0, h))

    return pl.pallas_call(
        attend_kernel,
        grid_spec=pltpu.PrefetchScalarGridSpec(
            num_scalar_prefetch=4,
            grid=(segs, 2),
            in_specs=[block(rows), block(KEYS), block(KEYS)],
            out_specs=[
                block(rows),
                pl.BlockSpec((1, wide // HEAD_DIM, KEYS, rows), lambda s, h, *_: (s, h, 0, 0)),
            ],
        ),
        out_shape=[
            jax.ShapeDtypeStruct(query.shape, BF16),
            jax.ShapeDtypeStruct((segs, width // HEAD_DIM, KEYS, rows), BF16),
        ],
        compiler_params=pltpu.CompilerParams(vmem_limit_bytes=60 << 20),
        cost_estimate=pl.CostEstimate(flops=1000, bytes_accessed=1000, transcendentals=0),
        name="attend",
    )(*scalars, query, keys, values)


def in_step_kernel(*refs):
    pass


def in_step(*values):
    anywhere = [pl.BlockSpec(memory_space=pl.ANY)] * len(values)
    return pl.pallas_call(
        in_step_kernel,
        in_specs=anywhere,
        out_specs=anywhere,
        out_shape=[jax.ShapeDtypeStruct(value.shape, value.dtype) for value in values],
        input_output_aliases={i: i for i in range(len(values))},
        name="in_step",
    )(*values)


def attend_back_kernel(through, place_ref, q_ref, k_ref, v_ref, d_ref, p_ref, *refs):
    dq_ref, own_ref, other_ref, mem_ref = refs[through:][:4]
    first_core = place_ref[CORE] == 0
    count = q_ref.shape[2] // HEAD_DIM
    q_masks, k_masks = lane_masks(q_ref.shape[1]), lane_masks(KEYS)

    def first(head):
        cols = pair_of(head)
        return nt(v_ref[0, :, cols], d_ref[0, :, cols] * q_masks[head % 2])

    def last(head, d_scores, held):
        cols, mask = pair_of(head), q_masks[head % 2]
        dv = nn(p_ref[0, head], d_ref[0, :, cols] * mask)
        dk = nn(d_scores, q_ref[0, :, cols] * mask)
        dq = tn(d_scores, k_ref[0, :, cols] * k_masks[head % 2])
        if head % 2 == 0:
            return dv, dk, dq
        for index, value in enumerate((held[1] + dk, held[0] + dv)):
            low, high = value[:HALF_ROWS], value[HALF_ROWS:SEG_LEN]
            own_ref[index, 0, :, cols] = jnp.where(first_core, low, high)
            other_ref[index, 0, :, cols] = jnp.where(first_core, high, low)
            mem_ref[index, 0, :, cols] = value[SEG_LEN:]
        dq_ref[0, :, cols] = ((held[2] + dq) * SCALE).astype(BF16)
        return None

    held = before = None
    later = first(0)
    for head in range(count):
        d_probs = later
        if head + 1 < count:
            later = first(head + 1)
        if before is not None:
            held = last(head - 1, before, held)
        probs = p_ref[0, head].astype(F32)
        delta = jnp.sum(probs * d_probs, axis=0, keepdims=True)
        before = (probs * (d_probs - delta)).astype(BF16)
    last(count - 1, before, held)


def attend_back(place, query, keys, values, d_context, probs, first, count, held=(), through=()):
    segs, rows, width = query.shape
    wide = width // 2

    def block(length):
        return pl.BlockSpec((1, length, wide), lambda s, h, place: (first + s, 0, h))

    def two(length):
        return pl.BlockSpec((2, 1, length, wide), lambda s, h, place: (0, first + s, 0, h))

    inputs = (query, keys, values, d_context, probs)
    at = 1 + len(inputs)
    aliases = {at + i: i for i in range(len(held))}
    aliases.update({at + len(held) + i: 4 + i for i in range(len(through))})
    return pl.pallas_call(
        partial(attend_back_kernel, len(held) + len(through)),
        grid_spec=pltpu.PrefetchScalarGridSpec(
            num_scalar_prefetch=1,
            grid=(count, 2),
            in_specs=[
                block(rows),
                block(KEYS),
                block(KEYS),
                block(rows),
                pl.BlockSpec(
                    (1, wide // HEAD_DIM, KEYS, rows),
                    lambda s, h, place: (first + s, h, 0, 0),
                ),
            ]
            + [pl.BlockSpec(memory_space=pl.ANY)] * (len(held) + len(through)),
            out_specs=[block(rows), two(HALF_ROWS), two(HALF_ROWS), two(MEM_PAD)]
            + [pl.BlockSpec(memory_space=pl.ANY)] * len(through),
        ),
        out_shape=[
            jax.ShapeDtypeStruct(query.shape, BF16),
            jax.ShapeDtypeStruct((2, segs, HALF_ROWS, width), F32),
            jax.ShapeDtypeStruct((2, segs, HALF_ROWS, width), F32),
            jax.ShapeDtypeStruct((2, segs, MEM_PAD, width), F32),
        ]
        + [jax.ShapeDtypeStruct(value.shape, value.dtype) for value in through],
        input_output_aliases=aliases,
        compiler_params=pltpu.CompilerParams(vmem_limit_bytes=60 << 20),
        cost_estimate=pl.CostEstimate(flops=1000, bytes_accessed=1000, transcendentals=0),
        name="attend_back",
    )(place, *inputs, *held, *through)


SUM_ROWS = 24
QUERY_SUM = 10
VALUE_SUM = 11
MEMORY_SUM = 12


def feed_kernel(
    place_ref,
    sizes_ref,
    sections_ref,
    last_ref,
    rows_ref,
    context_ref,
    cot_ref,
    out_weight_ref,
    inner_ref,
    outer_ref,
    vectors_ref,
    out_ref,
    out_rows_ref,
    d_hidden_ref,
    d_hidden_low_ref,
    d_context_ref,
    sums_ref,
    own_inner_hbm,
    own_outer_hbm,
    other_inner_hbm,
    other_outer_hbm,
    slope_ref,
    active_ref,
    grads_ref,
    sems,
):
    segment = pl.program_id(0)
    side, core = place_ref[SIDE], place_ref[CORE]
    vectors = vectors_ref[...]
    gain_one, gain_two = row_of(vectors, GAIN_ONE), row_of(vectors, GAIN_TWO)
    width = vectors.shape[1]
    half = width // 2
    quarter = width // 4
    chunks = [slice(at, at + width) for at in range(0, inner_ref.shape[1], width)]
    row = lax.broadcasted_iota(jnp.int32, (HALF_ROWS, 1), 0) + core * HALF_ROWS
    valid = row < limit_of(segment, place_ref, sizes_ref, sections_ref, last_ref)

    def of_side(value):
        return jnp.where(side == 0, value[:, :half], value[:, half:])

    def add_grads(which, index, value):
        for row_half in range(2):
            rows = value[quarter * row_half : quarter * (row_half + 1)]
            for part in range(2):
                at = 2 * index + part
                held = jnp.where(segment == 0, 0.0, grads_ref[which, row_half, at])
                grads_ref[which, row_half, at] = held + rows[:, half * part : half * (part + 1)]

    hidden = (
        rows_ref[0].astype(F32)
        + nn(context_ref[0], out_weight_ref[0])
        + row_of(vectors, OUT_BIAS)
    )
    normed, unit_one, root_one = norm_fwd(hidden, gain_one, row_of(vectors, SHIFT_ONE))
    normed_low = normed.astype(BF16)
    total = normed + row_of(vectors, OUTER_BIAS)
    for index, chunk in enumerate(chunks):
        inner = nn(normed_low, inner_ref[:, chunk]) + row_of(vectors, INNER_BIAS + index)
        active, slope = gelu_parts(inner)
        active = active.astype(BF16)
        active_ref[:, chunk] = active
        slope_ref[:, chunk] = slope
        total = total + nn(active, outer_ref[chunk])
    result, unit_two, root_two = norm_fwd(total, gain_two, row_of(vectors, SHIFT_TWO))
    result = jnp.where(valid, result, 0.0)
    out_ref[0] = result
    out_rows_ref[0] = result

    d_result = jnp.where(valid, cot_ref[0].astype(F32), 0.0)
    d_total = norm_bwd(d_result, unit_two, root_two, gain_two)
    d_total_low = d_total.astype(BF16)
    normed_half, d_total_half = of_side(normed_low), of_side(d_total_low)
    d_normed = d_total
    inner_sums = []
    for index, chunk in enumerate(chunks):
        d_inner = (nt(d_total_low, outer_ref[chunk]) * slope_ref[:, chunk]).astype(BF16)
        inner_sums.append(column_sum(d_inner.astype(F32)))
        d_normed = d_normed + nt(d_inner, inner_ref[:, chunk])
        add_grads(0, index, tn(normed_half, d_inner))
        add_grads(1, index, tn(d_total_half, active_ref[:, chunk]))
    final = segment == pl.num_programs(0) - 1
    targets = ((other_inner_hbm, own_inner_hbm), (other_outer_hbm, own_outer_hbm))
    copies = [
        pltpu.make_async_copy(
            grads_ref.at[which, core if own else 1 - core],
            targets[which][own],
            sems.at[which, own],
        )
        for own in range(2)
        for which in range(2)
    ]

    @pl.when(final)
    def _():
        for copy in copies:
            copy.start()

    d_hidden = norm_bwd(d_normed, unit_one, root_one, gain_one)
    d_hidden_ref[0] = d_hidden
    d_hidden_low = d_hidden.astype(BF16)
    d_hidden_low_ref[0] = d_hidden_low
    d_context_ref[0] = nt(d_hidden_low, out_weight_ref[0]).astype(BF16)
    sums = [
        column_sum(d_hidden),
        column_sum(d_normed * unit_one),
        column_sum(d_normed),
        column_sum(d_total),
        column_sum(d_result * unit_two),
        column_sum(d_result),
    ] + inner_sums
    sums = jnp.concatenate(sums + [jnp.zeros((SUM_ROWS - len(sums), width), F32)], 0)

    @pl.when(segment == 0)
    def _():
        sums_ref[...] = sums

    @pl.when(segment > 0)
    def _():
        sums_ref[...] += sums

    @pl.when(final)
    def _():
        for copy in copies:
            copy.wait()


def feed(scalars, tokens, context, cot, weights, inner_weight, outer_weight, vectors):
    width, ff = inner_weight.shape
    chunk = width // 2

    def own_half():
        return pl.BlockSpec((1, HALF_ROWS, width), lambda i, place, *_: (i, place[CORE], 0))

    def segment():
        return pl.BlockSpec((1, HALF_ROWS, width), lambda i, *_: (i, 0, 0))

    def fixed(shape, index=(0, 0)):
        return pl.BlockSpec(shape, lambda i, *_: index, pipeline_mode=pl.Buffered(1))

    like = pltpu.HBM
    per_segment = (SEGS, HALF_ROWS, width)
    grads_shape = (ff // chunk, width // 4, chunk)
    return pl.pallas_call(
        feed_kernel,
        grid_spec=pltpu.PrefetchScalarGridSpec(
            num_scalar_prefetch=4,
            grid=(SEGS,),
            in_specs=[
                own_half(),
                segment(),
                own_half(),
                fixed((1, width, width), (3, 0, 0)),
                fixed((width, ff)),
                fixed((ff, width)),
                fixed(vectors.shape),
            ],
            out_specs=[
                own_half(),
                segment(),
                segment(),
                segment(),
                segment(),
                pl.BlockSpec((SUM_ROWS, width), lambda i, *_: (0, 0)),
            ]
            + [pl.BlockSpec(memory_space=pl.ANY)] * 4,
            scratch_shapes=[
                pltpu.VMEM((HALF_ROWS, ff), F32),
                pltpu.VMEM((HALF_ROWS, ff), BF16),
                pltpu.VMEM((2, 2) + grads_shape, F32),
                pltpu.SemaphoreType.DMA((2, 2)),
            ],
        ),
        out_shape=[
            like((SEGS, SEG_LEN, width), F32),
            like(per_segment, F32),
            like(per_segment, F32),
            like(per_segment, BF16),
            like(per_segment, BF16),
            like((SUM_ROWS, width), F32),
        ]
        + [like(grads_shape, F32)] * 4,
        compiler_params=pltpu.CompilerParams(vmem_limit_bytes=60 << 20),
        cost_estimate=pl.CostEstimate(flops=1000, bytes_accessed=1000, transcendentals=0),
        name="feed",
    )(*scalars, tokens, context, cot, weights, inner_weight, outer_weight, vectors)


BLOCKS = 8
SUM_PART = SUM_ROWS // BLOCKS
SUM_SPACE = 8


def block_rows(width):
    rows = width // 4 // BLOCKS
    return 2 * rows, 2 * rows + SUM_SPACE


def to_blocks(ref, matrices, sums=None):
    rows = (ref.shape[1] - (0 if sums is None else SUM_SPACE)) // 2
    for block in range(BLOCKS):
        for index, matrix in enumerate(matrices):
            ref[block, rows * index : rows * (index + 1)] = matrix(rows * block, rows)
        if sums is not None:
            part = sums[SUM_PART * block : SUM_PART * (block + 1)]
            filler = jnp.zeros((SUM_SPACE - SUM_PART, part.shape[1]), F32)
            ref[block, 2 * rows :] = jnp.concatenate([part, filler], 0)


def memory_backward_kernel(
    packed,
    place_ref,
    kv_mem_ref,
    kv_mem_other_ref,
    low_ref,
    mem_query_ref,
    mem_context_ref,
    mem_probs_ref,
    mem_hidden_ref,
    mem_total_ref,
    mem_slope_ref,
    mem_active_ref,
    mem_normed_ref,
    vectors_ref,
    weights_hbm,
    keys_hbm,
    values_hbm,
    inner_hbm,
    outer_hbm,
    kv_rows_ref,
    query_dense_ref,
    dense_ref,
    *refs,
):
    share_refs, refs = refs[:-9], refs[-9:]
    weights_ref, keys_ref, values_ref, inner_ref, outer_ref, grad_ref, d_inner_ref, d_total_ref, sems = refs
    order = [(weights_hbm.at[at], weights_ref.at[at]) for at in (1, 2)]
    order += [(outer_hbm, outer_ref), (inner_hbm, inner_ref)]
    order += [(weights_hbm.at[3], weights_ref.at[3])]
    for segment in reversed(range(CHAINED)):
        order += [(values_hbm.at[segment], values_ref.at[segment])]
        order += [(keys_hbm.at[segment], keys_ref.at[segment])]
        if segment == CHAINED - 1:
            order += [(weights_hbm.at[0], weights_ref.at[0])]
    copies = [
        pltpu.make_async_copy(source, target, sems.at[index])
        for index, (source, target) in enumerate(order)
    ]
    for copy in copies:
        copy.start()
    arrived = iter(copies)

    def wait(count):
        for _ in range(count):
            next(arrived).wait()

    side, core = place_ref[0], place_ref[1]
    width = low_ref.shape[2]
    quarter = width // 4
    vectors = vectors_ref[...]
    gain_one, gain_two = row_of(vectors, GAIN_ONE), row_of(vectors, GAIN_TWO)
    mask = head_mask(width)
    own = pl.ds(core * HALF_ROWS, HALF_ROWS)
    d_memory = None
    sums = None
    queries, hiddens, key_rows, value_rows = [], [], [], []
    for segment in reversed(range(SEGS)):
        d_keys = kv_mem_ref[0, segment] + kv_mem_other_ref[0, segment]
        d_values = kv_mem_ref[1, segment] + kv_mem_other_ref[1, segment]
        if d_memory is None:
            d_next = None
        else:
            normed, unit_one, root_one = norm_fwd(
                mem_hidden_ref[segment], gain_one, row_of(vectors, SHIFT_ONE)
            )
            _, unit_two, root_two = norm_fwd(
                mem_total_ref[segment], gain_two, row_of(vectors, SHIFT_TWO)
            )
            d_total = norm_bwd(d_memory, unit_two, root_two, gain_two)
            d_total_low = d_total.astype(BF16)
            if segment == CHAINED - 1:
                wait(1)
            d_inner = (nt(d_total_low, outer_ref[...]) * mem_slope_ref[segment]).astype(BF16)
            if segment == CHAINED - 1:
                wait(1)
            d_normed = d_total + nt(d_inner, inner_ref[...])
            d_hidden = norm_bwd(d_normed, unit_one, root_one, gain_one)
            d_hidden_low = d_hidden.astype(BF16)
            if segment == CHAINED - 1:
                wait(1)
            d_context = spread_heads(nt(d_hidden_low, weights_ref[3]).astype(BF16), mask)
            query = spread_heads(mem_query_ref[segment], mask)
            probs = mem_probs_ref[segment]
            probs_low = probs.astype(BF16)
            wait(1)
            d_probs = nt(values_ref[segment], d_context)
            delta = jnp.sum(probs * d_probs, axis=0, keepdims=True)
            d_scores = (probs * (d_probs - delta)).astype(BF16)
            wait(1)
            d_query = gather_heads(tn(d_scores, keys_ref[segment]), mask) * SCALE
            d_query = d_query.astype(BF16)
            more_keys = nn(d_scores, query)
            more_values = nn(probs_low, d_context)
            grad_ref[0, :SEG_LEN] = more_keys[:SEG_LEN]
            grad_ref[1, :SEG_LEN] = more_values[:SEG_LEN]
            kv_rows_ref[0, segment] = grad_ref[0, own]
            kv_rows_ref[1, segment] = grad_ref[1, own]
            d_keys = d_keys + more_keys[SEG_LEN:]
            d_values = d_values + more_values[SEG_LEN:]
            if segment == CHAINED - 1:
                wait(1)
            d_next = d_hidden + nn(d_query, weights_ref[0])
            queries.append(d_query)
            hiddens.append(d_hidden_low)
            d_total_ref[segment] = d_total_low
            d_inner_ref[segment] = d_inner
            wide = column_sum(d_inner.astype(F32))
            rows = [
                column_sum(d_hidden),
                column_sum(d_normed * unit_one),
                column_sum(d_normed),
                column_sum(d_total),
                column_sum(d_memory * unit_two),
                column_sum(d_memory),
            ]
            rows += [wide[:, at : at + width] for at in range(0, wide.shape[1], width)]
            rows.append(column_sum(d_query.astype(F32)))
            rows = jnp.concatenate(rows, 0)
            sums = rows if sums is None else sums + rows
        d_keys, d_values = d_keys.astype(BF16), d_values.astype(BF16)
        key_rows.append(d_keys)
        value_rows.append(d_values)
        if segment == CHAINED:
            wait(2)
        d_next = 0.0 if d_next is None else d_next
        d_memory = d_next + nn(d_keys, weights_ref[1]) + nn(d_values, weights_ref[2])
    low = [low_ref[segment] for segment in reversed(range(SEGS))]
    low_all = jnp.concatenate(low, 0)
    low_chained = jnp.concatenate(low[1:], 0)
    context = jnp.concatenate([mem_context_ref[s] for s in reversed(range(CHAINED))], 0)
    pairs = (
        (jnp.concatenate(queries, 0), low_chained),
        (context, jnp.concatenate(hiddens, 0)),
        (jnp.concatenate(key_rows, 0), low_all),
        (jnp.concatenate(value_rows, 0), low_all),
    )
    start = (2 * side + core) * quarter

    def part(index):
        return lambda at, rows: grad_ref[index, pl.ds(pl.multiple_of(start + at, 8), rows)]

    value_sum = column_sum(jnp.concatenate(value_rows, 0).astype(F32))
    filler = jnp.zeros((SUM_ROWS - MEMORY_SUM - MEM, width), F32)
    sums = jnp.concatenate([sums, value_sum, d_memory[:MEM], filler], 0)
    for first, ref, extra in ((0, query_dense_ref, None), (2, dense_ref, sums)):
        for index in range(2):
            grad_ref[index, :width] = tn(*pairs[first + index])
        to_blocks(ref, [part(0), part(1)], extra)
    if not packed:
        share_refs[0][...] = d_inner_ref[...]
        share_refs[1][...] = d_total_ref[...]
        return
    share_out(place_ref, share_refs, d_inner_ref, d_total_ref)


def memory_backward(
    place, kv_mem, weights, keys, values, saved, vectors, inner_weight, outer_weight, packed
):
    width, ff = inner_weight.shape
    vmem = pl.BlockSpec(memory_space=pltpu.VMEM)
    query_rows, key_rows = block_rows(width)
    if packed:
        shares = [((CHAINED * MEM_PAD, width + SHARE_SPACE), F32)] * 4
    else:
        shares = [((CHAINED, MEM_PAD, ff), BF16), ((CHAINED, MEM_PAD, width), BF16)]
    shapes = [
        ((2, CHAINED, HALF_ROWS, width), F32),
        ((BLOCKS, query_rows, width), F32),
        ((BLOCKS, key_rows, width), F32),
    ] + shares
    return pl.pallas_call(
        partial(memory_backward_kernel, packed),
        in_specs=[pl.BlockSpec(memory_space=pltpu.SMEM)]
        + [vmem] * 12
        + [pl.BlockSpec(memory_space=pl.ANY)] * 5,
        out_specs=[vmem] * len(shapes),
        out_shape=[jax.ShapeDtypeStruct(shape, dtype) for shape, dtype in shapes],
        scratch_shapes=[
            pltpu.VMEM(weights.shape, BF16),
            pltpu.VMEM((CHAINED,) + keys.shape[1:], BF16),
            pltpu.VMEM((CHAINED,) + keys.shape[1:], BF16),
            pltpu.VMEM((width, ff), BF16),
            pltpu.VMEM((ff, width), BF16),
            pltpu.VMEM((2, width, width), F32),
            pltpu.VMEM((CHAINED, MEM_PAD, ff), BF16),
            pltpu.VMEM((CHAINED, MEM_PAD, width), BF16),
            pltpu.SemaphoreType.DMA((10,)),
        ],
        compiler_params=pltpu.CompilerParams(vmem_limit_bytes=60 << 20),
        cost_estimate=pl.CostEstimate(flops=1000, bytes_accessed=1000, transcendentals=0),
        name="memory_backward",
    )(place, *kv_mem, *saved, vectors, weights, keys, values, inner_weight, outer_weight)


def grads_out(place_ref, grads_ref, own_ref, other_ref, sums=None):
    quarter = grads_ref.shape[1] // 2
    core = place_ref[CORE]
    for ref, at in ((own_ref, core), (other_ref, 1 - core)):

        def part(index, at=at):
            return lambda row, rows: grads_ref[
                index, pl.ds(pl.multiple_of(at * quarter + row, 8), rows)
            ]

        to_blocks(ref, [part(0), part(1)], sums)


def query_grads_kernel(
    place_ref,
    tokens_ref,
    d_hidden_ref,
    d_query_ref,
    context_ref,
    d_hidden_low_ref,
    weights_ref,
    sums_in_ref,
    out_ref,
    own_ref,
    other_ref,
    sums_ref,
    grads_ref,
):
    segment = pl.program_id(0)
    half = out_ref.shape[2] // 2
    d_query = d_query_ref[0]
    out_ref[0] = d_hidden_ref[0] + nn(d_query, weights_ref[0])
    first_side = place_ref[SIDE] == 0

    @pl.when(segment == 0)
    def _():
        grads_ref[...] = jnp.zeros_like(grads_ref)
        sums_ref[...] = sums_in_ref[...]

    pairs = ((d_query, tokens_ref[0]), (context_ref[0], d_hidden_low_ref[0]))
    for index, (cols, against) in enumerate(pairs):
        grads_ref[index] += tn(jnp.where(first_side, cols[:, :half], cols[:, half:]), against)
    sums_ref[QUERY_SUM : QUERY_SUM + 1] += column_sum(d_query.astype(F32))

    @pl.when(segment == pl.num_programs(0) - 1)
    def _():
        grads_out(place_ref, grads_ref, own_ref, other_ref)


def query_grads(place, tokens, d_hidden, d_query, context, d_hidden_low, weights, sums):
    width = tokens.shape[2]

    def own_half():
        return pl.BlockSpec((1, HALF_ROWS, width), lambda i, place: (i, place[CORE], 0))

    def segment():
        return pl.BlockSpec((1, HALF_ROWS, width), lambda i, place: (i, 0, 0))

    def whole(shape):
        return pl.BlockSpec(shape, lambda i, place: (0,) * len(shape))

    shapes = [(BLOCKS, block_rows(width)[0], width)] * 2 + [(SUM_ROWS, width)]
    return pl.pallas_call(
        query_grads_kernel,
        grid_spec=pltpu.PrefetchScalarGridSpec(
            num_scalar_prefetch=1,
            grid=(SEGS,),
            in_specs=[
                own_half(),
                segment(),
                segment(),
                segment(),
                segment(),
                whole((1, width, width)),
                whole((SUM_ROWS, width)),
            ],
            out_specs=[segment()] + [whole(shape) for shape in shapes],
            scratch_shapes=[pltpu.VMEM((2, width // 2, width), F32)],
        ),
        out_shape=[
            jax.ShapeDtypeStruct(shape, F32) for shape in [(SEGS, HALF_ROWS, width)] + shapes
        ],
        compiler_params=pltpu.CompilerParams(vmem_limit_bytes=60 << 20),
        cost_estimate=pl.CostEstimate(flops=1000, bytes_accessed=1000, transcendentals=0),
        name="query_grads",
    )(place, tokens, d_hidden, d_query, context, d_hidden_low, weights, sums)


def input_grads_kernel(
    place_ref,
    tokens_ref,
    d_part_ref,
    kv_own_ref,
    kv_other_ref,
    kv_more_ref,
    key_ref,
    value_ref,
    sums_in_ref,
    out_ref,
    rows_ref,
    own_ref,
    other_ref,
    grads_ref,
    sums_ref,
):
    segment = pl.program_id(0)
    width = out_ref.shape[2]
    half = width // 2
    more = jnp.where(segment < CHAINED, 1.0, 0.0)
    d_keys = (kv_own_ref[0, 0] + kv_other_ref[0, 0] + more * kv_more_ref[0, 0]).astype(BF16)
    d_values = (kv_own_ref[1, 0] + kv_other_ref[1, 0] + more * kv_more_ref[1, 0]).astype(BF16)
    d_inputs = d_part_ref[0] + nn(d_keys, key_ref[0]) + nn(d_values, value_ref[0])
    out_ref[0] = d_inputs
    rows_ref[0] = d_inputs
    first_side = place_ref[SIDE] == 0

    @pl.when(segment == 0)
    def _():
        grads_ref[...] = jnp.zeros_like(grads_ref)
        sums_ref[...] = sums_in_ref[...]

    for index, cols in enumerate((d_keys, d_values)):
        cols = jnp.where(first_side, cols[:, :half], cols[:, half:])
        grads_ref[index] += tn(cols, tokens_ref[0])
    sums_ref[VALUE_SUM : VALUE_SUM + 1] += column_sum(d_values.astype(F32))

    @pl.when(segment == pl.num_programs(0) - 1)
    def _():
        grads_out(place_ref, grads_ref, own_ref, other_ref, sums_ref[...])


def input_grads(place, tokens, d_part, kv_own, kv_other, kv_more, weights, sums):
    width = tokens.shape[2]

    def own_half():
        return pl.BlockSpec((1, HALF_ROWS, width), lambda i, place: (i, place[CORE], 0))

    def segment():
        return pl.BlockSpec((1, HALF_ROWS, width), lambda i, place: (i, 0, 0))

    def two(last):
        return pl.BlockSpec(
            (2, 1, HALF_ROWS, width), lambda i, place: (0, jnp.minimum(i, last), 0, 0)
        )

    def weight(which):
        return pl.BlockSpec((1, width, width), lambda i, place: (which, 0, 0))

    dense = jax.ShapeDtypeStruct((BLOCKS, block_rows(width)[1], width), F32)
    dense_spec = pl.BlockSpec(dense.shape, lambda i, place: (0, 0, 0))
    return pl.pallas_call(
        input_grads_kernel,
        grid_spec=pltpu.PrefetchScalarGridSpec(
            num_scalar_prefetch=1,
            grid=(SEGS,),
            in_specs=[
                own_half(),
                segment(),
                two(SEGS - 1),
                two(SEGS - 1),
                two(CHAINED - 1),
                weight(1),
                weight(2),
                pl.BlockSpec((SUM_ROWS, width), lambda i, place: (0, 0)),
            ],
            out_specs=[own_half(), segment(), dense_spec, dense_spec],
            scratch_shapes=[
                pltpu.VMEM((2, width // 2, width), F32),
                pltpu.VMEM((SUM_ROWS, width), F32),
            ],
        ),
        out_shape=[
            jax.ShapeDtypeStruct((SEGS, SEG_LEN, width), F32),
            jax.ShapeDtypeStruct((SEGS, HALF_ROWS, width), F32),
            dense,
            dense,
        ],
        compiler_params=pltpu.CompilerParams(vmem_limit_bytes=60 << 20),
        cost_estimate=pl.CostEstimate(flops=1000, bytes_accessed=1000, transcendentals=0),
        name="input_grads",
    )(place, tokens, d_part, kv_own, kv_other, kv_more, weights, weights, sums)


def memory_shares_kernel(place_ref, *refs):
    early_refs, late_refs, refs = refs[:4], refs[4:8], refs[8:]
    inner_kept, inner_moved, outer_kept, outer_moved, keep_ref, send_ref = refs
    mine = place_ref[CHAIN] // 4
    quarter = keep_ref.shape[1]
    half = keep_ref.shape[2]
    width = 2 * half
    early, late = (
        jnp.concatenate([ref[...] for ref in share], 0).astype(BF16)
        for share in (early_refs, late_refs)
    )
    active, normed = early[:, :width], early[:, width : width + quarter]
    d_inner, d_total = late[:, :width], late[:, width : width + quarter]
    sides = (
        (inner_kept, inner_moved, normed, d_inner),
        (outer_kept, outer_moved, d_total, active),
    )
    for which, (kept_ref, moved_ref, factor, hidden) in enumerate(sides):
        more = tn(factor, hidden)
        parts = [kept_ref[at] + moved_ref[at] + more[:, half * at : half * (at + 1)] for at in (0, 1)]
        keep_ref[which] = jnp.where(mine == 0, parts[0], parts[1])
        send_ref[which] = jnp.where(mine == 0, parts[1], parts[0])


def memory_shares(place, early, late, inner_kept, inner_moved, outer_kept, outer_moved):
    vmem = pl.BlockSpec(memory_space=pltpu.VMEM)
    shape = jax.ShapeDtypeStruct((2,) + inner_kept.shape[1:], F32)
    return pl.pallas_call(
        memory_shares_kernel,
        in_specs=[pl.BlockSpec(memory_space=pltpu.SMEM)] + [vmem] * 12,
        out_specs=[vmem] * 2,
        out_shape=[shape, shape],
        compiler_params=pltpu.CompilerParams(vmem_limit_bytes=60 << 20),
        name="memory_shares",
    )(place, *early, *late, inner_kept, inner_moved, outer_kept, outer_moved)


def split_kernel(bits, counts, unused, place_ref, *refs):
    ins, outs = refs[: sum(counts)], refs[sum(counts) + unused :]
    for index, (bit, count) in enumerate(zip(bits, counts)):
        terms, ins = ins[:count], ins[count:]
        if bit is None:
            outs[2 * index][...] = sum((ref[...] for ref in terms[1:]), terms[0][...])
            continue
        mine = (place_ref[CHAIN] >> bit) & 1
        for out, at in ((outs[2 * index], mine), (outs[2 * index + 1], 1 - mine)):
            out[...] = sum((ref[:, at] for ref in terms[1:]), terms[0][:, at])


def split(place, *items, limit=32, after=()):
    terms, bits, counts, shapes, results = [], [], [], [], []
    for bit, axis, values in items:
        shape = values[0].shape
        bits.append(bit)
        counts.append(len(values))
        if bit is None:
            terms += values
            shapes += [shape, (8, 128)]
            results += [shape, (8, 128)]
            continue
        ahead = 1
        for size in shape[:axis]:
            ahead *= size
        terms += [value.reshape((ahead, 2, -1) + shape[-2:]) for value in values]
        half = shape[:axis] + shape[axis + 1 :]
        inner = terms[-1].shape
        shapes += [inner[:1] + inner[2:]] * 2
        results += [half] * 2
    vmem = pl.BlockSpec(memory_space=pltpu.VMEM)
    outs = pl.pallas_call(
        partial(split_kernel, tuple(bits), tuple(counts), len(after)),
        in_specs=[pl.BlockSpec(memory_space=pltpu.SMEM)]
        + [vmem] * len(terms)
        + [pl.BlockSpec(memory_space=pl.ANY)] * len(after),
        out_specs=[vmem] * len(shapes),
        out_shape=[jax.ShapeDtypeStruct(shape, F32) for shape in shapes],
        compiler_params=pltpu.CompilerParams(vmem_limit_bytes=limit << 20),
        name="split",
    )(place, *terms, *after)
    return [out.reshape(shape) for out, shape in zip(outs, results)]


def join_kernel(bits, unused, place_ref, *refs):
    ins, outs = refs[: 2 * len(bits)], refs[2 * len(bits) + unused :]
    for index, bit in enumerate(bits):
        mine = (place_ref[CHAIN] >> bit) & 1
        outs[index][:, mine] = ins[2 * index][...]
        outs[index][:, 1 - mine] = ins[2 * index + 1][...]


def join(place, *items, after=()):
    terms, bits, shapes, results = [], [], [], []
    for bit, axis, own, other in items:
        shape = own.shape
        ahead = 1
        for size in shape[:axis]:
            ahead *= size
        terms += [value.reshape((ahead, -1) + shape[-2:]) for value in (own, other)]
        bits.append(bit)
        inner = terms[-1].shape
        shapes.append(inner[:1] + (2,) + inner[1:])
        results.append(shape[:axis] + (2,) + shape[axis:])
    vmem = pl.BlockSpec(memory_space=pltpu.VMEM)
    outs = pl.pallas_call(
        partial(join_kernel, tuple(bits), len(after)),
        in_specs=[pl.BlockSpec(memory_space=pltpu.SMEM)]
        + [vmem] * len(terms)
        + [pl.BlockSpec(memory_space=pl.ANY)] * len(after),
        out_specs=[vmem] * len(shapes),
        out_shape=[jax.ShapeDtypeStruct(shape, F32) for shape in shapes],
        compiler_params=pltpu.CompilerParams(vmem_limit_bytes=32 << 20),
        name="join",
    )(place, *terms, *after)
    return [out.reshape(shape) for out, shape in zip(outs, results)]


def feed_final_kernel(place_ref, *refs):
    pieces, (inner_ref, outer_ref, wide_ref) = refs[:4], refs[4:]
    side, core = place_ref[SIDE], place_ref[CORE]
    quarter = pieces[0].shape[1]
    places = (
        2 * side + core,
        2 * side + 1 - core,
        2 * (1 - side) + core,
        2 * (1 - side) + 1 - core,
    )
    for ref, at in zip(pieces, places):
        rows = pl.ds(pl.multiple_of(at * quarter, 8), quarter)
        inner_ref[rows] = ref[0]
        wide_ref[rows] = ref[1]
    outer_ref[...] = wide_ref[...].T


def feed_final(place, pieces):
    quarter, piece = pieces[0].shape[1:]
    vmem = pl.BlockSpec(memory_space=pltpu.VMEM)
    shapes = [(4 * quarter, piece), (piece, 4 * quarter)]
    return pl.pallas_call(
        feed_final_kernel,
        in_specs=[pl.BlockSpec(memory_space=pltpu.SMEM)] + [vmem] * 4,
        out_specs=[vmem] * 2,
        out_shape=[jax.ShapeDtypeStruct(shape, F32) for shape in shapes],
        scratch_shapes=[pltpu.VMEM((4 * quarter, piece), F32)],
        compiler_params=pltpu.CompilerParams(vmem_limit_bytes=32 << 20),
        name="feed_final",
    )(place, *pieces)


def final_kernel(place_ref, query_own, query_other, dense_own, dense_other, *refs):
    grad_query, grad_out, grad_key, grad_value, memory_ref, *refs = refs
    *vector_refs, query_bias_ref, value_bias_ref, inner_bias_ref, sums_ref = refs
    chain = place_ref[CHAIN]
    fast = chain % 2

    def put(ref, block, value):
        rows = value.shape[0]
        ref[pl.ds(pl.multiple_of(block * rows, 8), rows)] = value

    rows = query_own.shape[2] // 2
    for far in range(2):
        for near in range(2):
            for source, at in ((query_own, fast), (query_other, 1 - fast)):
                block = 4 * far + 2 * near + at
                put(grad_query, block, source[far, near, :rows])
                put(grad_out, block, source[far, near, rows:])
            for source, at in ((dense_own, fast), (dense_other, 1 - fast)):
                block = 4 * far + 2 * near + at
                put(grad_key, block, source[far, near, :rows])
                put(grad_value, block, source[far, near, rows : 2 * rows])
                put(sums_ref, block, source[far, near, 2 * rows :])
    width = sums_ref.shape[1]
    quarter, piece = query_bias_ref.shape[0], inner_bias_ref.shape[0]

    def row(index):
        at = SUM_SPACE * (index // SUM_PART) + index % SUM_PART
        return sums_ref[at : at + 1]

    for index, ref in enumerate(vector_refs):
        ref[...] = row(index).reshape(width)
    own = 2 * place_ref[SIDE] + place_ref[CORE]
    for ref, index in ((query_bias_ref, QUERY_SUM), (value_bias_ref, VALUE_SUM)):
        whole = row(index)
        value = whole[:, :quarter]
        for other in range(1, 4):
            value = jnp.where(own == other, whole[:, quarter * other : quarter * (other + 1)], value)
        ref[...] = value.reshape(quarter)
    count = width // piece
    value = jnp.zeros((1, piece), F32)
    for index in range(QUERY_SUM - len(vector_refs)):
        whole = row(len(vector_refs) + index)
        for part in range(count):
            here = chain == count * index + part
            value = jnp.where(here, whole[:, piece * part : piece * (part + 1)], value)
    inner_bias_ref[...] = value.reshape(piece)
    for index in range(MEM):
        memory_ref[index : index + 1] = row(MEMORY_SUM + index)


def final(place, halves, piece):
    width = halves[0].shape[3]
    quarter = width // 4
    vmem = pl.BlockSpec(memory_space=pltpu.VMEM)
    shapes = [(quarter, width)] * 4 + [(MEM, width)] + [(width,)] * 6
    shapes += [(quarter,), (quarter,), (piece,)]
    return pl.pallas_call(
        final_kernel,
        in_specs=[pl.BlockSpec(memory_space=pltpu.SMEM)] + [vmem] * 4,
        out_specs=[vmem] * len(shapes),
        out_shape=[jax.ShapeDtypeStruct(shape, F32) for shape in shapes],
        scratch_shapes=[pltpu.VMEM((BLOCKS * SUM_SPACE, width), F32)],
        compiler_params=pltpu.CompilerParams(vmem_limit_bytes=32 << 20),
        name="final",
    )(place, *halves)


def swap_core(value):
    return lax.ppermute(value, "head", [(0, 1), (1, 0), (2, 3), (3, 2)])


def swap_side(value):
    return lax.ppermute(value, "head", [(0, 2), (2, 0), (1, 3), (3, 1)])


def swap_dp(value, bits):
    size = lax.axis_size("dp")
    return lax.ppermute(value, "dp", [(i, i ^ bits) for i in range(size)])


def fetch_far(value):
    part = lax.axis_index("dp") % 4
    mine = lax.dynamic_index_in_dim(value, part, 0, False)
    rows = mine.shape[0]
    half, quarter = rows // 2, rows // 4
    pieces = []
    for start in (0, half):
        own = swap_side(mine[start : start + half])
        fast, slow = swap_dp(own, 1), swap_dp(own, 2)
        pieces += [(0, start, own), (1, start, fast), (2, start, slow)]
        pieces.append((3, start, swap_dp(slow[:quarter], 1)))
        pieces.append((3, start + quarter, swap_dp(fast[quarter:], 2)))
    return pieces


def on_device(
    tokens,
    cotangent,
    memory,
    query_weight,
    query_bias,
    key_weight,
    value_weight,
    value_bias,
    out_weight,
    out_bias,
    gain_one,
    shift_one,
    inner_weight,
    inner_bias,
    outer_weight,
    outer_bias,
    gain_two,
    shift_two,
    group_sizes,
    group_section,
    last_valid,
):
    width = memory.shape[1]
    ff = inner_weight.shape[1]
    dp_size = lax.axis_size("dp")
    chain_index = lax.axis_index("dp")
    head_index = lax.axis_index("head")
    side = head_index // 2
    core = head_index % 2
    quarter = query_weight.shape[1]
    device = chain_index * 4 + head_index
    divisors, sizes = jnp.array([2, 1, 4, 4], jnp.int32), jnp.array([2, 2, 4, dp_size], jnp.int32)
    place = (device // divisors) % sizes
    scalars = (place, group_sizes, group_section, last_valid)

    own_weights = (query_weight.T, key_weight.T, value_weight.T, out_weight)
    wide_weights = jnp.stack([weight.astype(F32) for weight in own_weights])
    far = fetch_far(wide_weights)
    partner = swap_core(wide_weights)
    memory = jnp.pad(memory.astype(F32), ((0, MEM_PAD - MEM), (0, 0)))
    places, far = [piece[:2] for piece in far], [piece[2] for piece in far]
    far_partner = [swap_core(piece) for piece in far]
    vectors = pack_vectors(
        place,
        (out_bias, gain_one, shift_one, outer_bias, gain_two, shift_two),
        query_bias,
        value_bias,
        inner_bias,
    )
    row = jnp.arange(VECTOR_ROWS)[:, None]
    split_rows = (row == QUERY_BIAS) | (row == VALUE_BIAS)
    for swap in (swap_core, swap_side):
        vectors = vectors + jnp.where(split_rows, swap(vectors), 0.0)
    token_rows = tokens.reshape(SEGS, SEG_LEN, width)

    weights, keys, values, own_query, *saved = memory_forward(
        places,
        scalars,
        token_rows,
        memory,
        own_weights,
        partner,
        far,
        far_partner,
        vectors,
        inner_weight,
        outer_weight,
    )
    context, probs = attend(scalars, own_query, keys, values)
    (
        layer_out,
        out_rows,
        d_hidden,
        d_hidden_low,
        d_context,
        sums,
        own_inner,
        own_outer,
        other_inner,
        other_outer,
    ) = feed(
        scalars,
        token_rows,
        context,
        cotangent.reshape(SEGS, SEG_LEN, width),
        weights,
        inner_weight,
        outer_weight,
        vectors,
    )

    piece = ff // dp_size
    back = partial(attend_back, place, own_query, keys, values, d_context, probs)
    held = back(CHAINED, SEGS - CHAINED)
    fast_path = dp_size == BLOCKS
    run = on_block if fast_path else on_any
    results = run(
        place,
        scalars,
        back,
        held,
        (own_inner, own_outer, other_inner, other_outer),
        partial(query_grads, place, token_rows, d_hidden),
        (context, d_hidden_low, weights, sums),
        partial(
            memory_backward,
            place,
            weights=weights,
            keys=keys,
            values=values,
            saved=saved[:9],
            vectors=vectors,
            inner_weight=inner_weight,
            outer_weight=outer_weight,
            packed=fast_path,
        ),
        partial(input_grads, place, token_rows, weights=weights),
        saved,
        out_rows,
    )
    grads, smalls, grad_inner, grad_outer, grad_tokens, others = results
    grad_query, grad_out, grad_key, grad_value = grads
    grad_memory, *grad_vectors, grad_qb, grad_vb, inner_bias_grad = smalls

    def both_cores(value, other):
        start = (1 - core) * HALF_ROWS
        value = lax.dynamic_update_slice_in_dim(value, other, start, 1)
        return value.reshape(SEGS * SEG_LEN, width)

    return (
        both_cores(layer_out, others[0]),
        both_cores(grad_tokens, others[1]),
        grad_memory,
        grad_query.T,
        grad_qb,
        grad_key.T,
        grad_value.T,
        grad_vb,
        grad_out,
        *grad_vectors[:3],
        grad_inner,
        inner_bias_grad,
        grad_outer,
        *grad_vectors[3:],
    )


def at_bits(value, bits):
    axis = 0
    for bit in bits:
        if bit is None:
            axis += 1
        else:
            value = lax.dynamic_index_in_dim(value, bit, axis, False)
    return value


def on_block(
    place, scalars, back, held, ffn, query_part, query_args, backward, input_part, saved, out_rows
):
    index = lax.axis_index("dp")
    fast, slow = index & 1, (index >> 1) & 1
    own_inner, own_outer, other_inner, other_outer = ffn
    early = saved[9:]
    early = early[:1] + [swap_dp(share, bits) for bits, share in enumerate(early) if bits]
    ffn = in_step(
        own_inner, own_outer, swap_core(other_inner), swap_core(other_outer), *early, *held
    )
    ffn, early, held = ffn[:4], ffn[4:8], ffn[8:]
    own_inner, own_outer, other_inner, other_outer = (
        value.reshape((2, 2, 2) + value.shape[1:]) for value in ffn
    )
    inner, outer = (own_inner, other_inner), (own_outer, other_outer)

    def total(terms, bits):
        terms = [at_bits(term, bits) for term in terms]
        return sum(terms[1:], terms[0])

    inner_moved = swap_dp(total(inner, (None, 1 - slow, None)), 2)
    outer_moved = swap_dp(total(outer, (None, None, 1 - fast)), 1)
    d_query, kv_own, kv_other, kv_mem = back(0, CHAINED, held)
    d_part, query_own, query_other, sums = query_part(d_query, *query_args)
    weights = query_args[2]
    values = in_step(
        inner_moved,
        outer_moved,
        d_part,
        query_own,
        query_other,
        sums,
        kv_own,
        kv_other,
        kv_mem,
        swap_core(kv_mem),
    )
    inner_moved, outer_moved, d_part, query_own, query_other, sums, kv_own, kv_other = values[:8]
    kv_mem = values[8:]

    def second(terms, moved, bits, axis, bit):
        def half(at):
            here = [at if place == axis else value for place, value in enumerate(bits)]
            rest = [None if value is None or place != axis else at for place, value in enumerate(here)]
            del rest[[i for i, value in enumerate(bits) if value is not None][0]]
            return total(terms, here) + at_bits(moved, rest)

        return half(bit), half(1 - bit)

    inner_kept, inner_sent = second(inner, inner_moved, (None, slow, None), 2, fast)
    outer_kept, outer_sent = second(outer, outer_moved, (None, None, fast), 1, slow)
    inner_moved, outer_moved = swap_dp(inner_sent, 1), swap_dp(outer_sent, 2)
    kv_other = swap_core(kv_other)
    query_other = swap_core(query_other)
    kv_more, query_mem, dense_mem, *late = backward(kv_mem)

    def cube(*arrays):
        return [value.reshape((2, 2, 2) + value.shape[1:]) for value in arrays]

    q_kept, q_sent = split(place, (0, 2, cube(query_own, query_other, query_mem)), limit=60)
    values = in_step(
        inner_kept,
        inner_moved,
        outer_kept,
        outer_moved,
        kv_other,
        kv_more,
        q_kept,
        q_sent,
        dense_mem,
        *late,
    )
    inner_kept, inner_moved, outer_kept, outer_moved, kv_other, kv_more = values[:6]
    q_kept, q_sent, dense_mem, *late = values[6:]
    q_moved = swap_dp(q_sent, 1)
    late = late[:1] + [swap_dp(share, bits) for bits, share in enumerate(late) if bits]
    grad_tokens, token_rows, dense_own, dense_other = input_part(
        d_part, kv_own, kv_other, kv_more, sums=sums
    )
    q_moved, *late, dense_own, dense_other = in_step(q_moved, *late, dense_own, dense_other)

    ffn_kept, ffn_sent = memory_shares(place, early, late, inner_kept, inner_moved, outer_kept, outer_moved)
    ffn_kept, ffn_sent, dense_own, dense_other = in_step(
        ffn_kept, ffn_sent, dense_own, swap_core(dense_other)
    )
    ffn_moved = swap_dp(ffn_sent, 4)
    q_kept, q_sent = split(place, (1, 1, [q_kept, q_moved]))
    q_moved = swap_dp(q_sent, 2)
    d_kept, d_sent = split(place, (0, 2, cube(dense_own, dense_other, dense_mem)), limit=60)
    d_moved = swap_dp(d_sent, 1)
    q_part, _, d_kept, d_sent = split(
        place, (None, 0, [q_kept, q_moved]), (1, 1, [d_kept, d_moved])
    )
    q_moved, d_moved = swap_dp(q_part, 4), swap_dp(d_sent, 2)
    d_part, _, ffn_mine, _ = split(
        place, (None, 0, [d_kept, d_moved]), (None, 0, [ffn_kept, ffn_moved])
    )
    d_moved = swap_dp(d_part, 4)
    ffn_far = swap_side(ffn_mine)
    q_mine, _ = split(place, (None, 0, [q_part, q_moved]))
    (q_mine,) = join(place, (1, 1, q_mine, swap_dp(q_mine, 2)))
    d_mine, _ = split(place, (None, 0, [d_part, d_moved]), after=(q_mine,))
    q_moved = swap_dp(q_mine, 1)
    (d_mine,) = join(place, (1, 1, d_mine, swap_dp(d_mine, 2)), after=(q_moved,))
    pieces = (ffn_mine, swap_core(ffn_mine), ffn_far, swap_core(ffn_far))
    grad_inner, grad_outer = feed_final(place, pieces)
    halves = (q_mine, q_moved, d_mine, swap_dp(d_mine, 1))
    grads = final(place, halves, grad_inner.shape[1])
    others = (swap_core(out_rows), swap_core(token_rows))
    return grads[:4], grads[4:], grad_inner, grad_outer, grad_tokens, others


def on_any(
    place, scalars, back, held, ffn, query_part, query_args, backward, input_part, saved, out_rows
):
    own_inner, own_outer, other_inner, other_outer = ffn
    dp_size = lax.axis_size("dp")
    quarter = own_inner.shape[1]
    width = 4 * quarter
    head_index = lax.axis_index("head")
    d_query, kv_own, kv_other, kv_mem = back(0, CHAINED, held)
    d_part, query_own, query_other, sums = query_part(d_query, *query_args)
    kv_mem = (kv_mem, swap_core(kv_mem))
    kv_more, query_mem, dense_mem, mem_d_inner, mem_d_total = backward(kv_mem)
    grad_tokens, token_rows, dense_own, dense_other = input_part(
        d_part, kv_own, swap_core(kv_other), kv_more, sums=sums
    )
    query = query_own + swap_core(query_other) + query_mem
    dense = dense_own + swap_core(dense_other) + dense_mem
    query, dense = lax.psum((query, dense), "dp")
    mem_active, mem_normed = saved[7], saved[8]

    def whole(own, other, rows, hidden):
        rows = lax.dynamic_slice_in_dim(rows, head_index * quarter, quarter, 2)
        rows = rows.reshape(-1, quarter)
        value = own + swap_core(other)
        value = value.transpose(1, 0, 2).reshape(quarter, -1)
        value = value + tn(rows, hidden.reshape(rows.shape[0], -1))
        value = lax.psum_scatter(value, "dp", scatter_dimension=1, tiled=True)
        return lax.all_gather(value, "head").reshape(width, -1)

    grad_inner = whole(own_inner, other_inner, mem_normed, mem_d_inner)
    grad_outer = whole(own_outer, other_outer, mem_d_total, mem_active).T
    rows = quarter // BLOCKS

    def part(value, index):
        return value[:, rows * index : rows * (index + 1)].reshape(quarter, width)

    sums = dense[:, 2 * rows : 2 * rows + SUM_PART].reshape(SUM_ROWS, width)
    piece = grad_inner.shape[1]
    at = lax.axis_index("dp") * piece
    smalls = (
        sums[MEMORY_SUM : MEMORY_SUM + MEM],
        *sums[:6],
        lax.dynamic_slice_in_dim(sums[QUERY_SUM], head_index * quarter, quarter, 0),
        lax.dynamic_slice_in_dim(sums[VALUE_SUM], head_index * quarter, quarter, 0),
        lax.dynamic_slice_in_dim(sums[6:QUERY_SUM].reshape(-1), at, piece, 0),
    )
    grads = (part(query, 0), part(query, 1), part(dense, 0), part(dense, 1))
    others = (swap_core(out_rows), swap_core(token_rows))
    return grads, smalls, grad_inner, grad_outer, grad_tokens, others


def solution(mesh):
    row, col, vec, every = P("dp", None), P(None, "head"), P("head"), P()
    placed = (row, row, every, col, vec, col, col, vec, P("head", None)) + (every,) * 11
    return jax.shard_map(
        on_device,
        mesh=mesh,
        in_specs=placed + (P("dp"),),
        out_specs=(
            row,
            row,
            every,
            col,
            vec,
            col,
            col,
            vec,
            P("head", None),
            every,
            every,
            every,
            P(None, "dp"),
            P("dp"),
            row,
            every,
            every,
            every,
        ),
        check_vma=False,
    )
```

```python
from functools import partial

import jax
import jax.numpy as jnp
from jax import lax
from jax.experimental import pallas as pl
from jax.experimental.pallas import tpu as pltpu
from jax.sharding import PartitionSpec as P

HEAD_DIM = 64
MEM = 10
MEM_PAD = 16
SEG_LEN = 512
SEGS = 3
CHAINED = SEGS - 1
KEYS = SEG_LEN + MEM_PAD
HALF_ROWS = SEG_LEN // 2
EPS = 1e-06
SCALE = HEAD_DIM ** (-0.5)
MASKED = -1000000000.0
LN_TWO = 0.6931471805599453

F32 = jnp.float32
BF16 = jnp.bfloat16


def nn(left, right):
    return jnp.dot(left, right, preferred_element_type=F32)


def nt(left, right):
    return lax.dot_general(left, right, (((1,), (1,)), ((), ())), preferred_element_type=F32)


def tn(left, right):
    return lax.dot_general(left, right, (((0,), (0,)), ((), ())), preferred_element_type=F32)


def norm_fwd(value, gain, shift):
    centered = value - jnp.mean(value, axis=-1, keepdims=True)
    spread = jnp.mean(centered * centered, axis=-1, keepdims=True)
    root = lax.rsqrt(spread + EPS)
    unit = centered * root
    return unit * gain + shift, unit, root


def norm_bwd(d_out, unit, root, gain):
    d_unit = d_out * gain
    mean_one = jnp.mean(d_unit, axis=-1, keepdims=True)
    mean_two = jnp.mean(d_unit * unit, axis=-1, keepdims=True)
    return root * (d_unit - mean_one - unit * mean_two)


def gelu_parts(inner):
    cdf = 0.5 * (1.0 + lax.erf(inner * 0.7071067811865476))
    pdf = jnp.exp(-0.5 * inner * inner) * 0.3989422804014327
    return inner * cdf, cdf + inner * pdf


def column_sum(value):
    return jnp.sum(value, axis=0, keepdims=True)


SHARE_SPACE = 256

SIDE, CORE, PART, CHAIN = range(4)


def limit_of(segment, place_ref, sizes_ref, sections_ref, last_ref):
    chain = place_ref[CHAIN]
    end, section = 0, 0
    for group in range(sizes_ref.shape[0]):
        start, end = end, end + sizes_ref[group]
        inside = jnp.logical_and(start <= chain, chain < end)
        section = jnp.where(inside, sections_ref[group], section)
    last = section % (SEGS - 1) + 1
    return jnp.where(segment < last, SEG_LEN, jnp.where(segment == last, last_ref[0], 0))


def key_bias(limit):
    row = lax.broadcasted_iota(jnp.int32, (KEYS, 1), 0)
    beyond = jnp.where((row >= SEG_LEN) & (row < SEG_LEN + MEM), LN_TWO, MASKED)
    return jnp.where(row < limit, 0.0, beyond)


OUT_BIAS, GAIN_ONE, SHIFT_ONE, OUTER_BIAS, GAIN_TWO, SHIFT_TWO, QUERY_BIAS, VALUE_BIAS = range(8)
INNER_BIAS = 8
VECTOR_ROWS = 16


def row_of(vectors, index):
    return vectors[index : index + 1]


def head_mask(width):
    count = width // HEAD_DIM
    shape = (count, MEM_PAD, width)
    head = lax.broadcasted_iota(jnp.int32, shape, 0)
    lane = lax.broadcasted_iota(jnp.int32, shape, 2) // HEAD_DIM
    return (head == lane).astype(F32)


def spread_heads(value, mask):
    count, rows, width = mask.shape
    return (value.astype(F32)[None] * mask).reshape(count * rows, width).astype(BF16)


def gather_heads(value, mask):
    return jnp.sum(value.reshape(mask.shape) * mask, axis=0)


def pack_vectors_kernel(place_ref, *refs):
    *vector_refs, query_ref, value_ref, inner_ref, out_ref = refs
    width = out_ref.shape[1]
    quarter = query_ref.shape[0]
    out_ref[...] = jnp.zeros_like(out_ref)
    for index, ref in enumerate(vector_refs):
        out_ref[index : index + 1] = ref[...].reshape(1, width)
    index = 2 * place_ref[SIDE] + place_ref[CORE]
    for row, ref in ((QUERY_BIAS, query_ref), (VALUE_BIAS, value_ref)):
        piece = ref[...].reshape(1, quarter)
        for at in range(4):
            columns = slice(quarter * at, quarter * (at + 1))
            out_ref[row : row + 1, columns] = jnp.where(index == at, piece, 0.0)
    for at in range(inner_ref.shape[0] // width):
        piece = inner_ref[width * at : width * (at + 1)].reshape(1, width)
        out_ref[INNER_BIAS + at : INNER_BIAS + at + 1] = piece


def pack_vectors(place, vectors, query_bias, value_bias, inner_bias):
    width = vectors[0].shape[0]
    vmem = pl.BlockSpec(memory_space=pltpu.VMEM)
    return pl.pallas_call(
        pack_vectors_kernel,
        in_specs=[pl.BlockSpec(memory_space=pltpu.SMEM)] + [vmem] * (len(vectors) + 3),
        out_specs=vmem,
        out_shape=jax.ShapeDtypeStruct((VECTOR_ROWS, width), F32),
        name="pack_vectors",
    )(place, *vectors, query_bias, value_bias, inner_bias)


def share_out(place_ref, refs, hidden_ref, wide_ref):
    at_fast, at_slow = place_ref[PART] % 2, place_ref[PART] // 2
    index = 2 * place_ref[SIDE] + place_ref[CORE]
    width = wide_ref.shape[2]
    half, quarter = width // 2, width // 4
    for bits, ref in enumerate(refs):
        base = 2 * (at_slow ^ (bits // 2)) + (at_fast ^ (bits % 2))
        for segment in range(CHAINED):
            rows = slice(MEM_PAD * segment, MEM_PAD * (segment + 1))
            for far in range(2):
                columns = pl.ds(pl.multiple_of((4 * far + base) * half, half), half)
                ref[rows, far * half : (far + 1) * half] = hidden_ref[segment, :, columns].astype(F32)
            wide = wide_ref[segment]
            piece = wide[:, :quarter]
            for other in range(1, 4):
                piece = jnp.where(
                    index == other, wide[:, quarter * other : quarter * (other + 1)], piece
                )
            ref[rows, width : width + quarter] = piece.astype(F32)
            gap = jnp.zeros((MEM_PAD, SHARE_SPACE - quarter), F32)
            ref[rows, width + quarter :] = gap


def memory_forward_kernel(
    places,
    place_ref,
    sizes_ref,
    sections_ref,
    last_ref,
    tokens_ref,
    memory_ref,
    own_q_ref,
    own_k_ref,
    own_v_ref,
    own_o_ref,
    partner_ref,
    vectors_ref,
    *refs,
):
    far_refs, far_partner_refs, refs = (
        refs[: len(places)],
        refs[len(places) : 2 * len(places)],
        refs[2 * len(places) :],
    )
    inner_hbm, outer_hbm, weights_hbm, keys_hbm, values_hbm, query_hbm, *refs = refs
    saved_hbm, (weights_ref, keys_ref, values_ref, query_ref) = refs[:13], refs[13:17]
    saved, (inner_ref, outer_ref, sems) = refs[17:30], refs[30:]
    (
        low_ref,
        mem_query_ref,
        mem_context_ref,
        mem_probs_ref,
        mem_hidden_ref,
        mem_total_ref,
        mem_slope_ref,
        mem_active_ref,
        mem_normed_ref,
        *share_refs,
    ) = saved
    copies = [
        pltpu.make_async_copy(inner_hbm, inner_ref, sems.at[0]),
        pltpu.make_async_copy(outer_hbm, outer_ref, sems.at[1]),
    ]
    for copy in copies:
        copy.start()
    side, core, part = place_ref[SIDE], place_ref[CORE], place_ref[PART]
    quarter = own_q_ref.shape[0]
    width = memory_ref.shape[1]

    def span_of(at_side, at_core, start=0, rows=quarter):
        start = (2 * at_side + at_core) * quarter + start
        return pl.ds(pl.multiple_of(start, 16), rows)

    for which, ref in enumerate((own_q_ref, own_k_ref, own_v_ref, own_o_ref)):
        weights_ref[which, span_of(side, core)] = ref[...]
        weights_ref[which, span_of(side, 1 - core)] = partner_ref[which].astype(BF16)
    for (bits, start), near_ref, other_ref in zip(places, far_refs, far_partner_refs):
        which, rows = part ^ bits, near_ref.shape[0]
        weights_ref[which, span_of(1 - side, core, start, rows)] = near_ref[...].astype(BF16)
        weights_ref[which, span_of(1 - side, 1 - core, start, rows)] = other_ref[...].astype(BF16)
    writes = [pltpu.make_async_copy(weights_ref, weights_hbm, sems.at[2])]
    writes[0].start()
    vectors = vectors_ref[...]
    query_bias = row_of(vectors, QUERY_BIAS)
    value_bias = row_of(vectors, VALUE_BIAS)

    def project(index, carry):
        segment, half = index // 2, index % 2
        span = pl.ds(half * HALF_ROWS, HALF_ROWS)
        rows = tokens_ref[segment, span]
        keys_ref[segment, span] = nt(rows, weights_ref[1]).astype(BF16)
        values_ref[segment, span] = (nt(rows, weights_ref[2]) + value_bias).astype(BF16)

        @pl.when(half == core)
        def _():
            query_ref[segment] = (nt(rows, weights_ref[0]) + query_bias).astype(BF16) * SCALE

        return carry

    lax.fori_loop(0, 2 * SEGS, project, 0)
    token_rows, mem_rows = pl.ds(0, SEG_LEN), pl.ds(SEG_LEN, MEM_PAD)
    pairs = ((keys_ref, keys_hbm), (values_ref, values_hbm))
    writes.append(pltpu.make_async_copy(query_ref, query_hbm, sems.at[3]))
    for index, (ref, hbm) in enumerate(pairs):
        writes.append(
            pltpu.make_async_copy(ref.at[:, token_rows], hbm.at[:, token_rows], sems.at[4 + index])
        )
    for write in writes[1:]:
        write.start()

    mask = head_mask(width)
    now = memory_ref[...]
    for segment in range(SEGS):
        low = now.astype(BF16)
        low_ref[segment] = low
        keys_ref[segment, SEG_LEN:] = nt(low, weights_ref[1]).astype(BF16)
        values_ref[segment, SEG_LEN:] = (nt(low, weights_ref[2]) + value_bias).astype(BF16)
        if segment == CHAINED:
            break
        query = (nt(low, weights_ref[0]) + query_bias).astype(BF16) * SCALE
        mem_query_ref[segment] = query
        scores = nt(keys_ref[segment], spread_heads(query, mask))
        limit = limit_of(segment, place_ref, sizes_ref, sections_ref, last_ref)
        scores = scores + key_bias(limit)
        weights = jnp.exp(scores - jnp.max(scores, axis=0, keepdims=True))
        probs = weights * (1.0 / jnp.sum(weights, axis=0, keepdims=True))
        mem_probs_ref[segment] = probs
        context = gather_heads(tn(probs.astype(BF16), values_ref[segment]), mask).astype(BF16)
        mem_context_ref[segment] = context
        hidden = now + nn(context, weights_ref[3]) + row_of(vectors, OUT_BIAS)
        mem_hidden_ref[segment] = hidden
        normed, _, _ = norm_fwd(hidden, row_of(vectors, GAIN_ONE), row_of(vectors, SHIFT_ONE))
        mem_normed_ref[segment] = normed.astype(BF16)
        if segment == 0:
            copies[0].wait()
        inner_bias = [row_of(vectors, INNER_BIAS + i) for i in range(inner_ref.shape[1] // width)]
        inner_bias = jnp.concatenate(inner_bias, 1)
        active, slope = gelu_parts(nn(normed.astype(BF16), inner_ref[...]) + inner_bias)
        active = active.astype(BF16)
        mem_slope_ref[segment] = slope
        mem_active_ref[segment] = active
        if segment == 0:
            copies[1].wait()
        total = normed + nn(active, outer_ref[...]) + row_of(vectors, OUTER_BIAS)
        mem_total_ref[segment] = total
        now, _, _ = norm_fwd(total, row_of(vectors, GAIN_TWO), row_of(vectors, SHIFT_TWO))
    for index, (ref, hbm) in enumerate(pairs):
        writes.append(
            pltpu.make_async_copy(ref.at[:, mem_rows], hbm.at[:, mem_rows], sems.at[6 + index])
        )
        writes[-1].start()
    share_out(place_ref, share_refs, mem_active_ref, mem_normed_ref)
    for index, (ref, hbm) in enumerate(zip(saved, saved_hbm)):
        writes.append(pltpu.make_async_copy(ref, hbm, sems.at[8 + index]))
        writes[-1].start()
    for write in writes:
        write.wait()


def memory_forward(
    places, scalars, tokens, memory, own, partner, far, far_partner, vectors, inner_weight, outer_weight
):
    width = memory.shape[1]
    ff = inner_weight.shape[1]
    head_rows = MEM_PAD * width // HEAD_DIM
    vmem = pl.BlockSpec(memory_space=pltpu.VMEM)

    def like(shape, dtype):
        return jax.ShapeDtypeStruct(shape, dtype)

    saved = [
        ((SEGS, MEM_PAD, width), BF16),
        ((CHAINED, MEM_PAD, width), BF16),
        ((CHAINED, MEM_PAD, width), BF16),
        ((CHAINED, KEYS, head_rows), F32),
        ((CHAINED, MEM_PAD, width), F32),
        ((CHAINED, MEM_PAD, width), F32),
        ((CHAINED, MEM_PAD, ff), F32),
        ((CHAINED, MEM_PAD, ff), BF16),
        ((CHAINED, MEM_PAD, width), BF16),
    ] + [((CHAINED * MEM_PAD, width + SHARE_SPACE), F32)] * 4
    large = [
        ((4, width, width), BF16),
        ((SEGS, KEYS, width), BF16),
        ((SEGS, KEYS, width), BF16),
        ((SEGS, HALF_ROWS, width), BF16),
    ]
    return pl.pallas_call(
        partial(memory_forward_kernel, places),
        in_specs=[pl.BlockSpec(memory_space=pltpu.SMEM)] * 4
        + [vmem] * (8 + 2 * len(places))
        + [pl.BlockSpec(memory_space=pl.ANY)] * 2,
        out_specs=[pl.BlockSpec(memory_space=pltpu.HBM)] * 17,
        out_shape=[pltpu.HBM(*shape) for shape in large + saved],
        scratch_shapes=[pltpu.VMEM(*shape) for shape in large + saved]
        + [
            pltpu.VMEM((width, ff), BF16),
            pltpu.VMEM((ff, width), BF16),
            pltpu.SemaphoreType.DMA((21,)),
        ],
        compiler_params=pltpu.CompilerParams(vmem_limit_bytes=60 << 20),
        cost_estimate=pl.CostEstimate(flops=1000, bytes_accessed=1000, transcendentals=0),
        name="memory_forward",
    )(
        *scalars,
        tokens,
        memory,
        *own,
        partner,
        vectors,
        *far,
        *far_partner,
        inner_weight,
        outer_weight,
    )


def lane_masks(rows):
    lane = lax.broadcasted_iota(jnp.int32, (rows, 2 * HEAD_DIM), 1)
    first = (lane < HEAD_DIM).astype(F32)
    return first.astype(BF16), (1.0 - first).astype(BF16)


def pair_of(head):
    start = 2 * HEAD_DIM * (head // 2)
    return slice(start, start + 2 * HEAD_DIM)


def attend_kernel(
    place_ref, sizes_ref, sections_ref, last_ref, q_ref, k_ref, v_ref, out_ref, probs_ref
):
    limit = limit_of(pl.program_id(0), place_ref, sizes_ref, sections_ref, last_ref)
    bias = key_bias(limit)
    count = q_ref.shape[2] // HEAD_DIM
    q_masks, k_masks = lane_masks(q_ref.shape[1]), lane_masks(KEYS)

    def score(head):
        cols = pair_of(head)
        return nt(k_ref[0, :, cols], q_ref[0, :, cols] * q_masks[head % 2])

    def finish(head, probs, held):
        cols = pair_of(head)
        part = tn(probs, v_ref[0, :, cols] * k_masks[head % 2])
        if head % 2 == 0:
            return part
        out_ref[0, :, cols] = (held + part).astype(BF16)
        return None

    held = before = None
    later = score(0)
    for head in range(count):
        scores = later + bias
        if head + 1 < count:
            later = score(head + 1)
        if before is not None:
            held = finish(head - 1, before, held)
        weights = jnp.exp(scores - jnp.max(scores, axis=0, keepdims=True))
        before = (weights * (1.0 / jnp.sum(weights, axis=0, keepdims=True))).astype(BF16)
        probs_ref[0, head] = before
    finish(count - 1, before, held)


def attend(scalars, query, keys, values):
    segs, rows, width = query.shape
    wide = width // 2

    def block(length):
        return pl.BlockSpec((1, length, wide), lambda s, h, *_: (s, 0, h))

    return pl.pallas_call(
        attend_kernel,
        grid_spec=pltpu.PrefetchScalarGridSpec(
            num_scalar_prefetch=4,
            grid=(segs, 2),
            in_specs=[block(rows), block(KEYS), block(KEYS)],
            out_specs=[
                block(rows),
                pl.BlockSpec((1, wide // HEAD_DIM, KEYS, rows), lambda s, h, *_: (s, h, 0, 0)),
            ],
        ),
        out_shape=[
            jax.ShapeDtypeStruct(query.shape, BF16),
            jax.ShapeDtypeStruct((segs, width // HEAD_DIM, KEYS, rows), BF16),
        ],
        compiler_params=pltpu.CompilerParams(vmem_limit_bytes=60 << 20),
        cost_estimate=pl.CostEstimate(flops=1000, bytes_accessed=1000, transcendentals=0),
        name="attend",
    )(*scalars, query, keys, values)


def in_step_kernel(*refs):
    pass


def in_step(*values):
    anywhere = [pl.BlockSpec(memory_space=pl.ANY)] * len(values)
    return pl.pallas_call(
        in_step_kernel,
        in_specs=anywhere,
        out_specs=anywhere,
        out_shape=[jax.ShapeDtypeStruct(value.shape, value.dtype) for value in values],
        input_output_aliases={i: i for i in range(len(values))},
        name="in_step",
    )(*values)


def attend_back_kernel(through, place_ref, q_ref, k_ref, v_ref, d_ref, p_ref, *refs):
    dq_ref, own_ref, other_ref, mem_ref = refs[through:][:4]
    first_core = place_ref[CORE] == 0
    count = q_ref.shape[2] // HEAD_DIM
    q_masks, k_masks = lane_masks(q_ref.shape[1]), lane_masks(KEYS)

    def first(head):
        cols = pair_of(head)
        return nt(v_ref[0, :, cols], d_ref[0, :, cols] * q_masks[head % 2])

    def last(head, d_scores, held):
        cols, mask = pair_of(head), q_masks[head % 2]
        dv = nn(p_ref[0, head], d_ref[0, :, cols] * mask)
        dk = nn(d_scores, q_ref[0, :, cols] * mask)
        dq = tn(d_scores, k_ref[0, :, cols] * k_masks[head % 2])
        if head % 2 == 0:
            return dv, dk, dq
        for index, value in enumerate((held[1] + dk, held[0] + dv)):
            low, high = value[:HALF_ROWS], value[HALF_ROWS:SEG_LEN]
            own_ref[index, 0, :, cols] = jnp.where(first_core, low, high)
            other_ref[index, 0, :, cols] = jnp.where(first_core, high, low)
            mem_ref[index, 0, :, cols] = value[SEG_LEN:]
        dq_ref[0, :, cols] = ((held[2] + dq) * SCALE).astype(BF16)
        return None

    held = before = None
    later = first(0)
    for head in range(count):
        d_probs = later
        if head + 1 < count:
            later = first(head + 1)
        if before is not None:
            held = last(head - 1, before, held)
        probs = p_ref[0, head].astype(F32)
        delta = jnp.sum(probs * d_probs, axis=0, keepdims=True)
        before = (probs * (d_probs - delta)).astype(BF16)
    last(count - 1, before, held)


def attend_back(place, query, keys, values, d_context, probs, first, count, held=(), through=()):
    segs, rows, width = query.shape
    wide = width // 2

    def block(length):
        return pl.BlockSpec((1, length, wide), lambda s, h, place: (first + s, 0, h))

    def two(length):
        return pl.BlockSpec((2, 1, length, wide), lambda s, h, place: (0, first + s, 0, h))

    inputs = (query, keys, values, d_context, probs)
    at = 1 + len(inputs)
    aliases = {at + i: i for i in range(len(held))}
    aliases.update({at + len(held) + i: 4 + i for i in range(len(through))})
    return pl.pallas_call(
        partial(attend_back_kernel, len(held) + len(through)),
        grid_spec=pltpu.PrefetchScalarGridSpec(
            num_scalar_prefetch=1,
            grid=(count, 2),
            in_specs=[
                block(rows),
                block(KEYS),
                block(KEYS),
                block(rows),
                pl.BlockSpec(
                    (1, wide // HEAD_DIM, KEYS, rows),
                    lambda s, h, place: (first + s, h, 0, 0),
                ),
            ]
            + [pl.BlockSpec(memory_space=pl.ANY)] * (len(held) + len(through)),
            out_specs=[block(rows), two(HALF_ROWS), two(HALF_ROWS), two(MEM_PAD)]
            + [pl.BlockSpec(memory_space=pl.ANY)] * len(through),
        ),
        out_shape=[
            jax.ShapeDtypeStruct(query.shape, BF16),
            jax.ShapeDtypeStruct((2, segs, HALF_ROWS, width), F32),
            jax.ShapeDtypeStruct((2, segs, HALF_ROWS, width), F32),
            jax.ShapeDtypeStruct((2, segs, MEM_PAD, width), F32),
        ]
        + [jax.ShapeDtypeStruct(value.shape, value.dtype) for value in through],
        input_output_aliases=aliases,
        compiler_params=pltpu.CompilerParams(vmem_limit_bytes=60 << 20),
        cost_estimate=pl.CostEstimate(flops=1000, bytes_accessed=1000, transcendentals=0),
        name="attend_back",
    )(place, *inputs, *held, *through)


SUM_ROWS = 24
QUERY_SUM = 10
VALUE_SUM = 11
MEMORY_SUM = 12


def feed_kernel(
    place_ref,
    sizes_ref,
    sections_ref,
    last_ref,
    rows_ref,
    context_ref,
    cot_ref,
    out_weight_ref,
    inner_ref,
    outer_ref,
    vectors_ref,
    out_ref,
    out_rows_ref,
    d_hidden_ref,
    d_hidden_low_ref,
    d_context_ref,
    sums_ref,
    own_inner_hbm,
    own_outer_hbm,
    other_inner_hbm,
    other_outer_hbm,
    slope_ref,
    active_ref,
    grads_ref,
    sems,
):
    segment = pl.program_id(0)
    side, core = place_ref[SIDE], place_ref[CORE]
    vectors = vectors_ref[...]
    gain_one, gain_two = row_of(vectors, GAIN_ONE), row_of(vectors, GAIN_TWO)
    width = vectors.shape[1]
    half = width // 2
    quarter = width // 4
    chunks = [slice(at, at + width) for at in range(0, inner_ref.shape[1], width)]
    row = lax.broadcasted_iota(jnp.int32, (HALF_ROWS, 1), 0) + core * HALF_ROWS
    valid = row < limit_of(segment, place_ref, sizes_ref, sections_ref, last_ref)

    def of_side(value):
        return jnp.where(side == 0, value[:, :half], value[:, half:])

    def add_grads(which, index, value):
        for row_half in range(2):
            rows = value[quarter * row_half : quarter * (row_half + 1)]
            for part in range(2):
                at = 2 * index + part
                held = jnp.where(segment == 0, 0.0, grads_ref[which, row_half, at])
                grads_ref[which, row_half, at] = held + rows[:, half * part : half * (part + 1)]

    hidden = (
        rows_ref[0].astype(F32)
        + nn(context_ref[0], out_weight_ref[0])
        + row_of(vectors, OUT_BIAS)
    )
    normed, unit_one, root_one = norm_fwd(hidden, gain_one, row_of(vectors, SHIFT_ONE))
    normed_low = normed.astype(BF16)
    total = normed + row_of(vectors, OUTER_BIAS)
    for index, chunk in enumerate(chunks):
        inner = nn(normed_low, inner_ref[:, chunk]) + row_of(vectors, INNER_BIAS + index)
        active, slope = gelu_parts(inner)
        active = active.astype(BF16)
        active_ref[:, chunk] = active
        slope_ref[:, chunk] = slope
        total = total + nn(active, outer_ref[chunk])
    result, unit_two, root_two = norm_fwd(total, gain_two, row_of(vectors, SHIFT_TWO))
    result = jnp.where(valid, result, 0.0)
    out_ref[0] = result
    out_rows_ref[0] = result

    d_result = jnp.where(valid, cot_ref[0].astype(F32), 0.0)
    d_total = norm_bwd(d_result, unit_two, root_two, gain_two)
    d_total_low = d_total.astype(BF16)
    normed_half, d_total_half = of_side(normed_low), of_side(d_total_low)
    d_normed = d_total
    inner_sums = []
    for index, chunk in enumerate(chunks):
        d_inner = (nt(d_total_low, outer_ref[chunk]) * slope_ref[:, chunk]).astype(BF16)
        inner_sums.append(column_sum(d_inner.astype(F32)))
        d_normed = d_normed + nt(d_inner, inner_ref[:, chunk])
        add_grads(0, index, tn(normed_half, d_inner))
        add_grads(1, index, tn(d_total_half, active_ref[:, chunk]))
    final = segment == pl.num_programs(0) - 1
    targets = ((other_inner_hbm, own_inner_hbm), (other_outer_hbm, own_outer_hbm))
    copies = [
        pltpu.make_async_copy(
            grads_ref.at[which, core if own else 1 - core],
            targets[which][own],
            sems.at[which, own],
        )
        for own in range(2)
        for which in range(2)
    ]

    @pl.when(final)
    def _():
        for copy in copies:
            copy.start()

    d_hidden = norm_bwd(d_normed, unit_one, root_one, gain_one)
    d_hidden_ref[0] = d_hidden
    d_hidden_low = d_hidden.astype(BF16)
    d_hidden_low_ref[0] = d_hidden_low
    d_context_ref[0] = nt(d_hidden_low, out_weight_ref[0]).astype(BF16)
    sums = [
        column_sum(d_hidden),
        column_sum(d_normed * unit_one),
        column_sum(d_normed),
        column_sum(d_total),
        column_sum(d_result * unit_two),
        column_sum(d_result),
    ] + inner_sums
    sums = jnp.concatenate(sums + [jnp.zeros((SUM_ROWS - len(sums), width), F32)], 0)

    @pl.when(segment == 0)
    def _():
        sums_ref[...] = sums

    @pl.when(segment > 0)
    def _():
        sums_ref[...] += sums

    @pl.when(final)
    def _():
        for copy in copies:
            copy.wait()


def feed(scalars, tokens, context, cot, weights, inner_weight, outer_weight, vectors):
    width, ff = inner_weight.shape
    chunk = width // 2

    def own_half():
        return pl.BlockSpec((1, HALF_ROWS, width), lambda i, place, *_: (i, place[CORE], 0))

    def segment():
        return pl.BlockSpec((1, HALF_ROWS, width), lambda i, *_: (i, 0, 0))

    def fixed(shape, index=(0, 0)):
        return pl.BlockSpec(shape, lambda i, *_: index, pipeline_mode=pl.Buffered(1))

    like = pltpu.HBM
    per_segment = (SEGS, HALF_ROWS, width)
    grads_shape = (ff // chunk, width // 4, chunk)
    return pl.pallas_call(
        feed_kernel,
        grid_spec=pltpu.PrefetchScalarGridSpec(
            num_scalar_prefetch=4,
            grid=(SEGS,),
            in_specs=[
                own_half(),
                segment(),
                own_half(),
                fixed((1, width, width), (3, 0, 0)),
                fixed((width, ff)),
                fixed((ff, width)),
                fixed(vectors.shape),
            ],
            out_specs=[
                own_half(),
                segment(),
                segment(),
                segment(),
                segment(),
                pl.BlockSpec((SUM_ROWS, width), lambda i, *_: (0, 0)),
            ]
            + [pl.BlockSpec(memory_space=pl.ANY)] * 4,
            scratch_shapes=[
                pltpu.VMEM((HALF_ROWS, ff), F32),
                pltpu.VMEM((HALF_ROWS, ff), BF16),
                pltpu.VMEM((2, 2) + grads_shape, F32),
                pltpu.SemaphoreType.DMA((2, 2)),
            ],
        ),
        out_shape=[
            like((SEGS, SEG_LEN, width), F32),
            like(per_segment, F32),
            like(per_segment, F32),
            like(per_segment, BF16),
            like(per_segment, BF16),
            like((SUM_ROWS, width), F32),
        ]
        + [like(grads_shape, F32)] * 4,
        compiler_params=pltpu.CompilerParams(vmem_limit_bytes=60 << 20),
        cost_estimate=pl.CostEstimate(flops=1000, bytes_accessed=1000, transcendentals=0),
        name="feed",
    )(*scalars, tokens, context, cot, weights, inner_weight, outer_weight, vectors)


BLOCKS = 8
SUM_PART = SUM_ROWS // BLOCKS
SUM_SPACE = 8


def block_rows(width):
    rows = width // 4 // BLOCKS
    return 2 * rows, 2 * rows + SUM_SPACE


def to_blocks(ref, matrices, sums=None):
    rows = (ref.shape[1] - (0 if sums is None else SUM_SPACE)) // 2
    for block in range(BLOCKS):
        for index, matrix in enumerate(matrices):
            ref[block, rows * index : rows * (index + 1)] = matrix(rows * block, rows)
        if sums is not None:
            part = sums[SUM_PART * block : SUM_PART * (block + 1)]
            filler = jnp.zeros((SUM_SPACE - SUM_PART, part.shape[1]), F32)
            ref[block, 2 * rows :] = jnp.concatenate([part, filler], 0)


def memory_backward_kernel(
    packed,
    place_ref,
    kv_mem_ref,
    kv_mem_other_ref,
    low_ref,
    mem_query_ref,
    mem_context_ref,
    mem_probs_ref,
    mem_hidden_ref,
    mem_total_ref,
    mem_slope_ref,
    mem_active_ref,
    mem_normed_ref,
    vectors_ref,
    weights_hbm,
    keys_hbm,
    values_hbm,
    inner_hbm,
    outer_hbm,
    kv_rows_hbm,
    query_dense_ref,
    dense_ref,
    *refs,
):
    share_refs, kv_rows_ref, refs = refs[:-10], refs[-10], refs[-9:]
    writes = []
    weights_ref, keys_ref, values_ref, inner_ref, outer_ref, grad_ref, d_inner_ref, d_total_ref, sems = refs
    order = [(weights_hbm.at[at], weights_ref.at[at]) for at in (1, 2)]
    order += [(outer_hbm, outer_ref), (inner_hbm, inner_ref)]
    order += [(weights_hbm.at[3], weights_ref.at[3])]
    for segment in reversed(range(CHAINED)):
        order += [(values_hbm.at[segment], values_ref.at[segment])]
        order += [(keys_hbm.at[segment], keys_ref.at[segment])]
        if segment == CHAINED - 1:
            order += [(weights_hbm.at[0], weights_ref.at[0])]
    copies = [
        pltpu.make_async_copy(source, target, sems.at[index])
        for index, (source, target) in enumerate(order)
    ]
    for copy in copies:
        copy.start()
    arrived = iter(copies)

    def wait(count):
        for _ in range(count):
            next(arrived).wait()

    side, core = place_ref[0], place_ref[1]
    width = low_ref.shape[2]
    quarter = width // 4
    vectors = vectors_ref[...]
    gain_one, gain_two = row_of(vectors, GAIN_ONE), row_of(vectors, GAIN_TWO)
    mask = head_mask(width)
    own = pl.ds(core * HALF_ROWS, HALF_ROWS)
    d_memory = None
    sums = None
    queries, hiddens, key_rows, value_rows = [], [], [], []
    for segment in reversed(range(SEGS)):
        d_keys = kv_mem_ref[0, segment] + kv_mem_other_ref[0, segment]
        d_values = kv_mem_ref[1, segment] + kv_mem_other_ref[1, segment]
        if d_memory is None:
            d_next = None
        else:
            normed, unit_one, root_one = norm_fwd(
                mem_hidden_ref[segment], gain_one, row_of(vectors, SHIFT_ONE)
            )
            _, unit_two, root_two = norm_fwd(
                mem_total_ref[segment], gain_two, row_of(vectors, SHIFT_TWO)
            )
            d_total = norm_bwd(d_memory, unit_two, root_two, gain_two)
            d_total_low = d_total.astype(BF16)
            if segment == CHAINED - 1:
                wait(1)
            d_inner = (nt(d_total_low, outer_ref[...]) * mem_slope_ref[segment]).astype(BF16)
            if segment == CHAINED - 1:
                wait(1)
            d_normed = d_total + nt(d_inner, inner_ref[...])
            d_hidden = norm_bwd(d_normed, unit_one, root_one, gain_one)
            d_hidden_low = d_hidden.astype(BF16)
            if segment == CHAINED - 1:
                wait(1)
            d_context = spread_heads(nt(d_hidden_low, weights_ref[3]).astype(BF16), mask)
            query = spread_heads(mem_query_ref[segment], mask)
            probs = mem_probs_ref[segment]
            probs_low = probs.astype(BF16)
            wait(1)
            d_probs = nt(values_ref[segment], d_context)
            delta = jnp.sum(probs * d_probs, axis=0, keepdims=True)
            d_scores = (probs * (d_probs - delta)).astype(BF16)
            wait(1)
            d_query = gather_heads(tn(d_scores, keys_ref[segment]), mask) * SCALE
            d_query = d_query.astype(BF16)
            more_keys = nn(d_scores, query)
            more_values = nn(probs_low, d_context)
            grad_ref[0, :SEG_LEN] = more_keys[:SEG_LEN]
            grad_ref[1, :SEG_LEN] = more_values[:SEG_LEN]
            kv_rows_ref[0, segment] = grad_ref[0, own]
            kv_rows_ref[1, segment] = grad_ref[1, own]
            write = pltpu.make_async_copy(
                kv_rows_ref.at[:, segment], kv_rows_hbm.at[:, segment], sems.at[10 + segment]
            )
            write.start()
            writes.append(write)
            d_keys = d_keys + more_keys[SEG_LEN:]
            d_values = d_values + more_values[SEG_LEN:]
            if segment == CHAINED - 1:
                wait(1)
            d_next = d_hidden + nn(d_query, weights_ref[0])
            queries.append(d_query)
            hiddens.append(d_hidden_low)
            d_total_ref[segment] = d_total_low
            d_inner_ref[segment] = d_inner
            wide = column_sum(d_inner.astype(F32))
            rows = [
                column_sum(d_hidden),
                column_sum(d_normed * unit_one),
                column_sum(d_normed),
                column_sum(d_total),
                column_sum(d_memory * unit_two),
                column_sum(d_memory),
            ]
            rows += [wide[:, at : at + width] for at in range(0, wide.shape[1], width)]
            rows.append(column_sum(d_query.astype(F32)))
            rows = jnp.concatenate(rows, 0)
            sums = rows if sums is None else sums + rows
        d_keys, d_values = d_keys.astype(BF16), d_values.astype(BF16)
        key_rows.append(d_keys)
        value_rows.append(d_values)
        if segment == CHAINED:
            wait(2)
        d_next = 0.0 if d_next is None else d_next
        d_memory = d_next + nn(d_keys, weights_ref[1]) + nn(d_values, weights_ref[2])
    low = [low_ref[segment] for segment in reversed(range(SEGS))]
    low_all = jnp.concatenate(low, 0)
    low_chained = jnp.concatenate(low[1:], 0)
    context = jnp.concatenate([mem_context_ref[s] for s in reversed(range(CHAINED))], 0)
    pairs = (
        (jnp.concatenate(queries, 0), low_chained),
        (context, jnp.concatenate(hiddens, 0)),
        (jnp.concatenate(key_rows, 0), low_all),
        (jnp.concatenate(value_rows, 0), low_all),
    )
    start = (2 * side + core) * quarter

    def part(index):
        return lambda at, rows: grad_ref[index, pl.ds(pl.multiple_of(start + at, 8), rows)]

    value_sum = column_sum(jnp.concatenate(value_rows, 0).astype(F32))
    filler = jnp.zeros((SUM_ROWS - MEMORY_SUM - MEM, width), F32)
    sums = jnp.concatenate([sums, value_sum, d_memory[:MEM], filler], 0)
    for first, ref, extra in ((0, query_dense_ref, None), (2, dense_ref, sums)):
        for index in range(2):
            grad_ref[index, :width] = tn(*pairs[first + index])
        to_blocks(ref, [part(0), part(1)], extra)
    for write in writes:
        write.wait()
    if not packed:
        share_refs[0][...] = d_inner_ref[...]
        share_refs[1][...] = d_total_ref[...]
        return
    share_out(place_ref, share_refs, d_inner_ref, d_total_ref)


def memory_backward(
    place, kv_mem, weights, keys, values, saved, vectors, inner_weight, outer_weight, packed
):
    width, ff = inner_weight.shape
    vmem = pl.BlockSpec(memory_space=pltpu.VMEM)
    query_rows, key_rows = block_rows(width)
    if packed:
        shares = [((CHAINED * MEM_PAD, width + SHARE_SPACE), F32)] * 4
    else:
        shares = [((CHAINED, MEM_PAD, ff), BF16), ((CHAINED, MEM_PAD, width), BF16)]
    shapes = [
        ((2, CHAINED, HALF_ROWS, width), F32),
        ((BLOCKS, query_rows, width), F32),
        ((BLOCKS, key_rows, width), F32),
    ] + shares
    return pl.pallas_call(
        partial(memory_backward_kernel, packed),
        in_specs=[pl.BlockSpec(memory_space=pltpu.SMEM)]
        + [vmem] * 12
        + [pl.BlockSpec(memory_space=pl.ANY)] * 5,
        out_specs=[pl.BlockSpec(memory_space=pl.ANY)] + [vmem] * (len(shapes) - 1),
        out_shape=[pltpu.HBM(*shapes[0])]
        + [jax.ShapeDtypeStruct(shape, dtype) for shape, dtype in shapes[1:]],
        scratch_shapes=[
            pltpu.VMEM(*shapes[0]),
            pltpu.VMEM(weights.shape, BF16),
            pltpu.VMEM((CHAINED,) + keys.shape[1:], BF16),
            pltpu.VMEM((CHAINED,) + keys.shape[1:], BF16),
            pltpu.VMEM((width, ff), BF16),
            pltpu.VMEM((ff, width), BF16),
            pltpu.VMEM((2, width, width), F32),
            pltpu.VMEM((CHAINED, MEM_PAD, ff), BF16),
            pltpu.VMEM((CHAINED, MEM_PAD, width), BF16),
            pltpu.SemaphoreType.DMA((10 + CHAINED,)),
        ],
        compiler_params=pltpu.CompilerParams(vmem_limit_bytes=60 << 20),
        cost_estimate=pl.CostEstimate(flops=1000, bytes_accessed=1000, transcendentals=0),
        name="memory_backward",
    )(place, *kv_mem, *saved, vectors, weights, keys, values, inner_weight, outer_weight)


def grads_out(place_ref, grads_ref, own_ref, other_ref, sums=None):
    quarter = grads_ref.shape[1] // 2
    core = place_ref[CORE]
    for ref, at in ((own_ref, core), (other_ref, 1 - core)):

        def part(index, at=at):
            return lambda row, rows: grads_ref[
                index, pl.ds(pl.multiple_of(at * quarter + row, 8), rows)
            ]

        to_blocks(ref, [part(0), part(1)], sums)


def query_grads_kernel(
    place_ref,
    tokens_ref,
    d_hidden_ref,
    d_query_ref,
    context_ref,
    d_hidden_low_ref,
    weights_ref,
    sums_in_ref,
    out_ref,
    own_ref,
    other_ref,
    sums_ref,
    grads_ref,
):
    segment = pl.program_id(0)
    half = out_ref.shape[2] // 2
    d_query = d_query_ref[0]
    out_ref[0] = d_hidden_ref[0] + nn(d_query, weights_ref[0])
    first_side = place_ref[SIDE] == 0

    @pl.when(segment == 0)
    def _():
        grads_ref[...] = jnp.zeros_like(grads_ref)
        sums_ref[...] = sums_in_ref[...]

    pairs = ((d_query, tokens_ref[0]), (context_ref[0], d_hidden_low_ref[0]))
    for index, (cols, against) in enumerate(pairs):
        grads_ref[index] += tn(jnp.where(first_side, cols[:, :half], cols[:, half:]), against)
    sums_ref[QUERY_SUM : QUERY_SUM + 1] += column_sum(d_query.astype(F32))

    @pl.when(segment == pl.num_programs(0) - 1)
    def _():
        grads_out(place_ref, grads_ref, own_ref, other_ref)


def query_grads(place, tokens, d_hidden, d_query, context, d_hidden_low, weights, sums):
    width = tokens.shape[2]

    def own_half():
        return pl.BlockSpec((1, HALF_ROWS, width), lambda i, place: (i, place[CORE], 0))

    def segment():
        return pl.BlockSpec((1, HALF_ROWS, width), lambda i, place: (i, 0, 0))

    def whole(shape):
        return pl.BlockSpec(shape, lambda i, place: (0,) * len(shape))

    shapes = [(BLOCKS, block_rows(width)[0], width)] * 2 + [(SUM_ROWS, width)]
    return pl.pallas_call(
        query_grads_kernel,
        grid_spec=pltpu.PrefetchScalarGridSpec(
            num_scalar_prefetch=1,
            grid=(SEGS,),
            in_specs=[
                own_half(),
                segment(),
                segment(),
                segment(),
                segment(),
                whole((1, width, width)),
                whole((SUM_ROWS, width)),
            ],
            out_specs=[segment()] + [whole(shape) for shape in shapes],
            scratch_shapes=[pltpu.VMEM((2, width // 2, width), F32)],
        ),
        out_shape=[
            jax.ShapeDtypeStruct(shape, F32) for shape in [(SEGS, HALF_ROWS, width)] + shapes
        ],
        compiler_params=pltpu.CompilerParams(vmem_limit_bytes=60 << 20),
        cost_estimate=pl.CostEstimate(flops=1000, bytes_accessed=1000, transcendentals=0),
        name="query_grads",
    )(place, tokens, d_hidden, d_query, context, d_hidden_low, weights, sums)


def input_grads_kernel(
    place_ref,
    tokens_ref,
    d_part_ref,
    kv_own_ref,
    kv_other_ref,
    kv_more_ref,
    key_ref,
    value_ref,
    sums_in_ref,
    out_ref,
    rows_ref,
    own_ref,
    other_ref,
    grads_ref,
    sums_ref,
):
    segment = pl.program_id(0)
    width = out_ref.shape[2]
    half = width // 2
    more = jnp.where(segment < CHAINED, 1.0, 0.0)
    d_keys = (kv_own_ref[0, 0] + kv_other_ref[0, 0] + more * kv_more_ref[0, 0]).astype(BF16)
    d_values = (kv_own_ref[1, 0] + kv_other_ref[1, 0] + more * kv_more_ref[1, 0]).astype(BF16)
    d_inputs = d_part_ref[0] + nn(d_keys, key_ref[0]) + nn(d_values, value_ref[0])
    out_ref[0] = d_inputs
    rows_ref[0] = d_inputs
    first_side = place_ref[SIDE] == 0

    @pl.when(segment == 0)
    def _():
        grads_ref[...] = jnp.zeros_like(grads_ref)
        sums_ref[...] = sums_in_ref[...]

    for index, cols in enumerate((d_keys, d_values)):
        cols = jnp.where(first_side, cols[:, :half], cols[:, half:])
        grads_ref[index] += tn(cols, tokens_ref[0])
    sums_ref[VALUE_SUM : VALUE_SUM + 1] += column_sum(d_values.astype(F32))

    @pl.when(segment == pl.num_programs(0) - 1)
    def _():
        grads_out(place_ref, grads_ref, own_ref, other_ref, sums_ref[...])


def input_grads(place, tokens, d_part, kv_own, kv_other, kv_more, weights, sums):
    width = tokens.shape[2]

    def own_half():
        return pl.BlockSpec((1, HALF_ROWS, width), lambda i, place: (i, place[CORE], 0))

    def segment():
        return pl.BlockSpec((1, HALF_ROWS, width), lambda i, place: (i, 0, 0))

    def two(last):
        return pl.BlockSpec(
            (2, 1, HALF_ROWS, width), lambda i, place: (0, jnp.minimum(i, last), 0, 0)
        )

    def weight(which):
        return pl.BlockSpec((1, width, width), lambda i, place: (which, 0, 0))

    dense = jax.ShapeDtypeStruct((BLOCKS, block_rows(width)[1], width), F32)
    dense_spec = pl.BlockSpec(dense.shape, lambda i, place: (0, 0, 0))
    return pl.pallas_call(
        input_grads_kernel,
        grid_spec=pltpu.PrefetchScalarGridSpec(
            num_scalar_prefetch=1,
            grid=(SEGS,),
            in_specs=[
                own_half(),
                segment(),
                two(SEGS - 1),
                two(SEGS - 1),
                two(CHAINED - 1),
                weight(1),
                weight(2),
                pl.BlockSpec((SUM_ROWS, width), lambda i, place: (0, 0)),
            ],
            out_specs=[own_half(), segment(), dense_spec, dense_spec],
            scratch_shapes=[
                pltpu.VMEM((2, width // 2, width), F32),
                pltpu.VMEM((SUM_ROWS, width), F32),
            ],
        ),
        out_shape=[
            jax.ShapeDtypeStruct((SEGS, SEG_LEN, width), F32),
            jax.ShapeDtypeStruct((SEGS, HALF_ROWS, width), F32),
            dense,
            dense,
        ],
        compiler_params=pltpu.CompilerParams(vmem_limit_bytes=60 << 20),
        cost_estimate=pl.CostEstimate(flops=1000, bytes_accessed=1000, transcendentals=0),
        name="input_grads",
    )(place, tokens, d_part, kv_own, kv_other, kv_more, weights, weights, sums)


def memory_shares_kernel(place_ref, *refs):
    early_refs, late_refs, refs = refs[:4], refs[4:8], refs[8:]
    inner_kept, inner_moved, outer_kept, outer_moved, keep_ref, send_ref = refs
    mine = place_ref[CHAIN] // 4
    quarter = keep_ref.shape[1]
    half = keep_ref.shape[2]
    width = 2 * half
    early, late = (
        jnp.concatenate([ref[...] for ref in share], 0).astype(BF16)
        for share in (early_refs, late_refs)
    )
    active, normed = early[:, :width], early[:, width : width + quarter]
    d_inner, d_total = late[:, :width], late[:, width : width + quarter]
    sides = (
        (inner_kept, inner_moved, normed, d_inner),
        (outer_kept, outer_moved, d_total, active),
    )
    for which, (kept_ref, moved_ref, factor, hidden) in enumerate(sides):
        more = tn(factor, hidden)
        parts = [kept_ref[at] + moved_ref[at] + more[:, half * at : half * (at + 1)] for at in (0, 1)]
        keep_ref[which] = jnp.where(mine == 0, parts[0], parts[1])
        send_ref[which] = jnp.where(mine == 0, parts[1], parts[0])


def memory_shares(place, early, late, inner_kept, inner_moved, outer_kept, outer_moved):
    vmem = pl.BlockSpec(memory_space=pltpu.VMEM)
    shape = jax.ShapeDtypeStruct((2,) + inner_kept.shape[1:], F32)
    return pl.pallas_call(
        memory_shares_kernel,
        in_specs=[pl.BlockSpec(memory_space=pltpu.SMEM)] + [vmem] * 12,
        out_specs=[vmem] * 2,
        out_shape=[shape, shape],
        compiler_params=pltpu.CompilerParams(vmem_limit_bytes=60 << 20),
        name="memory_shares",
    )(place, *early, *late, inner_kept, inner_moved, outer_kept, outer_moved)


def split_kernel(bits, counts, unused, place_ref, *refs):
    ins, outs = refs[: sum(counts)], refs[sum(counts) + unused :]
    for index, (bit, count) in enumerate(zip(bits, counts)):
        terms, ins = ins[:count], ins[count:]
        if bit is None:
            outs[2 * index][...] = sum((ref[...] for ref in terms[1:]), terms[0][...])
            continue
        mine = (place_ref[CHAIN] >> bit) & 1
        for out, at in ((outs[2 * index], mine), (outs[2 * index + 1], 1 - mine)):
            out[...] = sum((ref[:, at] for ref in terms[1:]), terms[0][:, at])


def split(place, *items, limit=32, after=()):
    terms, bits, counts, shapes, results = [], [], [], [], []
    for bit, axis, values in items:
        shape = values[0].shape
        bits.append(bit)
        counts.append(len(values))
        if bit is None:
            terms += values
            shapes += [shape, (8, 128)]
            results += [shape, (8, 128)]
            continue
        ahead = 1
        for size in shape[:axis]:
            ahead *= size
        terms += [value.reshape((ahead, 2, -1) + shape[-2:]) for value in values]
        half = shape[:axis] + shape[axis + 1 :]
        inner = terms[-1].shape
        shapes += [inner[:1] + inner[2:]] * 2
        results += [half] * 2
    vmem = pl.BlockSpec(memory_space=pltpu.VMEM)
    outs = pl.pallas_call(
        partial(split_kernel, tuple(bits), tuple(counts), len(after)),
        in_specs=[pl.BlockSpec(memory_space=pltpu.SMEM)]
        + [vmem] * len(terms)
        + [pl.BlockSpec(memory_space=pl.ANY)] * len(after),
        out_specs=[vmem] * len(shapes),
        out_shape=[jax.ShapeDtypeStruct(shape, F32) for shape in shapes],
        compiler_params=pltpu.CompilerParams(vmem_limit_bytes=limit << 20),
        name="split",
    )(place, *terms, *after)
    return [out.reshape(shape) for out, shape in zip(outs, results)]


def join_kernel(bits, unused, place_ref, *refs):
    ins, outs = refs[: 2 * len(bits)], refs[2 * len(bits) + unused :]
    for index, bit in enumerate(bits):
        mine = (place_ref[CHAIN] >> bit) & 1
        outs[index][:, mine] = ins[2 * index][...]
        outs[index][:, 1 - mine] = ins[2 * index + 1][...]


def join(place, *items, after=()):
    terms, bits, shapes, results = [], [], [], []
    for bit, axis, own, other in items:
        shape = own.shape
        ahead = 1
        for size in shape[:axis]:
            ahead *= size
        terms += [value.reshape((ahead, -1) + shape[-2:]) for value in (own, other)]
        bits.append(bit)
        inner = terms[-1].shape
        shapes.append(inner[:1] + (2,) + inner[1:])
        results.append(shape[:axis] + (2,) + shape[axis:])
    vmem = pl.BlockSpec(memory_space=pltpu.VMEM)
    outs = pl.pallas_call(
        partial(join_kernel, tuple(bits), len(after)),
        in_specs=[pl.BlockSpec(memory_space=pltpu.SMEM)]
        + [vmem] * len(terms)
        + [pl.BlockSpec(memory_space=pl.ANY)] * len(after),
        out_specs=[vmem] * len(shapes),
        out_shape=[jax.ShapeDtypeStruct(shape, F32) for shape in shapes],
        compiler_params=pltpu.CompilerParams(vmem_limit_bytes=32 << 20),
        name="join",
    )(place, *terms, *after)
    return [out.reshape(shape) for out, shape in zip(outs, results)]


def feed_final_kernel(place_ref, *refs):
    pieces, (inner_ref, outer_ref, wide_ref) = refs[:4], refs[4:]
    side, core = place_ref[SIDE], place_ref[CORE]
    quarter = pieces[0].shape[1]
    places = (
        2 * side + core,
        2 * side + 1 - core,
        2 * (1 - side) + core,
        2 * (1 - side) + 1 - core,
    )
    for ref, at in zip(pieces, places):
        rows = pl.ds(pl.multiple_of(at * quarter, 8), quarter)
        inner_ref[rows] = ref[0]
        wide_ref[rows] = ref[1]
    outer_ref[...] = wide_ref[...].T


def feed_final(place, pieces):
    quarter, piece = pieces[0].shape[1:]
    vmem = pl.BlockSpec(memory_space=pltpu.VMEM)
    shapes = [(4 * quarter, piece), (piece, 4 * quarter)]
    return pl.pallas_call(
        feed_final_kernel,
        in_specs=[pl.BlockSpec(memory_space=pltpu.SMEM)] + [vmem] * 4,
        out_specs=[vmem] * 2,
        out_shape=[jax.ShapeDtypeStruct(shape, F32) for shape in shapes],
        scratch_shapes=[pltpu.VMEM((4 * quarter, piece), F32)],
        compiler_params=pltpu.CompilerParams(vmem_limit_bytes=32 << 20),
        name="feed_final",
    )(place, *pieces)


def final_kernel(place_ref, query_own, query_other, dense_own, dense_other, *refs):
    grad_query, grad_out, grad_key, grad_value, memory_ref, *refs = refs
    *vector_refs, query_bias_ref, value_bias_ref, inner_bias_ref, sums_ref = refs
    chain = place_ref[CHAIN]
    fast = chain % 2

    def put(ref, block, value):
        rows = value.shape[0]
        ref[pl.ds(pl.multiple_of(block * rows, 8), rows)] = value

    rows = query_own.shape[2] // 2
    for far in range(2):
        for near in range(2):
            for source, at in ((query_own, fast), (query_other, 1 - fast)):
                block = 4 * far + 2 * near + at
                put(grad_query, block, source[far, near, :rows])
                put(grad_out, block, source[far, near, rows:])
            for source, at in ((dense_own, fast), (dense_other, 1 - fast)):
                block = 4 * far + 2 * near + at
                put(grad_key, block, source[far, near, :rows])
                put(grad_value, block, source[far, near, rows : 2 * rows])
                put(sums_ref, block, source[far, near, 2 * rows :])
    width = sums_ref.shape[1]
    quarter, piece = query_bias_ref.shape[0], inner_bias_ref.shape[0]

    def row(index):
        at = SUM_SPACE * (index // SUM_PART) + index % SUM_PART
        return sums_ref[at : at + 1]

    for index, ref in enumerate(vector_refs):
        ref[...] = row(index).reshape(width)
    own = 2 * place_ref[SIDE] + place_ref[CORE]
    for ref, index in ((query_bias_ref, QUERY_SUM), (value_bias_ref, VALUE_SUM)):
        whole = row(index)
        value = whole[:, :quarter]
        for other in range(1, 4):
            value = jnp.where(own == other, whole[:, quarter * other : quarter * (other + 1)], value)
        ref[...] = value.reshape(quarter)
    count = width // piece
    value = jnp.zeros((1, piece), F32)
    for index in range(QUERY_SUM - len(vector_refs)):
        whole = row(len(vector_refs) + index)
        for part in range(count):
            here = chain == count * index + part
            value = jnp.where(here, whole[:, piece * part : piece * (part + 1)], value)
    inner_bias_ref[...] = value.reshape(piece)
    for index in range(MEM):
        memory_ref[index : index + 1] = row(MEMORY_SUM + index)


def final(place, halves, piece):
    width = halves[0].shape[3]
    quarter = width // 4
    vmem = pl.BlockSpec(memory_space=pltpu.VMEM)
    shapes = [(quarter, width)] * 4 + [(MEM, width)] + [(width,)] * 6
    shapes += [(quarter,), (quarter,), (piece,)]
    return pl.pallas_call(
        final_kernel,
        in_specs=[pl.BlockSpec(memory_space=pltpu.SMEM)] + [vmem] * 4,
        out_specs=[vmem] * len(shapes),
        out_shape=[jax.ShapeDtypeStruct(shape, F32) for shape in shapes],
        scratch_shapes=[pltpu.VMEM((BLOCKS * SUM_SPACE, width), F32)],
        compiler_params=pltpu.CompilerParams(vmem_limit_bytes=32 << 20),
        name="final",
    )(place, *halves)


def swap_core(value):
    return lax.ppermute(value, "head", [(0, 1), (1, 0), (2, 3), (3, 2)])


def swap_side(value):
    return lax.ppermute(value, "head", [(0, 2), (2, 0), (1, 3), (3, 1)])


def swap_dp(value, bits):
    size = lax.axis_size("dp")
    return lax.ppermute(value, "dp", [(i, i ^ bits) for i in range(size)])


def fetch_far(value):
    part = lax.axis_index("dp") % 4
    mine = lax.dynamic_index_in_dim(value, part, 0, False)
    rows = mine.shape[0]
    half, quarter = rows // 2, rows // 4
    pieces = []
    for start in (0, half):
        own = swap_side(mine[start : start + half])
        fast, slow = swap_dp(own, 1), swap_dp(own, 2)
        pieces += [(0, start, own), (1, start, fast), (2, start, slow)]
        pieces.append((3, start, swap_dp(slow[:quarter], 1)))
        pieces.append((3, start + quarter, swap_dp(fast[quarter:], 2)))
    return pieces


def on_device(
    tokens,
    cotangent,
    memory,
    query_weight,
    query_bias,
    key_weight,
    value_weight,
    value_bias,
    out_weight,
    out_bias,
    gain_one,
    shift_one,
    inner_weight,
    inner_bias,
    outer_weight,
    outer_bias,
    gain_two,
    shift_two,
    group_sizes,
    group_section,
    last_valid,
):
    width = memory.shape[1]
    ff = inner_weight.shape[1]
    dp_size = lax.axis_size("dp")
    chain_index = lax.axis_index("dp")
    head_index = lax.axis_index("head")
    side = head_index // 2
    core = head_index % 2
    quarter = query_weight.shape[1]
    device = chain_index * 4 + head_index
    divisors, sizes = jnp.array([2, 1, 4, 4], jnp.int32), jnp.array([2, 2, 4, dp_size], jnp.int32)
    place = (device // divisors) % sizes
    scalars = (place, group_sizes, group_section, last_valid)

    own_weights = (query_weight.T, key_weight.T, value_weight.T, out_weight)
    wide_weights = jnp.stack([weight.astype(F32) for weight in own_weights])
    far = fetch_far(wide_weights)
    partner = swap_core(wide_weights)
    memory = jnp.pad(memory.astype(F32), ((0, MEM_PAD - MEM), (0, 0)))
    places, far = [piece[:2] for piece in far], [piece[2] for piece in far]
    far_partner = [swap_core(piece) for piece in far]
    vectors = pack_vectors(
        place,
        (out_bias, gain_one, shift_one, outer_bias, gain_two, shift_two),
        query_bias,
        value_bias,
        inner_bias,
    )
    row = jnp.arange(VECTOR_ROWS)[:, None]
    split_rows = (row == QUERY_BIAS) | (row == VALUE_BIAS)
    for swap in (swap_core, swap_side):
        vectors = vectors + jnp.where(split_rows, swap(vectors), 0.0)
    token_rows = tokens.reshape(SEGS, SEG_LEN, width)

    weights, keys, values, own_query, *saved = memory_forward(
        places,
        scalars,
        token_rows,
        memory,
        own_weights,
        partner,
        far,
        far_partner,
        vectors,
        inner_weight,
        outer_weight,
    )
    context, probs = attend(scalars, own_query, keys, values)
    (
        layer_out,
        out_rows,
        d_hidden,
        d_hidden_low,
        d_context,
        sums,
        own_inner,
        own_outer,
        other_inner,
        other_outer,
    ) = feed(
        scalars,
        token_rows,
        context,
        cotangent.reshape(SEGS, SEG_LEN, width),
        weights,
        inner_weight,
        outer_weight,
        vectors,
    )

    piece = ff // dp_size
    back = partial(attend_back, place, own_query, keys, values, d_context, probs)
    held = back(CHAINED, SEGS - CHAINED)
    fast_path = dp_size == BLOCKS
    run = on_block if fast_path else on_any
    results = run(
        place,
        scalars,
        back,
        held,
        (own_inner, own_outer, other_inner, other_outer),
        partial(query_grads, place, token_rows, d_hidden),
        (context, d_hidden_low, weights, sums),
        partial(
            memory_backward,
            place,
            weights=weights,
            keys=keys,
            values=values,
            saved=saved[:9],
            vectors=vectors,
            inner_weight=inner_weight,
            outer_weight=outer_weight,
            packed=fast_path,
        ),
        partial(input_grads, place, token_rows, weights=weights),
        saved,
        out_rows,
    )
    grads, smalls, grad_inner, grad_outer, grad_tokens, others = results
    grad_query, grad_out, grad_key, grad_value = grads
    grad_memory, *grad_vectors, grad_qb, grad_vb, inner_bias_grad = smalls

    def both_cores(value, other):
        start = (1 - core) * HALF_ROWS
        value = lax.dynamic_update_slice_in_dim(value, other, start, 1)
        return value.reshape(SEGS * SEG_LEN, width)

    return (
        both_cores(layer_out, others[0]),
        both_cores(grad_tokens, others[1]),
        grad_memory,
        grad_query.T,
        grad_qb,
        grad_key.T,
        grad_value.T,
        grad_vb,
        grad_out,
        *grad_vectors[:3],
        grad_inner,
        inner_bias_grad,
        grad_outer,
        *grad_vectors[3:],
    )


def at_bits(value, bits):
    axis = 0
    for bit in bits:
        if bit is None:
            axis += 1
        else:
            value = lax.dynamic_index_in_dim(value, bit, axis, False)
    return value


def on_block(
    place, scalars, back, held, ffn, query_part, query_args, backward, input_part, saved, out_rows
):
    index = lax.axis_index("dp")
    fast, slow = index & 1, (index >> 1) & 1
    own_inner, own_outer, other_inner, other_outer = ffn
    early = saved[9:]
    early = early[:1] + [swap_dp(share, bits) for bits, share in enumerate(early) if bits]
    ffn = in_step(
        own_inner, own_outer, swap_core(other_inner), swap_core(other_outer), *early, *held
    )
    ffn, early, held = ffn[:4], ffn[4:8], ffn[8:]
    own_inner, own_outer, other_inner, other_outer = (
        value.reshape((2, 2, 2) + value.shape[1:]) for value in ffn
    )
    inner, outer = (own_inner, other_inner), (own_outer, other_outer)

    def total(terms, bits):
        terms = [at_bits(term, bits) for term in terms]
        return sum(terms[1:], terms[0])

    inner_moved = swap_dp(total(inner, (None, 1 - slow, None)), 2)
    outer_moved = swap_dp(total(outer, (None, None, 1 - fast)), 1)
    d_query, kv_own, kv_other, kv_mem = back(0, CHAINED, held)
    d_part, query_own, query_other, sums = query_part(d_query, *query_args)
    weights = query_args[2]
    values = in_step(
        inner_moved,
        outer_moved,
        d_part,
        query_own,
        query_other,
        sums,
        kv_own,
        kv_other,
        kv_mem,
        swap_core(kv_mem),
    )
    inner_moved, outer_moved, d_part, query_own, query_other, sums, kv_own, kv_other = values[:8]
    kv_mem = values[8:]

    def second(terms, moved, bits, axis, bit):
        def half(at):
            here = [at if place == axis else value for place, value in enumerate(bits)]
            rest = [None if value is None or place != axis else at for place, value in enumerate(here)]
            del rest[[i for i, value in enumerate(bits) if value is not None][0]]
            return total(terms, here) + at_bits(moved, rest)

        return half(bit), half(1 - bit)

    inner_kept, inner_sent = second(inner, inner_moved, (None, slow, None), 2, fast)
    outer_kept, outer_sent = second(outer, outer_moved, (None, None, fast), 1, slow)
    inner_moved, outer_moved = swap_dp(inner_sent, 1), swap_dp(outer_sent, 2)
    kv_other = swap_core(kv_other)
    query_other = swap_core(query_other)
    kv_more, query_mem, dense_mem, *late = backward(kv_mem)

    def cube(*arrays):
        return [value.reshape((2, 2, 2) + value.shape[1:]) for value in arrays]

    q_kept, q_sent = split(place, (0, 2, cube(query_own, query_other, query_mem)), limit=60)
    values = in_step(
        inner_kept,
        inner_moved,
        outer_kept,
        outer_moved,
        kv_other,
        kv_more,
        q_kept,
        q_sent,
        dense_mem,
        *late,
    )
    inner_kept, inner_moved, outer_kept, outer_moved, kv_other, kv_more = values[:6]
    q_kept, q_sent, dense_mem, *late = values[6:]
    q_moved = swap_dp(q_sent, 1)
    late = late[:1] + [swap_dp(share, bits) for bits, share in enumerate(late) if bits]
    grad_tokens, token_rows, dense_own, dense_other = input_part(
        d_part, kv_own, kv_other, kv_more, sums=sums
    )
    q_moved, *late, dense_own, dense_other = in_step(q_moved, *late, dense_own, dense_other)

    ffn_kept, ffn_sent = memory_shares(place, early, late, inner_kept, inner_moved, outer_kept, outer_moved)
    ffn_kept, ffn_sent, dense_own, dense_other = in_step(
        ffn_kept, ffn_sent, dense_own, swap_core(dense_other)
    )
    ffn_moved = swap_dp(ffn_sent, 4)
    q_kept, q_sent = split(place, (1, 1, [q_kept, q_moved]))
    q_moved = swap_dp(q_sent, 2)
    d_kept, d_sent = split(place, (0, 2, cube(dense_own, dense_other, dense_mem)), limit=60)
    d_moved = swap_dp(d_sent, 1)
    q_part, _, d_kept, d_sent = split(
        place, (None, 0, [q_kept, q_moved]), (1, 1, [d_kept, d_moved])
    )
    q_moved, d_moved = swap_dp(q_part, 4), swap_dp(d_sent, 2)
    d_part, _, ffn_mine, _ = split(
        place, (None, 0, [d_kept, d_moved]), (None, 0, [ffn_kept, ffn_moved])
    )
    d_moved = swap_dp(d_part, 4)
    ffn_far = swap_side(ffn_mine)
    q_mine, _ = split(place, (None, 0, [q_part, q_moved]))
    (q_mine,) = join(place, (1, 1, q_mine, swap_dp(q_mine, 2)))
    d_mine, _ = split(place, (None, 0, [d_part, d_moved]), after=(q_mine,))
    q_moved = swap_dp(q_mine, 1)
    (d_mine,) = join(place, (1, 1, d_mine, swap_dp(d_mine, 2)), after=(q_moved,))
    pieces = (ffn_mine, swap_core(ffn_mine), ffn_far, swap_core(ffn_far))
    grad_inner, grad_outer = feed_final(place, pieces)
    halves = (q_mine, q_moved, d_mine, swap_dp(d_mine, 1))
    grads = final(place, halves, grad_inner.shape[1])
    others = (swap_core(out_rows), swap_core(token_rows))
    return grads[:4], grads[4:], grad_inner, grad_outer, grad_tokens, others


def on_any(
    place, scalars, back, held, ffn, query_part, query_args, backward, input_part, saved, out_rows
):
    own_inner, own_outer, other_inner, other_outer = ffn
    dp_size = lax.axis_size("dp")
    quarter = own_inner.shape[1]
    width = 4 * quarter
    head_index = lax.axis_index("head")
    d_query, kv_own, kv_other, kv_mem = back(0, CHAINED, held)
    d_part, query_own, query_other, sums = query_part(d_query, *query_args)
    kv_mem = (kv_mem, swap_core(kv_mem))
    kv_more, query_mem, dense_mem, mem_d_inner, mem_d_total = backward(kv_mem)
    grad_tokens, token_rows, dense_own, dense_other = input_part(
        d_part, kv_own, swap_core(kv_other), kv_more, sums=sums
    )
    query = query_own + swap_core(query_other) + query_mem
    dense = dense_own + swap_core(dense_other) + dense_mem
    query, dense = lax.psum((query, dense), "dp")
    mem_active, mem_normed = saved[7], saved[8]

    def whole(own, other, rows, hidden):
        rows = lax.dynamic_slice_in_dim(rows, head_index * quarter, quarter, 2)
        rows = rows.reshape(-1, quarter)
        value = own + swap_core(other)
        value = value.transpose(1, 0, 2).reshape(quarter, -1)
        value = value + tn(rows, hidden.reshape(rows.shape[0], -1))
        value = lax.psum_scatter(value, "dp", scatter_dimension=1, tiled=True)
        return lax.all_gather(value, "head").reshape(width, -1)

    grad_inner = whole(own_inner, other_inner, mem_normed, mem_d_inner)
    grad_outer = whole(own_outer, other_outer, mem_d_total, mem_active).T
    rows = quarter // BLOCKS

    def part(value, index):
        return value[:, rows * index : rows * (index + 1)].reshape(quarter, width)

    sums = dense[:, 2 * rows : 2 * rows + SUM_PART].reshape(SUM_ROWS, width)
    piece = grad_inner.shape[1]
    at = lax.axis_index("dp") * piece
    smalls = (
        sums[MEMORY_SUM : MEMORY_SUM + MEM],
        *sums[:6],
        lax.dynamic_slice_in_dim(sums[QUERY_SUM], head_index * quarter, quarter, 0),
        lax.dynamic_slice_in_dim(sums[VALUE_SUM], head_index * quarter, quarter, 0),
        lax.dynamic_slice_in_dim(sums[6:QUERY_SUM].reshape(-1), at, piece, 0),
    )
    grads = (part(query, 0), part(query, 1), part(dense, 0), part(dense, 1))
    others = (swap_core(out_rows), swap_core(token_rows))
    return grads, smalls, grad_inner, grad_outer, grad_tokens, others


def solution(mesh):
    row, col, vec, every = P("dp", None), P(None, "head"), P("head"), P()
    placed = (row, row, every, col, vec, col, col, vec, P("head", None)) + (every,) * 11
    return jax.shard_map(
        on_device,
        mesh=mesh,
        in_specs=placed + (P("dp"),),
        out_specs=(
            row,
            row,
            every,
            col,
            vec,
            col,
            col,
            vec,
            P("head", None),
            every,
            every,
            every,
            P(None, "dp"),
            P("dp"),
            row,
            every,
            every,
            every,
        ),
        check_vma=False,
    )
```
